32 devices in a mesh: ctx: 16 (over z, x, core), wa: 2 (over y).
Axes of the slice: x: 2, y: 2, z: 4, core: 2. Of those that a mesh axis runs over, the one named last changes fastest.
Arguments:
- tokens: bfloat16 [2, 1024, 2048], P(None, 'ctx'), may hold values from -6 to 6
- norm_in: bfloat16 [2048], P('ctx'), may hold values from 0.099609375 to 1.8984375
- query_weight: bfloat16 [2048, 3072], P('ctx', 'wa'), may hold values from -0.125 to 0.125
- latent_down: bfloat16 [2048, 576], P('ctx'), may hold values from -0.125 to 0.125
- latent_norm: bfloat16 [512], P('ctx'), may hold values from 0.099609375 to 1.8984375
- latent_up: bfloat16 [512, 4096], P('ctx', 'wa'), may hold values from -0.25 to 0.25
- output_weight: bfloat16 [2048, 2048], P('wa', 'ctx'), may hold values from -0.75 to 0.75
- norm_ffn: bfloat16 [2048], P('ctx'), may hold values from 0.099609375 to 1.8984375
- router_weight: bfloat16 [2048, 16], P('ctx'), may hold values from -0.0625 to 0.0625
- shared_gate: bfloat16 [2048, 2816], P('ctx', 'wa'), may hold values from -0.125 to 0.125
- shared_up: bfloat16 [2048, 2816], P('ctx', 'wa'), may hold values from -0.125 to 0.125
- shared_down: bfloat16 [2816, 2048], P('wa', 'ctx'), may hold values from -0.109375 to 0.109375
- expert_gate: bfloat16 [16, 2048, 1408], P('ctx', None, 'wa'), may hold values from -0.125 to 0.125
- expert_up: bfloat16 [16, 2048, 1408], P('ctx', None, 'wa'), may hold values from -0.125 to 0.125
- expert_down: bfloat16 [16, 1408, 2048], P('ctx', 'wa'), may hold values from -2.5 to 2.5
- routes: int32 [2, 1024, 6], P(None, 'ctx'), may hold values from 0 to 15, all different within a row; in each aligned block of 64 rows (0 to 63, 64 to 127, ..., all dimensions but the last counted through in order) at most 32 rows name the same one
- cotangent: bfloat16 [2, 1024, 2048], P(None, 'ctx'), may hold values from -6 to 6
Outputs:
- block_output: bfloat16 [2, 1024, 2048], P(None, 'ctx')
- tokens_gradient: float32 [2, 1024, 2048], P(None, 'ctx')
- norm_in_gradient: float32 [2048], P('ctx')
- query_weight_gradient: float32 [2048, 3072], P('ctx', 'wa')
- latent_down_gradient: float32 [2048, 576], P('ctx')
- latent_norm_gradient: float32 [512], P('ctx')
- latent_up_gradient: float32 [512, 4096], P('ctx', 'wa')
- output_weight_gradient: float32 [2048, 2048], P('wa', 'ctx')
- norm_ffn_gradient: float32 [2048], P('ctx')
- router_weight_gradient: float32 [2048, 16], P('ctx')
- shared_gate_gradient: float32 [2048, 2816], P('ctx', 'wa')
- shared_up_gradient: float32 [2048, 2816], P('ctx', 'wa')
- shared_down_gradient: float32 [2816, 2048], P('wa', 'ctx')
- expert_gate_gradient: float32 [16, 2048, 1408], P('ctx', None, 'wa')
- expert_up_gradient: float32 [16, 2048, 1408], P('ctx', None, 'wa')
- expert_down_gradient: float32 [16, 1408, 2048], P('ctx', 'wa')
The draws below stay inside these ranges and needn't reach their ends.
Inputs may be any that keep to these rules, and one draw needn't show every extreme that they name: `routes`: each row names 6 different experts. In each aligned block of 64 rows (one sequence's positions on one index of ctx) no expert is named by more than 32 rows, and some block reaches 32.
All inputs are finite; a program needn't handle non-finite values.
Results may differ from the reference program's by a relative error of at most 0.028.
Values may be sent and summed in bfloat16 or wider, within the bound.
No kernel may reach another device: no remote copies, remote signals or barrier semaphores. Data moves between devices by JAX's collectives and lax.ppermute only.
A program may use at most 256 MiB of HBM per device.

```python
import math
from functools import partial
import jax
import jax.numpy as jnp
import numpy as np
from jax import lax

D = 2048
H = 16
DN = 128
DR = 64
DV = 128
R = 512
FE = 1408
FS = 2816
TOPK = 6
SEQS = 2
BLK = 64
EXPERTS = 16
LEN = 1024
CAPB = 32
N_CTX = 16


def block_scale(key, shape, cuts, low, largest):
    def one(position, parts):
        steps = jax.random.uniform(jax.random.fold_in(jax.random.fold_in(key, 6), position), (parts,), jnp.float32, low / len(cuts), largest / len(cuts))
        return jnp.repeat(jnp.exp(steps), shape[position] // parts).reshape((-1,) + (1,) * (len(shape) - position - 1))

    level = one(*cuts[0])
    for cut in cuts[1:]:
        level = level * one(*cut)
    return level


def deal_out(stream_key, own, number, rows, amount, top, reach, lean):
    ranking = jax.random.permutation(stream_key, amount)
    packed, ordinary = load_shares(amount, rows * top, reach, lean, True), load_shares(amount, rows * top, reach, lean, False)
    places = jnp.arange(amount)

    def named(tallies, turn):
        used = int((tallies > 0).sum())
        fixed = max(1, used // 4)
        passed = fixed + (places - fixed + turn * (used - fixed)) % max(1, amount - fixed)
        return jnp.zeros((amount,), jnp.int32).at[ranking[jnp.where(places < fixed, places, passed)]].set(jnp.asarray(tallies, jnp.int32))

    tallies = jnp.where(number % 4 == 0, named(packed, number // 4), named(ordinary, number - number // 4 - 1))
    mixed = jax.random.permutation(jax.random.fold_in(own, 3), amount)
    giver, receiver = mixed[0:amount // 2 * 2:2], mixed[1:amount // 2 * 2:2]
    room = jnp.minimum(tallies[giver] - 1, reach - tallies[receiver]) // 2
    room = jnp.where((giver == ranking[0]) | (receiver == ranking[0]) | (tallies[receiver] == 0), 0, jnp.maximum(room, 0))
    passed = jax.random.randint(jax.random.fold_in(own, 4), (amount // 2,), 0, 1 << 20) % (room + 1)
    tallies = tallies.at[giver].add(-passed).at[receiver].add(passed)
    items = jnp.searchsorted(jnp.cumsum(tallies), jnp.arange(rows * top), side="right").astype(jnp.int32)
    grid = items.reshape(top, rows).T
    grid = grid[jax.random.permutation(jax.random.fold_in(own, 1), rows)]
    turn = jax.random.randint(jax.random.fold_in(own, 2), (rows, 1), 0, top)
    return jnp.take_along_axis(grid, (jnp.arange(top)[None, :] + turn) % top, axis=1)


def load_shares(amount, total, most, skew, full):
    portions = [(1 << 20) // math.isqrt(rank ** skew) + 1 for rank in range(1, amount + 1)]
    largest = most if full else min(most, max(-(-total // amount), total * portions[0] // sum(portions)))
    least = 1 if total - largest >= amount - 1 else 0
    given, surplus = [largest] + [least] * (amount - 1), total - largest - least * (amount - 1)
    while surplus > 0:
        free = [i for i in range(1, amount) if given[i] < largest] or [i for i in range(1, amount) if given[i] < most]
        pool, remaining = sum([portions[i] for i in free]), surplus
        for i in free:
            more = min(most - given[i], max(1, remaining * portions[i] // pool), surplus)
            given[i] = given[i] + more
            surplus = surplus - more
    return np.array(given)


def bell_draw(stream_key, extent, deviation, bound, shards=(), held_as=jnp.bfloat16):
    values = deviation * jax.random.normal(stream_key, extent, jnp.float32)
    if shards:
        values = values * block_scale(stream_key, extent, shards, -0.22, 0.18)
    return jnp.clip(values, -bound, bound).astype(held_as)


def setup_inputs(seed: int = 0) -> dict:
    arg_keys = jax.random.split(jax.random.key(seed), 18)
    tokens = bell_draw(arg_keys[0], (SEQS, LEN, D), 1.0, 6.0, ((1, 16),))
    norm_in = jnp.clip(1.0 + 0.18 * jax.random.normal(arg_keys[1], (D,), jnp.float32), 0.099609375, 1.8984375).astype(jnp.bfloat16)
    query_weight = bell_draw(arg_keys[2], (D, H * (DN + DR)), D ** -0.5, 0.125, ((0, 16), (1, 2)))
    latent_down = bell_draw(arg_keys[3], (D, R + DR), D ** -0.5, 0.125, ((0, 16),))
    latent_norm = jnp.clip(1.0 + 0.18 * jax.random.normal(arg_keys[4], (R,), jnp.float32), 0.099609375, 1.8984375).astype(jnp.bfloat16)
    latent_up = bell_draw(arg_keys[5], (R, H * (DN + DV)), R ** -0.5, 0.25, ((0, 16), (1, 2)))
    output_weight = bell_draw(arg_keys[6], (H * DV, D), (H * DV // 32) ** -0.5, 0.75, ((0, 2), (1, 16)))
    norm_ffn = jnp.clip(1.0 + 0.18 * jax.random.normal(arg_keys[7], (D,), jnp.float32), 0.099609375, 1.8984375).astype(jnp.bfloat16)
    router_weight = bell_draw(arg_keys[8], (D, EXPERTS), (4 * D) ** -0.5, 0.0625, ((0, 16),))
    shared_gate = bell_draw(arg_keys[9], (D, FS), D ** -0.5, 0.125, ((0, 16), (1, 2)))
    shared_up = bell_draw(arg_keys[10], (D, FS), D ** -0.5, 0.125, ((0, 16), (1, 2)))
    shared_down = bell_draw(arg_keys[11], (FS, D), FS ** -0.5, 0.109375, ((0, 2), (1, 16)))
    expert_gate = bell_draw(arg_keys[12], (EXPERTS, D, FE), D ** -0.5, 0.125, ((0, 16), (2, 2)))
    expert_up = bell_draw(arg_keys[13], (EXPERTS, D, FE), D ** -0.5, 0.125, ((0, 16), (2, 2)))
    expert_down = bell_draw(arg_keys[14], (EXPERTS, FE, D), (max(1, FE // (EXPERTS * EXPERTS))) ** -0.5, 2.5, ((0, 16), (1, 2)))
    routes_keys = jax.random.split(jax.random.fold_in(arg_keys[15], 1), SEQS * LEN // BLK)
    routes_turns = jax.random.permutation(jax.random.fold_in(arg_keys[15], 3), SEQS * LEN // BLK)
    routes = jax.vmap(lambda own, number: deal_out(jax.random.fold_in(arg_keys[15], 2), own, number, BLK, EXPERTS, TOPK, CAPB, 2))(routes_keys, routes_turns).reshape((SEQS, LEN, TOPK))
    cotangent = bell_draw(arg_keys[16], (SEQS, LEN, D), 1.0, 6.0, ((1, 16),))
    return dict(tokens=tokens, norm_in=norm_in, query_weight=query_weight, latent_down=latent_down, latent_norm=latent_norm, latent_up=latent_up, output_weight=output_weight, norm_ffn=norm_ffn, router_weight=router_weight, shared_gate=shared_gate, shared_up=shared_up, shared_down=shared_down, expert_gate=expert_gate, expert_up=expert_up, expert_down=expert_down, routes=routes, cotangent=cotangent)


@jax.custom_vjp
def low(v):
    return lax.optimization_barrier(v.astype(jnp.bfloat16)).astype(jnp.float32)

@jax.custom_vjp
def low_back(v):
    return v

def low_keep(v):
    return (low(v), None)

def low_pass(kept, grad):
    return (grad,)

def back_keep(v):
    return (v, None)

def back_low(kept, grad):
    return (low(grad),)
low.defvjp(low_keep, low_pass)
low_back.defvjp(back_keep, back_low)
epsilon = 1e-06
highest = lax.Precision.HIGHEST

def product(left, right):
    return jnp.einsum('...i,ij->...j', left, right, precision=highest)

def root_norm(values, gain):
    return values * lax.rsqrt(lax.optimization_barrier(jnp.mean(values * values, axis=-1, keepdims=True)) + epsilon) * gain

def rotary_tables(positions, width):
    half = width // 2
    frequency = 10000.0 ** (-jnp.arange(half, dtype=jnp.float32) * 2.0 / width)
    angle = positions.astype(jnp.float32)[:, None] * frequency[None, :]
    return (jnp.cos(angle), jnp.sin(angle))

def rotate(values, cosine, sine):
    half = values.shape[-1] // 2
    first = values[..., :half]
    second = values[..., half:]
    return jnp.concatenate([first * cosine - second * sine, second * cosine + first * sine], axis=-1)

def attend_sequence(members):
    query_rows, key_rows = members
    length = key_rows.shape[0]
    allowed = jnp.arange(length)[:, None] >= jnp.arange(length)[None, :]

    def one_head(rows):
        scores = low_back(jnp.einsum('qc,kc->qk', rows, key_rows, precision=highest) * (DN + DR) ** (-0.5))
        scores = jnp.where(allowed, scores, -1e+30)
        top = lax.optimization_barrier(jnp.max(scores, axis=-1, keepdims=True))
        weights = jnp.exp(scores - top)
        shares = low(weights / lax.optimization_barrier(jnp.sum(weights, axis=-1, keepdims=True)))
        return jnp.einsum('qk,kr->qr', shares, key_rows[:, :R], precision=highest)
    return lax.map(jax.checkpoint(one_head), query_rows)

def forward(routes, tokens, norm_in, query_weight, latent_down, latent_norm, latent_up, output_weight, norm_ffn, router_weight, shared_gate, shared_up, shared_down, expert_gate, expert_up, expert_down):
    sequences, length, width = tokens.shape
    cosine, sine = rotary_tables(jnp.arange(length), DR)
    input_low = low(root_norm(tokens, norm_in))
    query_raw = low_back(product(input_low, query_weight)).reshape(sequences, length, H, DN + DR)
    query_low = low(jnp.concatenate([query_raw[..., :DN], rotate(query_raw[..., DN:], cosine[:, None, :], sine[:, None, :])], axis=-1))
    up_view = latent_up.reshape(R, H, DN + DV)
    absorbed = jnp.einsum('slhn,rhn->shlr', query_low[..., :DN], up_view[..., :DN], precision=highest)
    query_rows = low_back(low(jnp.concatenate([absorbed, jnp.transpose(query_low[..., DN:], (0, 2, 1, 3))], axis=-1)))
    latent_raw = low_back(product(input_low, latent_down))
    key_rows = low(jnp.concatenate([root_norm(latent_raw[..., :R], latent_norm), rotate(latent_raw[..., R:], cosine, sine)], axis=-1))
    latent_out = low_back(low(lax.map(attend_sequence, (query_rows, key_rows))))
    head_out = low_back(low(jnp.einsum('shlr,rhv->slhv', latent_out, up_view[..., DN:], precision=highest))).reshape(sequences, length, H * DV)
    hidden_in = tokens + low_back(product(head_out, output_weight))
    ffn_low = low(root_norm(hidden_in, norm_ffn))
    shares = jax.nn.softmax(product(ffn_low, router_weight), axis=-1)
    shared_g = low_back(product(ffn_low, shared_gate))
    shared_u = low_back(product(ffn_low, shared_up))
    shared_result = low_back(product(low(jax.nn.silu(shared_g) * shared_u), shared_down))
    flat_rows = ffn_low.reshape(-1, width)
    flat_shares = shares.reshape(-1, EXPERTS)
    flat_routes = routes.reshape(-1)
    owner = (jnp.arange(flat_routes.shape[0]) // TOPK).astype(jnp.int32)
    limit = SEQS * N_CTX * CAPB

    def run_expert(members):
        index, gate_weight, up_weight, down_weight = members
        member = flat_routes == index
        order = jnp.argsort(jnp.where(member, 0, 1).astype(jnp.int32), stable=True)[:limit]
        valid = member[order]
        rows_at = owner[order]
        rows = jnp.where(valid[:, None], flat_rows[rows_at], 0.0)
        gate_pre = low_back(product(rows, gate_weight))
        up_pre = low_back(product(rows, up_weight))
        result = low_back(product(low(jax.nn.silu(gate_pre) * up_pre), down_weight))
        weight = jnp.where(valid, flat_shares[rows_at, index], 0.0)
        return (result * weight[:, None], rows_at)
    weighted, places = lax.map(jax.checkpoint(run_expert), (jnp.arange(EXPERTS, dtype=jnp.int32), expert_gate, expert_up, expert_down))
    routed = jnp.zeros_like(flat_rows).at[places.reshape(-1)].add(weighted.reshape(-1, width)).reshape(sequences, length, width)
    return hidden_in + shared_result + routed

def reference(tokens, norm_in, query_weight, latent_down, latent_norm, latent_up, output_weight, norm_ffn, router_weight, shared_gate, shared_up, shared_down, expert_gate, expert_up, expert_down, routes, cotangent):
    floats = [member.astype(jnp.float32) for member in (tokens, norm_in, query_weight, latent_down, latent_norm, latent_up, output_weight, norm_ffn, router_weight, shared_gate, shared_up, shared_down, expert_gate, expert_up, expert_down)]
    output, pullback = jax.vjp(partial(forward, routes), *floats)
    grads = pullback(cotangent.astype(jnp.float32))
    return (output.astype(jnp.bfloat16), grads[0], grads[1], grads[2], grads[3], grads[4], grads[5], grads[6], grads[7], grads[8], grads[9], grads[10], grads[11], grads[12], grads[13], grads[14])
```

```python
import jax
import jax.numpy as jnp
from jax import lax
from jax.sharding import Mesh, PartitionSpec as P

DN = 128
DR = 64
DV = 128
R = 512
TOPK = 6


epsilon = 1e-06
highest = lax.Precision.HIGHEST


def shifted(value, axis, steps):
    count = lax.axis_size(axis)
    pairs = [(source, (source + steps) % count) for source in range(count)]
    return lax.ppermute(value, axis, pairs)


def root_norm(values, gain):
    inverse = lax.rsqrt(jnp.mean(values * values, axis=-1, keepdims=True) + epsilon)
    unit = values * inverse
    return (unit * gain, unit, inverse)


def root_norm_back(upstream, unit, inverse, gain):
    scaled = upstream * gain
    inner = jnp.mean(scaled * unit, axis=-1, keepdims=True)
    leading = tuple(range(upstream.ndim - 1))
    return (inverse * (scaled - unit * inner), jnp.sum(upstream * unit, axis=leading))


def rotary_tables(positions, width):
    half = width // 2
    frequency = 10000.0 ** (-jnp.arange(half, dtype=jnp.float32) * 2.0 / width)
    angle = positions.astype(jnp.float32)[:, None] * frequency[None, :]
    return (jnp.cos(angle), jnp.sin(angle))


def rotate(values, cosine, sine):
    half = values.shape[-1] // 2
    first = values[..., :half]
    second = values[..., half:]
    return jnp.concatenate(
        [first * cosine - second * sine, second * cosine + first * sine], axis=-1
    )


def silu_slope(values):
    sigmoid = jax.nn.sigmoid(values)
    return sigmoid * (1.0 + values * (1.0 - sigmoid))


def fetch_weights(
    norm_in,
    query_weight,
    latent_down,
    latent_norm,
    latent_up,
    output_weight,
    norm_ffn,
    router_weight,
    shared_gate,
    shared_up,
    shared_down,
):
    return (
        lax.all_gather(norm_in, "ctx", axis=0, tiled=True),
        lax.all_gather(query_weight, "ctx", axis=0, tiled=True),
        lax.all_gather(latent_down, "ctx", axis=0, tiled=True),
        lax.all_gather(latent_norm, "ctx", axis=0, tiled=True),
        lax.all_gather(latent_up, "ctx", axis=0, tiled=True),
        lax.all_gather(output_weight, "ctx", axis=1, tiled=True),
        lax.all_gather(norm_ffn, "ctx", axis=0, tiled=True),
        lax.all_gather(router_weight, "ctx", axis=0, tiled=True),
        lax.all_gather(shared_gate, "ctx", axis=0, tiled=True),
        lax.all_gather(shared_up, "ctx", axis=0, tiled=True),
        lax.all_gather(shared_down, "ctx", axis=1, tiled=True),
    )


def shards(
    tokens,
    norm_in,
    query_weight,
    latent_down,
    latent_norm,
    latent_up,
    output_weight,
    norm_ffn,
    router_weight,
    shared_gate,
    shared_up,
    shared_down,
    expert_gate,
    expert_up,
    expert_down,
    routes,
    cotangent,
):
    context_count = lax.axis_size("ctx")
    context_index = lax.axis_index("ctx")
    lead = (lax.axis_index("wa") == 0).astype(jnp.float32)
    sequences, block, width = tokens.shape
    local_experts = expert_gate.shape[0]
    experts = context_count * local_experts
    capacity = max(2, block * TOPK * 4 // (3 * experts))
    scale = (DN + DR) ** (-0.5)
    gathered = fetch_weights(
        norm_in,
        query_weight,
        latent_down,
        latent_norm,
        latent_up,
        output_weight,
        norm_ffn,
        router_weight,
        shared_gate,
        shared_up,
        shared_down,
    )
    (
        full_norm_in,
        full_query,
        full_down,
        full_latent_norm,
        full_up,
        full_output,
        full_norm_ffn,
        full_router,
        full_shared_gate,
        full_shared_up,
        full_shared_down,
    ) = gathered
    heads_here = full_up.shape[1] // (DN + DV)
    positions = context_index * block + jnp.arange(block)
    cosine, sine = rotary_tables(positions, DR)
    source = tokens.astype(jnp.float32)
    normed_in, unit_in, inverse_in = root_norm(source, full_norm_in.astype(jnp.float32))
    input_low = normed_in.astype(jnp.bfloat16)
    query_raw = jnp.dot(input_low, full_query, preferred_element_type=jnp.float32).reshape(
        sequences, block, heads_here, DN + DR
    )
    query_low = jnp.concatenate(
        [query_raw[..., :DN], rotate(query_raw[..., DN:], cosine[:, None, :], sine[:, None, :])],
        axis=-1,
    ).astype(jnp.bfloat16)
    up_view = full_up.reshape(R, heads_here, DN + DV)
    key_up = up_view[..., :DN]
    value_up = up_view[..., DN:]
    absorbed = jnp.einsum(
        "sbhn,rhn->shbr", query_low[..., :DN], key_up, preferred_element_type=jnp.float32
    )
    query_rows = jnp.concatenate(
        [absorbed.astype(jnp.bfloat16), jnp.transpose(query_low[..., DN:], (0, 2, 1, 3))], axis=-1
    )
    latent_raw = jnp.dot(input_low, full_down, preferred_element_type=jnp.float32)
    latent_scaled, latent_unit, latent_inverse = root_norm(
        latent_raw[..., :R], full_latent_norm.astype(jnp.float32)
    )
    key_rows = jnp.concatenate(
        [latent_scaled, rotate(latent_raw[..., R:], cosine, sine)], axis=-1
    ).astype(jnp.bfloat16)
    piece = lax.all_gather(key_rows, "ctx", axis=1, tiled=True)
    top = jnp.full((sequences, heads_here, block), -1e30, jnp.float32)
    scores = (
        jnp.einsum("shqc,skc->shqk", query_rows, piece, preferred_element_type=jnp.float32) * scale
    )
    key_positions = jnp.arange(piece.shape[1])
    allowed = positions[:, None] >= key_positions[None, :]
    scores = jnp.where(allowed, scores, -1e30)
    new_top = jnp.maximum(top, jnp.max(scores, axis=-1))
    weights = jnp.where(allowed, jnp.exp(scores - new_top[..., None]), 0.0)
    total = jnp.sum(weights, axis=-1)
    weights_high = weights.astype(jnp.bfloat16)
    weights_rest = (weights - weights_high.astype(jnp.float32)).astype(jnp.bfloat16)
    running = jnp.einsum(
        "shqk,skr->shqr", weights_high, piece[..., :R], preferred_element_type=jnp.float32
    )
    remainder = jnp.einsum(
        "shqk,skr->shqr", weights_rest, piece[..., :R], preferred_element_type=jnp.float32
    )
    top, total, running, remainder = (new_top, total, running, remainder)
    log_total = top + jnp.log(total)
    latent_out = (running / total[..., None]).astype(jnp.bfloat16)
    latent_exact = (running + remainder) / total[..., None]
    head_out = (
        jnp.einsum("shbr,rhv->sbhv", latent_out, value_up, preferred_element_type=jnp.float32)
        .astype(jnp.bfloat16)
        .reshape(sequences, block, heads_here * DV)
    )
    attention_part = jnp.dot(head_out, full_output, preferred_element_type=jnp.float32)
    hidden_in = source + lax.psum(attention_part, "wa")
    normed_ffn, unit_ffn, inverse_ffn = root_norm(hidden_in, full_norm_ffn.astype(jnp.float32))
    ffn_low = normed_ffn.astype(jnp.bfloat16)
    shares = jax.nn.softmax(
        jnp.dot(ffn_low, full_router, preferred_element_type=jnp.float32), axis=-1
    )
    shared_g = jnp.dot(ffn_low, full_shared_gate, preferred_element_type=jnp.float32)
    shared_u = jnp.dot(ffn_low, full_shared_up, preferred_element_type=jnp.float32)
    shared_silu = jax.nn.silu(shared_g)
    shared_activation = (shared_silu * shared_u).astype(jnp.bfloat16)
    shared_part = jnp.dot(shared_activation, full_shared_down, preferred_element_type=jnp.float32)
    expert_ids = jnp.arange(experts, dtype=jnp.int32)
    chosen = (
        (routes[..., None] == expert_ids)
        .astype(jnp.int32)
        .reshape(sequences, block * TOPK, experts)
    )
    earlier = jnp.cumsum(chosen, axis=1) - chosen
    slot_of = jnp.sum(earlier * chosen, axis=-1).reshape(sequences, block, TOPK)
    slot_ids = jnp.arange(capacity, dtype=jnp.int32)
    hit = (routes[None, :, :, :, None] == expert_ids[:, None, None, None, None]) & (
        slot_of[None, :, :, :, None] == slot_ids[None, None, None, None, :]
    )
    dispatch = jnp.transpose(jnp.any(hit, axis=3), (0, 1, 3, 2)).astype(jnp.float32)
    send = (
        jnp.einsum(
            "escb,sbd->escd",
            dispatch.astype(jnp.bfloat16),
            ffn_low,
            preferred_element_type=jnp.float32,
        )
        .astype(jnp.bfloat16)
        .reshape(experts, sequences * capacity, width)
    )
    slot_share = jnp.einsum("escb,sbe->esc", dispatch, shares, precision=highest)
    received = lax.all_to_all(send, "ctx", split_axis=0, concat_axis=0, tiled=True)
    count = received.shape[1]
    rows = received.reshape(context_count, local_experts, count, width)
    gate_pre = jnp.einsum("nesd,edf->nesf", rows, expert_gate, preferred_element_type=jnp.float32)
    up_pre = jnp.einsum("nesd,edf->nesf", rows, expert_up, preferred_element_type=jnp.float32)
    activation = (jax.nn.silu(gate_pre) * up_pre).astype(jnp.bfloat16)
    result = jnp.einsum(
        "nesf,efd->nesd", activation, expert_down, preferred_element_type=jnp.float32
    ).reshape(experts, count, width)
    returned = lax.all_to_all(result, "ctx", split_axis=0, concat_axis=0, tiled=True)
    hidden_units = gate_pre.shape[-1]
    returned, received, gate_keep, up_keep = (
        returned,
        received,
        gate_pre.reshape(experts, count, hidden_units),
        up_pre.reshape(experts, count, hidden_units),
    )
    returned = returned.reshape(experts, sequences, capacity, width)
    routed_part = jnp.einsum(
        "escb,escd->sbd", dispatch, returned * slot_share[..., None], precision=highest
    )
    output = hidden_in + lax.psum(shared_part + routed_part, "wa")
    gathered = fetch_weights(
        norm_in,
        query_weight,
        latent_down,
        latent_norm,
        latent_up,
        output_weight,
        norm_ffn,
        router_weight,
        shared_gate,
        shared_up,
        shared_down,
    )
    (
        full_norm_in,
        full_query,
        full_down,
        full_latent_norm,
        full_up,
        full_output,
        full_norm_ffn,
        full_router,
        full_shared_gate,
        full_shared_up,
        full_shared_down,
    ) = gathered
    up_view = full_up.reshape(R, heads_here, DN + DV)
    key_up = up_view[..., :DN]
    value_up = up_view[..., DN:]
    grad_y = cotangent.astype(jnp.float32)
    shared_grad = jnp.einsum(
        "sbd,fd->sbf", cotangent, full_shared_down, preferred_element_type=jnp.float32
    )
    shared_gate_grad = (shared_grad * shared_u * silu_slope(shared_g)).astype(jnp.bfloat16)
    shared_up_grad = (shared_grad * shared_silu).astype(jnp.bfloat16)
    grad_shared_down = jnp.einsum(
        "sbf,sbd->fd", shared_activation, cotangent, preferred_element_type=jnp.float32
    )
    grad_shared_gate = jnp.einsum(
        "sbd,sbf->df", ffn_low, shared_gate_grad, preferred_element_type=jnp.float32
    )
    grad_shared_up = jnp.einsum(
        "sbd,sbf->df", ffn_low, shared_up_grad, preferred_element_type=jnp.float32
    )
    ffn_grad = jnp.einsum(
        "sbf,df->sbd", shared_gate_grad, full_shared_gate, preferred_element_type=jnp.float32
    )
    ffn_grad = ffn_grad + jnp.einsum(
        "sbf,df->sbd", shared_up_grad, full_shared_up, preferred_element_type=jnp.float32
    )
    grad_at_slots = jnp.einsum("escb,sbd->escd", dispatch, grad_y, precision=highest)
    slot_grads = (
        (grad_at_slots * slot_share[..., None])
        .astype(jnp.bfloat16)
        .reshape(experts, sequences * capacity, width)
    )
    slot_dot = jnp.sum(returned * grad_at_slots, axis=-1)
    share_grad = jnp.einsum("escb,esc->sbe", dispatch, slot_dot, precision=highest)
    logit_grad = shares * (share_grad - jnp.sum(shares * share_grad, axis=-1, keepdims=True))
    grad_router = jnp.einsum(
        "sbd,sbe->de", ffn_low.astype(jnp.float32), logit_grad, precision=highest
    )
    ffn_grad = ffn_grad + jnp.einsum(
        "sbe,de->sbd", logit_grad, full_router.astype(jnp.float32), precision=highest
    )
    slot_back = lax.all_to_all(slot_grads, "ctx", split_axis=0, concat_axis=0, tiled=True).reshape(
        context_count, local_experts, -1, width
    )
    rows = received.reshape(context_count, local_experts, -1, width)
    gate_pre = gate_keep.reshape(context_count, local_experts, -1, gate_keep.shape[-1])
    up_pre = up_keep.reshape(context_count, local_experts, -1, up_keep.shape[-1])
    hidden_grad = jnp.einsum(
        "nesd,efd->nesf", slot_back, expert_down, preferred_element_type=jnp.float32
    )
    silu_gate = jax.nn.silu(gate_pre)
    gate_grad = (hidden_grad * up_pre * silu_slope(gate_pre)).astype(jnp.bfloat16)
    up_grad = (hidden_grad * silu_gate).astype(jnp.bfloat16)
    activation = (silu_gate * up_pre).astype(jnp.bfloat16)
    grad_expert_down = jnp.einsum(
        "nesf,nesd->efd", activation, slot_back, preferred_element_type=jnp.float32
    )
    grad_expert_gate = jnp.einsum(
        "nesd,nesf->edf", rows, gate_grad, preferred_element_type=jnp.float32
    )
    grad_expert_up = jnp.einsum("nesd,nesf->edf", rows, up_grad, preferred_element_type=jnp.float32)
    rows_grad = jnp.einsum(
        "nesf,edf->nesd", gate_grad, expert_gate, preferred_element_type=jnp.float32
    )
    rows_grad = rows_grad + jnp.einsum(
        "nesf,edf->nesd", up_grad, expert_up, preferred_element_type=jnp.float32
    )
    slot_grad = lax.all_to_all(
        rows_grad.reshape(experts, -1, width), "ctx", split_axis=0, concat_axis=0, tiled=True
    ).reshape(experts, sequences, capacity, width)
    ffn_grad = ffn_grad + jnp.einsum("escb,escd->sbd", dispatch, slot_grad, precision=highest)
    hidden_part, grad_norm_ffn = root_norm_back(
        ffn_grad, unit_ffn, inverse_ffn, full_norm_ffn.astype(jnp.float32)
    )
    grad_hidden = grad_y + lax.psum(hidden_part, "wa")
    attention_grad = grad_hidden.astype(jnp.bfloat16)
    grad_output = jnp.einsum(
        "sbk,sbd->kd", head_out, attention_grad, preferred_element_type=jnp.float32
    )
    head_grad = (
        jnp.einsum("sbd,kd->sbk", attention_grad, full_output, preferred_element_type=jnp.float32)
        .astype(jnp.bfloat16)
        .reshape(sequences, block, heads_here, DV)
    )
    grad_value_up = jnp.einsum(
        "shbr,sbhv->rhv", latent_out, head_grad, preferred_element_type=jnp.float32
    )
    latent_out_grad = jnp.einsum(
        "sbhv,rhv->shbr", head_grad, value_up, preferred_element_type=jnp.float32
    ).astype(jnp.bfloat16)
    row_dot = jnp.sum(latent_out_grad.astype(jnp.float32) * latent_exact, axis=-1)

    def turn_body(turn, carry):
        keys_here, key_grad, query_grad = carry
        source_index = (context_index + turn) % context_count
        key_positions = source_index * block + jnp.arange(block)
        allowed = positions[:, None] >= key_positions[None, :]
        scores = (
            jnp.einsum("shqc,skc->shqk", query_rows, keys_here, preferred_element_type=jnp.float32)
            * scale
        )
        weights = jnp.where(allowed[None, None], jnp.exp(scores - log_total[..., None]), 0.0)
        weight_grad = jnp.einsum(
            "shqr,skr->shqk",
            latent_out_grad,
            keys_here[..., :R],
            preferred_element_type=jnp.float32,
        )
        score_grad = (weights * (weight_grad - row_dot[..., None])).astype(jnp.bfloat16)
        query_grad = (
            query_grad
            + jnp.einsum(
                "shqk,skc->shqc", score_grad, keys_here, preferred_element_type=jnp.float32
            )
            * scale
        )
        key_part = (
            jnp.einsum("shqk,shqc->skc", score_grad, query_rows, preferred_element_type=jnp.float32)
            * scale
        )
        value_part = jnp.einsum(
            "shqk,shqr->skr",
            weights.astype(jnp.bfloat16),
            latent_out_grad,
            preferred_element_type=jnp.float32,
        )
        key_grad = key_grad + key_part + jnp.pad(value_part, ((0, 0), (0, 0), (0, DR)))
        keys_next = shifted(keys_here, "ctx", -1)
        grad_next = shifted(key_grad, "ctx", -1)
        return (keys_next, grad_next, query_grad)

    start_back = (
        key_rows,
        jnp.zeros((sequences, block, R + DR), jnp.float32),
        jnp.zeros((sequences, heads_here, block, R + DR), jnp.float32),
    )
    unused_keys, key_grad, query_grad = lax.fori_loop(0, context_count, turn_body, start_back)
    key_grad_total = lax.psum(key_grad, "wa")
    query_grad_low = query_grad.astype(jnp.bfloat16)
    absorbed_grad = query_grad_low[..., :R]
    rope_query_grad = jnp.transpose(query_grad_low[..., R:], (0, 2, 1, 3)).astype(jnp.float32)
    grad_key_up = jnp.einsum(
        "shbr,sbhn->rhn", absorbed_grad, query_low[..., :DN], preferred_element_type=jnp.float32
    )
    nope_grad = jnp.einsum(
        "shbr,rhn->sbhn", absorbed_grad, key_up, preferred_element_type=jnp.float32
    )
    rope_raw_grad = rotate(rope_query_grad, cosine[:, None, :], -sine[:, None, :])
    query_raw_grad = (
        jnp.concatenate([nope_grad, rope_raw_grad], axis=-1)
        .astype(jnp.bfloat16)
        .reshape(sequences, block, heads_here * (DN + DR))
    )
    grad_query = jnp.einsum(
        "sbd,sbk->dk", input_low, query_raw_grad, preferred_element_type=jnp.float32
    )
    input_part = jnp.einsum(
        "sbk,dk->sbd", query_raw_grad, full_query, preferred_element_type=jnp.float32
    )
    grad_latent_up = jnp.concatenate([grad_key_up, grad_value_up], axis=-1).reshape(
        R, heads_here * (DN + DV)
    )
    latent_grad, grad_latent_norm = root_norm_back(
        key_grad_total[..., :R], latent_unit, latent_inverse, full_latent_norm.astype(jnp.float32)
    )
    rope_key_grad = rotate(key_grad_total[..., R:], cosine, -sine)
    latent_raw_grad = jnp.concatenate([latent_grad, rope_key_grad], axis=-1).astype(jnp.bfloat16)
    grad_down = jnp.einsum(
        "sbd,sbc->dc", input_low, latent_raw_grad, preferred_element_type=jnp.float32
    )
    input_part = input_part + lead * jnp.einsum(
        "sbc,dc->sbd", latent_raw_grad, full_down, preferred_element_type=jnp.float32
    )
    source_part, grad_norm_in = root_norm_back(
        input_part, unit_in, inverse_in, full_norm_in.astype(jnp.float32)
    )
    summed = lax.psum((source_part, grad_norm_in, grad_norm_ffn, grad_router), "wa")
    tokens_gradient = grad_hidden + summed[0]
    reduced = (
        lax.psum_scatter(summed[1], "ctx", scatter_dimension=0, tiled=True),
        lax.psum_scatter(grad_query, "ctx", scatter_dimension=0, tiled=True),
        lax.psum_scatter(grad_down, "ctx", scatter_dimension=0, tiled=True),
        lax.psum_scatter(grad_latent_norm, "ctx", scatter_dimension=0, tiled=True),
        lax.psum_scatter(grad_latent_up, "ctx", scatter_dimension=0, tiled=True),
        lax.psum_scatter(grad_output, "ctx", scatter_dimension=1, tiled=True),
        lax.psum_scatter(summed[2], "ctx", scatter_dimension=0, tiled=True),
        lax.psum_scatter(summed[3], "ctx", scatter_dimension=0, tiled=True),
        lax.psum_scatter(grad_shared_gate, "ctx", scatter_dimension=0, tiled=True),
        lax.psum_scatter(grad_shared_up, "ctx", scatter_dimension=0, tiled=True),
        lax.psum_scatter(grad_shared_down, "ctx", scatter_dimension=1, tiled=True),
    )
    return (
        output.astype(jnp.bfloat16),
        tokens_gradient,
        reduced[0],
        reduced[1],
        reduced[2],
        reduced[3],
        reduced[4],
        reduced[5],
        reduced[6],
        reduced[7],
        reduced[8],
        reduced[9],
        reduced[10],
        grad_expert_gate,
        grad_expert_up,
        grad_expert_down,
    )


CTX = ("z", "x", "c")


def swap(value, axis):
    return lax.ppermute(value, axis, [(0, 1), (1, 0)])


def from_z(value, steps):
    count = lax.axis_size("z")
    return lax.ppermute(value, "z", [((i + steps) % count, i) for i in range(count)])


def to_z(value, steps):
    count = lax.axis_size("z")
    return lax.ppermute(value, "z", [(i, (i + steps) % count) for i in range(count)])


def trade(value, axes):
    return lax.all_to_all(value, axes, split_axis=0, concat_axis=0, tiled=True)


def add(left, right):
    return left.astype(jnp.float32) + right.astype(jnp.float32)


def low(value):
    return value.astype(jnp.bfloat16)


def dot(left, right):
    return jnp.dot(left, right, preferred_element_type=jnp.float32)


def dot_nt(left, right):
    return lax.dot_general(
        left, right, (((1,), (1,)), ((), ())), preferred_element_type=jnp.float32
    )


def dot_tn(left, right):
    return lax.dot_general(
        left, right, (((0,), (0,)), ((), ())), preferred_element_type=jnp.float32
    )


def by_own(value, axis_name, dim):
    flipped = jnp.flip(value, axis=dim)
    return jnp.where(lax.axis_index(axis_name) == 0, value, flipped)


def gather_z(value):
    count = lax.axis_size("z")
    return trade(jnp.broadcast_to(value[None], (count,) + value.shape), "z")


def gather_ctx(value):
    slabs = gather_z(value)
    slabs = by_own(jnp.stack([slabs, swap(slabs, "x")], axis=1), "x", 1)
    slabs = by_own(jnp.stack([slabs, swap(slabs, "c")], axis=2), "c", 2)
    return slabs.reshape((-1,) + value.shape)


def gather_plane(rows):
    half = rows.shape[0] // 2
    over_x = swap(rows, "x")
    over_y = swap(rows, "y")
    both = jnp.concatenate([swap(over_y[:half], "x"), swap(over_x[half:], "y")], axis=0)
    return jnp.stack([jnp.stack([rows, over_y]), jnp.stack([over_x, both])])


def scatter_plane(rows):
    half = rows.shape[2] // 2
    lower, upper = (rows[:, :, :half], rows[:, :, half:])
    lower = low(add(lower[0], swap(lower[1], "x")))
    upper = low(add(upper[:, 0], swap(upper[:, 1], "y")))
    lower = add(lower[0], swap(lower[1], "y"))
    upper = add(upper[0], swap(upper[1], "x"))
    return jnp.concatenate([lower, upper], axis=0)


def gather_all(rows):
    count = lax.axis_size("z")
    slabs = jnp.concatenate([rows] + [from_z(rows, s) for s in range(1, count)], axis=0)
    own = gather_plane(slabs)
    return (own, swap(own, "c"))


def scatter_all(own, other):
    count = lax.axis_size("z")
    own = low(add(own, swap(other, "c")))
    slabs = scatter_plane(own)
    block = slabs.shape[0] // count
    sent = low(slabs)
    total = slabs[:block]
    for s in range(1, count):
        total = total + to_z(sent[s * block : (s + 1) * block], s).astype(jnp.float32)
    return total


def sum_z(value):
    return jnp.sum(trade(value, "z").astype(jnp.float32).reshape((lax.axis_size("z"), -1) + value.shape[1:]), axis=0)


def both_halves(rows):
    other = swap(rows, "y")
    return by_own(jnp.stack([rows, other]), "y", 0)


def dense_shards(
    tokens,
    norm_in,
    query_weight,
    latent_down,
    latent_norm,
    latent_up,
    output_weight,
    norm_ffn,
    router_weight,
    shared_gate,
    shared_up,
    shared_down,
    expert_gate,
    expert_up,
    expert_down,
    routes,
    cotangent,
):
    zs = lax.axis_size("z")
    z, x, c = (lax.axis_index("z"), lax.axis_index("x"), lax.axis_index("c"))
    me = (z * 2 + x) * 2 + c
    sequences, block, width = tokens.shape
    count = 4 * zs
    rows_here = width // count
    slab = 4 * block
    experts = router_weight.shape[1]
    hidden_here = expert_gate.shape[2]
    shared_here = shared_gate.shape[1] // count
    used = hidden_here + shared_here
    padded = -(-(used + experts) // 128) * 128
    heads = latent_up.shape[1] // (4 * (DN + DV))
    query_columns = heads * (DN + DR)
    rank_rows = R // count
    head_rows = heads * DV
    scale = (DN + DR) ** (-0.5)

    extra = jnp.zeros((rows_here, 1), jnp.bfloat16)
    latent_column = jnp.pad(latent_norm, (0, rows_here - rank_rows))[:, None]
    small = jnp.concatenate(
        [
            latent_down,
            router_weight,
            norm_in[:, None],
            norm_ffn[:, None],
            latent_column,
            routes.reshape(sequences * block, TOPK).astype(jnp.bfloat16),
        ],
        axis=1,
    )
    small = jnp.pad(small, ((0, 0), (0, -small.shape[1] % 128)))
    small = gather_ctx(small)
    small_rows = small.reshape(width, -1)
    at = R + DR
    full_down = small_rows[:, :at]
    full_router = small_rows[:, at : at + experts]
    full_norm_in = small_rows[:, at + experts].astype(jnp.float32)
    full_norm_ffn = small_rows[:, at + experts + 1].astype(jnp.float32)
    full_latent_norm = small[:, :rank_rows, at + experts + 2].reshape(R).astype(jnp.float32)
    all_routes = small[:, :, at + experts + 3 : at + experts + 3 + TOPK]

    by_heads = jnp.transpose(query_weight.reshape(rows_here, 4, query_columns), (1, 0, 2))
    query_here = gather_z(trade(by_heads, ("x", "c"))).reshape(width, query_columns)
    up_part = jnp.transpose(
        latent_up.reshape(rank_rows, 4, heads * (DN + DV)), (1, 0, 2)
    ).reshape(4, -1, 128)
    out_part = jnp.transpose(output_weight.reshape(4, heads, DV, rows_here), (0, 2, 1, 3)).reshape(
        4, DV, heads * rows_here
    )
    up_columns = heads * (DN + DV) * rank_rows // DV
    up_part = up_part.reshape(4, DV, up_columns)
    by_heads = jnp.concatenate([up_part, out_part], axis=2)
    up_out = gather_z(trade(by_heads, ("x", "c"))).reshape(count, DV, -1)
    up_here = up_out[:, :, :up_columns].reshape(R, heads, DN + DV)
    key_up = up_here[..., :DN]
    value_up = up_here[..., DN:]
    out_here = jnp.transpose(
        up_out[:, :, up_columns:].reshape(count, DV, heads, rows_here), (2, 1, 0, 3)
    ).reshape(head_rows, width)

    shared_mine = jnp.concatenate(
        [
            shared_gate.T.reshape(count, shared_here, rows_here),
            shared_up.T.reshape(count, shared_here, rows_here),
            shared_down.reshape(count, shared_here, rows_here),
        ],
        axis=1,
    )
    shared_here_rows = jnp.transpose(trade(shared_mine, CTX), (1, 0, 2)).reshape(-1, width)
    gate_rows = shared_here_rows[:shared_here]
    up_rows = shared_here_rows[shared_here : 2 * shared_here]
    down_rows = shared_here_rows[2 * shared_here :]
    first = jnp.concatenate(
        [
            expert_gate[0],
            gate_rows.T,
            full_router,
            jnp.zeros((width, padded - used - experts), jnp.bfloat16),
            expert_up[0],
            up_rows.T,
            jnp.zeros((width, padded - used), jnp.bfloat16),
        ],
        axis=1,
    )
    second = jnp.concatenate(
        [expert_down[0], down_rows, jnp.zeros((padded - used, width), jnp.bfloat16)], axis=0
    )

    mine = by_own(tokens, "y", 0)
    line = jnp.stack([mine, swap(mine, "x")], axis=1)
    line = jnp.stack([line, swap(line, "c")], axis=1)
    source = line.reshape(sequences * slab, width).astype(jnp.float32)
    grad_mine = by_own(cotangent, "y", 0)[0]
    grads_own, grads_other = gather_all(grad_mine)

    def places(turn):
        columns = jnp.arange(2)
        base = ((z + turn) % zs) * 4 + (x ^ columns[None, :]) * 2 + (c ^ columns[:, None])
        return (base[:, :, None] * block + jnp.arange(block)).reshape(slab)

    positions = places(0)
    key_positions = jnp.concatenate([places(turn) for turn in range(zs)])
    cosine, sine = rotary_tables(positions, DR)
    normed, unit_in, inverse_in = root_norm(source, full_norm_in)
    input_low = low(normed)
    query_raw = dot(input_low, query_here).reshape(sequences, slab, heads, DN + DR)
    query_low = low(
        jnp.concatenate(
            [
                query_raw[..., :DN],
                rotate(query_raw[..., DN:], cosine[:, None, :], sine[:, None, :]),
            ],
            axis=-1,
        )
    )
    absorbed = jnp.einsum(
        "sbhn,rhn->shbr", query_low[..., :DN], key_up, preferred_element_type=jnp.float32
    )
    query_rows = jnp.concatenate(
        [low(absorbed), jnp.transpose(query_low[..., DN:], (0, 2, 1, 3))], axis=-1
    )
    latent_raw = dot(input_low, full_down).reshape(sequences, slab, R + DR)
    latent_scaled, latent_unit, latent_inverse = root_norm(latent_raw[..., :R], full_latent_norm)
    key_slab = low(
        jnp.concatenate([latent_scaled, rotate(latent_raw[..., R:], cosine, sine)], axis=-1)
    )
    half_keys = key_slab[:, : slab // 2]
    far = jnp.stack([from_z(half_keys, s) for s in range(1, zs)], axis=1)
    far = jnp.stack([far, swap(far, "c")], axis=2).reshape(sequences, (zs - 1) * slab, R + DR)
    keys = jnp.concatenate([key_slab, far], axis=1)

    scores = (
        jnp.einsum("shqc,skc->shqk", query_rows, keys, preferred_element_type=jnp.float32) * scale
    )
    allowed = positions[:, None] >= key_positions[None, :]
    scores = jnp.where(allowed, scores, -1e30)
    top = jnp.max(scores, axis=-1, keepdims=True)
    weights = jnp.exp(scores - top)
    prob = weights / jnp.sum(weights, axis=-1, keepdims=True)
    prob_low = low(prob)
    latent_out = low(
        jnp.einsum("shqk,skr->shqr", prob_low, keys[..., :R], preferred_element_type=jnp.float32)
    )
    head_out = low(
        jnp.einsum("shbr,rhv->sbhv", latent_out, value_up, preferred_element_type=jnp.float32)
    ).reshape(sequences * slab, head_rows)

    def scatter_slab(partial):
        parts = partial.reshape(2, 2, 2, block, -1)
        kept = low(add(parts[:, 0], swap(parts[:, 1], "c")))
        return scatter_plane(jnp.transpose(kept, (1, 0, 2, 3)))

    def gather_slab(rows):
        plane = jnp.transpose(gather_plane(rows), (1, 0, 2, 3))
        return jnp.stack([plane, swap(plane, "c")], axis=1).reshape(sequences * slab, -1)

    attention = scatter_slab(low(dot(head_out, out_here)))
    hidden_in = mine[0].astype(jnp.float32) + attention
    normed_ffn, unit_ffn, inverse_ffn = root_norm(hidden_in, full_norm_ffn)
    ffn_low = low(normed_ffn)
    shares = jax.nn.softmax(dot(ffn_low, full_router), axis=-1)
    ffn_own, ffn_other = gather_all(ffn_low)

    relative = all_routes.reshape(zs, 2, 2, sequences, block, TOPK)
    relative = by_own(by_own(by_own(relative, "x", 1), "c", 2), "y", 3)
    relative = jnp.roll(relative, -z, axis=0)
    routed = jnp.any(relative == me.astype(jnp.bfloat16), axis=-1)
    routed = jnp.transpose(routed, (2, 1, 3, 0, 4)).reshape(2, -1).astype(jnp.float32)
    column = jnp.arange(padded)
    is_expert = (column < hidden_here)[None, :]
    is_shared = ((column >= hidden_here) & (column < used))[None, :]
    picked = (jnp.arange(experts) == me)[None, :]

    def feed(rows, grads, named):
        rows = rows.reshape(-1, width)
        grads = grads.reshape(-1, width)
        both = dot(rows, first)
        gate = both[:, :padded]
        up = both[:, padded:]
        chances = jax.nn.softmax(gate[:, used : used + experts], axis=-1)
        share = jnp.sum(jnp.where(picked, chances, 0.0), axis=-1) * named
        factor = jnp.where(is_expert, share[:, None], jnp.where(is_shared, 1.0, 0.0))
        sigmoid = jax.nn.sigmoid(gate)
        silu = gate * sigmoid
        slope = sigmoid * (1.0 + gate * (1.0 - sigmoid))
        act = silu * up
        back = dot_nt(grads, second)
        gain = jnp.sum(jnp.where(is_expert, low(act).astype(jnp.float32) * back, 0.0), axis=-1)
        back = back * factor
        pre = jnp.concatenate([low(back * up * slope), low(back * silu)], axis=1)
        act = low(act * factor)
        return (act, pre, gain * named)

    act_own, pre_own, gain_own = feed(ffn_own, grads_own, routed[0])
    act_other, pre_other, gain_other = feed(ffn_other, grads_other, routed[1])
    shape = (2, 2, zs * block, width)
    ffn_grad = scatter_all(
        low(dot_nt(pre_own, first)).reshape(shape), low(dot_nt(pre_other, first)).reshape(shape)
    )
    routed_sum = scatter_all(
        low(dot(act_own, second)).reshape(shape), low(dot(act_other, second)).reshape(shape)
    )
    output = both_halves(low(hidden_in + routed_sum))

    gains = jnp.stack([gain_own, gain_other]).reshape(2, 2, 2, zs, block)
    gains = by_own(by_own(by_own(gains, "c", 0), "x", 1), "y", 2)
    gains = jnp.roll(jnp.transpose(gains, (3, 1, 0, 2, 4)), z, axis=0)
    gains = trade(gains.reshape(2 * count, block), CTX + ("y",))
    share_grad = jnp.sum(gains.reshape(count, 2, block), axis=1).T
    logit_grad = shares * (share_grad - jnp.sum(shares * share_grad, axis=-1, keepdims=True))

    all_rows = jnp.concatenate([ffn_own.reshape(-1, width), ffn_other.reshape(-1, width)])
    all_grads = jnp.concatenate([grads_own.reshape(-1, width), grads_other.reshape(-1, width)])
    all_act = jnp.concatenate([act_own, act_other])
    all_pre = jnp.concatenate([pre_own, pre_other])
    grad_expert_down = dot_tn(all_act[:, :hidden_here], all_grads)[None]
    grad_expert_gate = dot_tn(all_rows, all_pre[:, :hidden_here])[None]
    grad_expert_up = dot_tn(all_rows, all_pre[:, padded : padded + hidden_here])[None]
    shared_pre = jnp.concatenate(
        [all_pre[:, hidden_here:used], all_pre[:, padded + hidden_here : padded + used]], axis=1
    )
    shared_back = jnp.concatenate(
        [
            low(dot_tn(shared_pre, all_rows)),
            low(dot_tn(all_act[:, hidden_here:used], all_grads)),
        ]
    )
    shared_back = trade(
        jnp.transpose(shared_back.reshape(-1, count, rows_here), (1, 0, 2)), CTX
    ).astype(jnp.float32)
    grad_shared_gate = shared_back[:, :shared_here].reshape(-1, rows_here).T
    grad_shared_up = shared_back[:, shared_here : 2 * shared_here].reshape(-1, rows_here).T
    grad_shared_down = shared_back[:, 2 * shared_here :].reshape(-1, rows_here)

    ffn_grad = ffn_grad + dot_nt(low(logit_grad), full_router)
    grad_router = dot_tn(ffn_low, low(logit_grad))
    hidden_part, grad_norm_ffn = root_norm_back(ffn_grad, unit_ffn, inverse_ffn, full_norm_ffn)
    grad_hidden = grad_mine.astype(jnp.float32) + hidden_part

    attention_grad = gather_slab(low(grad_hidden))
    grad_out_here = dot_tn(head_out, attention_grad)
    head_grad = low(dot_nt(attention_grad, out_here)).reshape(sequences, slab, heads, DV)
    grad_value_up = jnp.einsum(
        "shbr,sbhv->rhv", latent_out, head_grad, preferred_element_type=jnp.float32
    )
    latent_grad = low(
        jnp.einsum("sbhv,rhv->shbr", head_grad, value_up, preferred_element_type=jnp.float32)
    )
    prob_grad = jnp.einsum(
        "shqr,skr->shqk", latent_grad, keys[..., :R], preferred_element_type=jnp.float32
    )
    inner = jnp.sum(prob * prob_grad, axis=-1, keepdims=True)
    score_grad = low(prob * (prob_grad - inner))
    query_grad = low(
        jnp.einsum("shqk,skc->shqc", score_grad, keys, preferred_element_type=jnp.float32) * scale
    )
    key_grad = (
        jnp.einsum("shqk,shqc->skc", score_grad, query_rows, preferred_element_type=jnp.float32)
        * scale
    )
    value_grad = jnp.einsum(
        "shqk,shqr->skr", prob_low, latent_grad, preferred_element_type=jnp.float32
    )
    key_grad = low(key_grad + jnp.pad(value_grad, ((0, 0), (0, 0), (0, DR))))
    key_grad = jnp.transpose(
        key_grad.reshape(sequences, zs, 2, 2, block, R + DR), (2, 3, 0, 1, 4, 5)
    ).reshape(2, 2, 2, zs * block, R + DR)
    key_sum = scatter_all(key_grad[0], key_grad[1])

    absorbed_grad = query_grad[..., :R]
    rope_grad = jnp.transpose(query_grad[..., R:], (0, 2, 1, 3)).astype(jnp.float32)
    grad_key_up = jnp.einsum(
        "shbr,sbhn->rhn", absorbed_grad, query_low[..., :DN], preferred_element_type=jnp.float32
    )
    nope_grad = jnp.einsum(
        "shbr,rhn->sbhn", absorbed_grad, key_up, preferred_element_type=jnp.float32
    )
    rope_raw = rotate(rope_grad, cosine[:, None, :], -sine[:, None, :])
    query_raw_grad = low(jnp.concatenate([nope_grad, rope_raw], axis=-1)).reshape(
        sequences * slab, query_columns
    )
    grad_query_here = dot_tn(input_low, query_raw_grad)
    input_grad = scatter_slab(low(dot_nt(query_raw_grad, query_here)))

    latent_back, grad_latent_norm = root_norm_back(
        key_sum[:, :R], latent_unit[0, :block], latent_inverse[0, :block], full_latent_norm
    )
    rope_key = rotate(key_sum[:, R:], cosine[:block], -sine[:block])
    latent_raw_grad = low(jnp.concatenate([latent_back, rope_key], axis=-1))
    input_grad = input_grad + dot_nt(latent_raw_grad, full_down)
    source_part, grad_norm_in = root_norm_back(
        input_grad, unit_in[:block], inverse_in[:block], full_norm_in
    )
    tokens_gradient = both_halves(low(grad_hidden + source_part)).astype(jnp.float32)

    slab_latent_grad = gather_slab(latent_raw_grad)
    columns = lax.dynamic_index_in_dim(
        input_low.reshape(sequences * slab, zs, 4, rows_here), x * 2 + c, 2, keepdims=False
    ).reshape(sequences * slab, zs * rows_here)
    grad_down = sum_z(low(dot_tn(columns, slab_latent_grad)))

    grad_out_here = jnp.transpose(
        grad_out_here.reshape(heads, DV, count, rows_here), (2, 1, 0, 3)
    ).reshape(count * DV, heads * rows_here)
    grad_out = trade(low(sum_z(low(grad_out_here))), ("x", "c"))
    grad_output = jnp.transpose(
        grad_out.reshape(4, DV, heads, rows_here), (0, 2, 1, 3)
    ).reshape(-1, rows_here).astype(jnp.float32)
    grad_up_here = jnp.concatenate([grad_key_up, grad_value_up], axis=-1).reshape(
        count * DV, up_columns
    )
    both = jnp.concatenate([grad_query_here.reshape(width, query_columns), grad_up_here], axis=1)
    both = trade(low(sum_z(low(both))), ("x", "c")).astype(jnp.float32).reshape(4, rows_here, -1)
    grad_query = jnp.transpose(both[..., :query_columns], (1, 0, 2)).reshape(rows_here, -1)
    grad_latent_up = jnp.transpose(
        both[..., query_columns:].reshape(4, rank_rows, heads * (DN + DV)), (1, 0, 2)
    ).reshape(rank_rows, -1)

    small_grads = jnp.concatenate(
        [
            grad_router.T.reshape(experts, count, rows_here),
            grad_norm_in.reshape(1, count, rows_here),
            grad_norm_ffn.reshape(1, count, rows_here),
            jnp.pad(
                grad_latent_norm.reshape(1, count, rank_rows),
                ((0, 0), (0, 0), (0, rows_here - rank_rows)),
            ),
        ]
    )
    small_grads = trade(jnp.transpose(small_grads, (1, 0, 2)), CTX)
    small_grads = jnp.sum(small_grads, axis=0)
    small_grads = small_grads + swap(small_grads, "y")
    return (
        output,
        tokens_gradient,
        small_grads[experts],
        grad_query,
        grad_down,
        small_grads[experts + 2, :rank_rows],
        grad_latent_up,
        grad_output,
        small_grads[experts + 1],
        small_grads[:experts].T,
        grad_shared_gate,
        grad_shared_up,
        grad_shared_down,
        grad_expert_gate,
        grad_expert_up,
        grad_expert_down,
    )


IN_SPECS = (
    (None, "ctx", None),
    ("ctx",),
    ("ctx", "wa"),
    ("ctx", None),
    ("ctx",),
    ("ctx", "wa"),
    ("wa", "ctx"),
    ("ctx",),
    ("ctx", None),
    ("ctx", "wa"),
    ("ctx", "wa"),
    ("wa", "ctx"),
    ("ctx", None, "wa"),
    ("ctx", None, "wa"),
    ("ctx", "wa", None),
    (None, "ctx", None),
    (None, "ctx", None),
)
OUT_SPECS = ((None, "ctx", None),) * 2 + IN_SPECS[1:15]


def solution(mesh):
    count = mesh.shape["ctx"]

    def run(*arguments):
        experts = arguments[12].shape[0]
        if experts > 4 * TOPK or experts != count or mesh.shape["wa"] != 2 or count % 8:
            return jax.shard_map(
                shards,
                mesh=mesh,
                in_specs=tuple(P(*spec) for spec in IN_SPECS),
                out_specs=tuple(P(*spec) for spec in OUT_SPECS),
                check_vma=False,
            )(*arguments)
        grid = Mesh(mesh.devices.reshape(count // 4, 2, 2, 2), ("z", "x", "c", "y"))
        names = {"ctx": CTX, "wa": "y", None: None}
        return jax.shard_map(
            dense_shards,
            mesh=grid,
            in_specs=tuple(P(*[names[n] for n in spec]) for spec in IN_SPECS),
            out_specs=tuple(P(*[names[n] for n in spec]) for spec in OUT_SPECS),
            check_vma=False,
        )(*arguments)

    return run
```

```python
from functools import partial

import jax
import jax.numpy as jnp
from jax import lax
from jax.experimental import pallas as pl
from jax.experimental.layout import Layout, with_layout_constraint
from jax.experimental.pallas import tpu as pltpu
from jax.sharding import Mesh, PartitionSpec as P

DN = 128
DR = 64
DV = 128
R = 512
TOPK = 6


epsilon = 1e-06
highest = lax.Precision.HIGHEST


def shifted(value, axis, steps):
    count = lax.axis_size(axis)
    pairs = [(source, (source + steps) % count) for source in range(count)]
    return lax.ppermute(value, axis, pairs)


def root_norm(values, gain):
    inverse = lax.rsqrt(jnp.mean(values * values, axis=-1, keepdims=True) + epsilon)
    unit = values * inverse
    return (unit * gain, unit, inverse)


def root_norm_back(upstream, unit, inverse, gain):
    scaled = upstream * gain
    inner = jnp.mean(scaled * unit, axis=-1, keepdims=True)
    leading = tuple(range(upstream.ndim - 1))
    return (inverse * (scaled - unit * inner), jnp.sum(upstream * unit, axis=leading))


def rotary_tables(positions, width):
    half = width // 2
    frequency = 10000.0 ** (-jnp.arange(half, dtype=jnp.float32) * 2.0 / width)
    angle = positions.astype(jnp.float32)[:, None] * frequency[None, :]
    return (jnp.cos(angle), jnp.sin(angle))


def rotate(values, cosine, sine):
    half = values.shape[-1] // 2
    first = values[..., :half]
    second = values[..., half:]
    return jnp.concatenate(
        [first * cosine - second * sine, second * cosine + first * sine], axis=-1
    )


def silu_slope(values):
    sigmoid = jax.nn.sigmoid(values)
    return sigmoid * (1.0 + values * (1.0 - sigmoid))


def fetch_weights(
    norm_in,
    query_weight,
    latent_down,
    latent_norm,
    latent_up,
    output_weight,
    norm_ffn,
    router_weight,
    shared_gate,
    shared_up,
    shared_down,
):
    return (
        lax.all_gather(norm_in, "ctx", axis=0, tiled=True),
        lax.all_gather(query_weight, "ctx", axis=0, tiled=True),
        lax.all_gather(latent_down, "ctx", axis=0, tiled=True),
        lax.all_gather(latent_norm, "ctx", axis=0, tiled=True),
        lax.all_gather(latent_up, "ctx", axis=0, tiled=True),
        lax.all_gather(output_weight, "ctx", axis=1, tiled=True),
        lax.all_gather(norm_ffn, "ctx", axis=0, tiled=True),
        lax.all_gather(router_weight, "ctx", axis=0, tiled=True),
        lax.all_gather(shared_gate, "ctx", axis=0, tiled=True),
        lax.all_gather(shared_up, "ctx", axis=0, tiled=True),
        lax.all_gather(shared_down, "ctx", axis=1, tiled=True),
    )


def shards(
    tokens,
    norm_in,
    query_weight,
    latent_down,
    latent_norm,
    latent_up,
    output_weight,
    norm_ffn,
    router_weight,
    shared_gate,
    shared_up,
    shared_down,
    expert_gate,
    expert_up,
    expert_down,
    routes,
    cotangent,
):
    context_count = lax.axis_size("ctx")
    context_index = lax.axis_index("ctx")
    lead = (lax.axis_index("wa") == 0).astype(jnp.float32)
    sequences, block, width = tokens.shape
    local_experts = expert_gate.shape[0]
    experts = context_count * local_experts
    capacity = max(2, block * TOPK * 4 // (3 * experts))
    scale = (DN + DR) ** (-0.5)
    gathered = fetch_weights(
        norm_in,
        query_weight,
        latent_down,
        latent_norm,
        latent_up,
        output_weight,
        norm_ffn,
        router_weight,
        shared_gate,
        shared_up,
        shared_down,
    )
    (
        full_norm_in,
        full_query,
        full_down,
        full_latent_norm,
        full_up,
        full_output,
        full_norm_ffn,
        full_router,
        full_shared_gate,
        full_shared_up,
        full_shared_down,
    ) = gathered
    heads_here = full_up.shape[1] // (DN + DV)
    positions = context_index * block + jnp.arange(block)
    cosine, sine = rotary_tables(positions, DR)
    source = tokens.astype(jnp.float32)
    normed_in, unit_in, inverse_in = root_norm(source, full_norm_in.astype(jnp.float32))
    input_low = normed_in.astype(jnp.bfloat16)
    query_raw = jnp.dot(input_low, full_query, preferred_element_type=jnp.float32).reshape(
        sequences, block, heads_here, DN + DR
    )
    query_low = jnp.concatenate(
        [query_raw[..., :DN], rotate(query_raw[..., DN:], cosine[:, None, :], sine[:, None, :])],
        axis=-1,
    ).astype(jnp.bfloat16)
    up_view = full_up.reshape(R, heads_here, DN + DV)
    key_up = up_view[..., :DN]
    value_up = up_view[..., DN:]
    absorbed = jnp.einsum(
        "sbhn,rhn->shbr", query_low[..., :DN], key_up, preferred_element_type=jnp.float32
    )
    query_rows = jnp.concatenate(
        [absorbed.astype(jnp.bfloat16), jnp.transpose(query_low[..., DN:], (0, 2, 1, 3))], axis=-1
    )
    latent_raw = jnp.dot(input_low, full_down, preferred_element_type=jnp.float32)
    latent_scaled, latent_unit, latent_inverse = root_norm(
        latent_raw[..., :R], full_latent_norm.astype(jnp.float32)
    )
    key_rows = jnp.concatenate(
        [latent_scaled, rotate(latent_raw[..., R:], cosine, sine)], axis=-1
    ).astype(jnp.bfloat16)
    piece = lax.all_gather(key_rows, "ctx", axis=1, tiled=True)
    top = jnp.full((sequences, heads_here, block), -1e30, jnp.float32)
    scores = (
        jnp.einsum("shqc,skc->shqk", query_rows, piece, preferred_element_type=jnp.float32) * scale
    )
    key_positions = jnp.arange(piece.shape[1])
    allowed = positions[:, None] >= key_positions[None, :]
    scores = jnp.where(allowed, scores, -1e30)
    new_top = jnp.maximum(top, jnp.max(scores, axis=-1))
    weights = jnp.where(allowed, jnp.exp(scores - new_top[..., None]), 0.0)
    total = jnp.sum(weights, axis=-1)
    weights_high = weights.astype(jnp.bfloat16)
    weights_rest = (weights - weights_high.astype(jnp.float32)).astype(jnp.bfloat16)
    running = jnp.einsum(
        "shqk,skr->shqr", weights_high, piece[..., :R], preferred_element_type=jnp.float32
    )
    remainder = jnp.einsum(
        "shqk,skr->shqr", weights_rest, piece[..., :R], preferred_element_type=jnp.float32
    )
    top, total, running, remainder = (new_top, total, running, remainder)
    log_total = top + jnp.log(total)
    latent_out = (running / total[..., None]).astype(jnp.bfloat16)
    latent_exact = (running + remainder) / total[..., None]
    head_out = (
        jnp.einsum("shbr,rhv->sbhv", latent_out, value_up, preferred_element_type=jnp.float32)
        .astype(jnp.bfloat16)
        .reshape(sequences, block, heads_here * DV)
    )
    attention_part = jnp.dot(head_out, full_output, preferred_element_type=jnp.float32)
    hidden_in = source + lax.psum(attention_part, "wa")
    normed_ffn, unit_ffn, inverse_ffn = root_norm(hidden_in, full_norm_ffn.astype(jnp.float32))
    ffn_low = normed_ffn.astype(jnp.bfloat16)
    shares = jax.nn.softmax(
        jnp.dot(ffn_low, full_router, preferred_element_type=jnp.float32), axis=-1
    )
    shared_g = jnp.dot(ffn_low, full_shared_gate, preferred_element_type=jnp.float32)
    shared_u = jnp.dot(ffn_low, full_shared_up, preferred_element_type=jnp.float32)
    shared_silu = jax.nn.silu(shared_g)
    shared_activation = (shared_silu * shared_u).astype(jnp.bfloat16)
    shared_part = jnp.dot(shared_activation, full_shared_down, preferred_element_type=jnp.float32)
    expert_ids = jnp.arange(experts, dtype=jnp.int32)
    chosen = (
        (routes[..., None] == expert_ids)
        .astype(jnp.int32)
        .reshape(sequences, block * TOPK, experts)
    )
    earlier = jnp.cumsum(chosen, axis=1) - chosen
    slot_of = jnp.sum(earlier * chosen, axis=-1).reshape(sequences, block, TOPK)
    slot_ids = jnp.arange(capacity, dtype=jnp.int32)
    hit = (routes[None, :, :, :, None] == expert_ids[:, None, None, None, None]) & (
        slot_of[None, :, :, :, None] == slot_ids[None, None, None, None, :]
    )
    dispatch = jnp.transpose(jnp.any(hit, axis=3), (0, 1, 3, 2)).astype(jnp.float32)
    send = (
        jnp.einsum(
            "escb,sbd->escd",
            dispatch.astype(jnp.bfloat16),
            ffn_low,
            preferred_element_type=jnp.float32,
        )
        .astype(jnp.bfloat16)
        .reshape(experts, sequences * capacity, width)
    )
    slot_share = jnp.einsum("escb,sbe->esc", dispatch, shares, precision=highest)
    received = lax.all_to_all(send, "ctx", split_axis=0, concat_axis=0, tiled=True)
    count = received.shape[1]
    rows = received.reshape(context_count, local_experts, count, width)
    gate_pre = jnp.einsum("nesd,edf->nesf", rows, expert_gate, preferred_element_type=jnp.float32)
    up_pre = jnp.einsum("nesd,edf->nesf", rows, expert_up, preferred_element_type=jnp.float32)
    activation = (jax.nn.silu(gate_pre) * up_pre).astype(jnp.bfloat16)
    result = jnp.einsum(
        "nesf,efd->nesd", activation, expert_down, preferred_element_type=jnp.float32
    ).reshape(experts, count, width)
    returned = lax.all_to_all(result, "ctx", split_axis=0, concat_axis=0, tiled=True)
    hidden_units = gate_pre.shape[-1]
    returned, received, gate_keep, up_keep = (
        returned,
        received,
        gate_pre.reshape(experts, count, hidden_units),
        up_pre.reshape(experts, count, hidden_units),
    )
    returned = returned.reshape(experts, sequences, capacity, width)
    routed_part = jnp.einsum(
        "escb,escd->sbd", dispatch, returned * slot_share[..., None], precision=highest
    )
    output = hidden_in + lax.psum(shared_part + routed_part, "wa")
    gathered = fetch_weights(
        norm_in,
        query_weight,
        latent_down,
        latent_norm,
        latent_up,
        output_weight,
        norm_ffn,
        router_weight,
        shared_gate,
        shared_up,
        shared_down,
    )
    (
        full_norm_in,
        full_query,
        full_down,
        full_latent_norm,
        full_up,
        full_output,
        full_norm_ffn,
        full_router,
        full_shared_gate,
        full_shared_up,
        full_shared_down,
    ) = gathered
    up_view = full_up.reshape(R, heads_here, DN + DV)
    key_up = up_view[..., :DN]
    value_up = up_view[..., DN:]
    grad_y = cotangent.astype(jnp.float32)
    shared_grad = jnp.einsum(
        "sbd,fd->sbf", cotangent, full_shared_down, preferred_element_type=jnp.float32
    )
    shared_gate_grad = (shared_grad * shared_u * silu_slope(shared_g)).astype(jnp.bfloat16)
    shared_up_grad = (shared_grad * shared_silu).astype(jnp.bfloat16)
    grad_shared_down = jnp.einsum(
        "sbf,sbd->fd", shared_activation, cotangent, preferred_element_type=jnp.float32
    )
    grad_shared_gate = jnp.einsum(
        "sbd,sbf->df", ffn_low, shared_gate_grad, preferred_element_type=jnp.float32
    )
    grad_shared_up = jnp.einsum(
        "sbd,sbf->df", ffn_low, shared_up_grad, preferred_element_type=jnp.float32
    )
    ffn_grad = jnp.einsum(
        "sbf,df->sbd", shared_gate_grad, full_shared_gate, preferred_element_type=jnp.float32
    )
    ffn_grad = ffn_grad + jnp.einsum(
        "sbf,df->sbd", shared_up_grad, full_shared_up, preferred_element_type=jnp.float32
    )
    grad_at_slots = jnp.einsum("escb,sbd->escd", dispatch, grad_y, precision=highest)
    slot_grads = (
        (grad_at_slots * slot_share[..., None])
        .astype(jnp.bfloat16)
        .reshape(experts, sequences * capacity, width)
    )
    slot_dot = jnp.sum(returned * grad_at_slots, axis=-1)
    share_grad = jnp.einsum("escb,esc->sbe", dispatch, slot_dot, precision=highest)
    logit_grad = shares * (share_grad - jnp.sum(shares * share_grad, axis=-1, keepdims=True))
    grad_router = jnp.einsum(
        "sbd,sbe->de", ffn_low.astype(jnp.float32), logit_grad, precision=highest
    )
    ffn_grad = ffn_grad + jnp.einsum(
        "sbe,de->sbd", logit_grad, full_router.astype(jnp.float32), precision=highest
    )
    slot_back = lax.all_to_all(slot_grads, "ctx", split_axis=0, concat_axis=0, tiled=True).reshape(
        context_count, local_experts, -1, width
    )
    rows = received.reshape(context_count, local_experts, -1, width)
    gate_pre = gate_keep.reshape(context_count, local_experts, -1, gate_keep.shape[-1])
    up_pre = up_keep.reshape(context_count, local_experts, -1, up_keep.shape[-1])
    hidden_grad = jnp.einsum(
        "nesd,efd->nesf", slot_back, expert_down, preferred_element_type=jnp.float32
    )
    silu_gate = jax.nn.silu(gate_pre)
    gate_grad = (hidden_grad * up_pre * silu_slope(gate_pre)).astype(jnp.bfloat16)
    up_grad = (hidden_grad * silu_gate).astype(jnp.bfloat16)
    activation = (silu_gate * up_pre).astype(jnp.bfloat16)
    grad_expert_down = jnp.einsum(
        "nesf,nesd->efd", activation, slot_back, preferred_element_type=jnp.float32
    )
    grad_expert_gate = jnp.einsum(
        "nesd,nesf->edf", rows, gate_grad, preferred_element_type=jnp.float32
    )
    grad_expert_up = jnp.einsum("nesd,nesf->edf", rows, up_grad, preferred_element_type=jnp.float32)
    rows_grad = jnp.einsum(
        "nesf,edf->nesd", gate_grad, expert_gate, preferred_element_type=jnp.float32
    )
    rows_grad = rows_grad + jnp.einsum(
        "nesf,edf->nesd", up_grad, expert_up, preferred_element_type=jnp.float32
    )
    slot_grad = lax.all_to_all(
        rows_grad.reshape(experts, -1, width), "ctx", split_axis=0, concat_axis=0, tiled=True
    ).reshape(experts, sequences, capacity, width)
    ffn_grad = ffn_grad + jnp.einsum("escb,escd->sbd", dispatch, slot_grad, precision=highest)
    hidden_part, grad_norm_ffn = root_norm_back(
        ffn_grad, unit_ffn, inverse_ffn, full_norm_ffn.astype(jnp.float32)
    )
    grad_hidden = grad_y + lax.psum(hidden_part, "wa")
    attention_grad = grad_hidden.astype(jnp.bfloat16)
    grad_output = jnp.einsum(
        "sbk,sbd->kd", head_out, attention_grad, preferred_element_type=jnp.float32
    )
    head_grad = (
        jnp.einsum("sbd,kd->sbk", attention_grad, full_output, preferred_element_type=jnp.float32)
        .astype(jnp.bfloat16)
        .reshape(sequences, block, heads_here, DV)
    )
    grad_value_up = jnp.einsum(
        "shbr,sbhv->rhv", latent_out, head_grad, preferred_element_type=jnp.float32
    )
    latent_out_grad = jnp.einsum(
        "sbhv,rhv->shbr", head_grad, value_up, preferred_element_type=jnp.float32
    ).astype(jnp.bfloat16)
    row_dot = jnp.sum(latent_out_grad.astype(jnp.float32) * latent_exact, axis=-1)

    def turn_body(turn, carry):
        keys_here, key_grad, query_grad = carry
        source_index = (context_index + turn) % context_count
        key_positions = source_index * block + jnp.arange(block)
        allowed = positions[:, None] >= key_positions[None, :]
        scores = (
            jnp.einsum("shqc,skc->shqk", query_rows, keys_here, preferred_element_type=jnp.float32)
            * scale
        )
        weights = jnp.where(allowed[None, None], jnp.exp(scores - log_total[..., None]), 0.0)
        weight_grad = jnp.einsum(
            "shqr,skr->shqk",
            latent_out_grad,
            keys_here[..., :R],
            preferred_element_type=jnp.float32,
        )
        score_grad = (weights * (weight_grad - row_dot[..., None])).astype(jnp.bfloat16)
        query_grad = (
            query_grad
            + jnp.einsum(
                "shqk,skc->shqc", score_grad, keys_here, preferred_element_type=jnp.float32
            )
            * scale
        )
        key_part = (
            jnp.einsum("shqk,shqc->skc", score_grad, query_rows, preferred_element_type=jnp.float32)
            * scale
        )
        value_part = jnp.einsum(
            "shqk,shqr->skr",
            weights.astype(jnp.bfloat16),
            latent_out_grad,
            preferred_element_type=jnp.float32,
        )
        key_grad = key_grad + key_part + jnp.pad(value_part, ((0, 0), (0, 0), (0, DR)))
        keys_next = shifted(keys_here, "ctx", -1)
        grad_next = shifted(key_grad, "ctx", -1)
        return (keys_next, grad_next, query_grad)

    start_back = (
        key_rows,
        jnp.zeros((sequences, block, R + DR), jnp.float32),
        jnp.zeros((sequences, heads_here, block, R + DR), jnp.float32),
    )
    unused_keys, key_grad, query_grad = lax.fori_loop(0, context_count, turn_body, start_back)
    key_grad_total = lax.psum(key_grad, "wa")
    query_grad_low = query_grad.astype(jnp.bfloat16)
    absorbed_grad = query_grad_low[..., :R]
    rope_query_grad = jnp.transpose(query_grad_low[..., R:], (0, 2, 1, 3)).astype(jnp.float32)
    grad_key_up = jnp.einsum(
        "shbr,sbhn->rhn", absorbed_grad, query_low[..., :DN], preferred_element_type=jnp.float32
    )
    nope_grad = jnp.einsum(
        "shbr,rhn->sbhn", absorbed_grad, key_up, preferred_element_type=jnp.float32
    )
    rope_raw_grad = rotate(rope_query_grad, cosine[:, None, :], -sine[:, None, :])
    query_raw_grad = (
        jnp.concatenate([nope_grad, rope_raw_grad], axis=-1)
        .astype(jnp.bfloat16)
        .reshape(sequences, block, heads_here * (DN + DR))
    )
    grad_query = jnp.einsum(
        "sbd,sbk->dk", input_low, query_raw_grad, preferred_element_type=jnp.float32
    )
    input_part = jnp.einsum(
        "sbk,dk->sbd", query_raw_grad, full_query, preferred_element_type=jnp.float32
    )
    grad_latent_up = jnp.concatenate([grad_key_up, grad_value_up], axis=-1).reshape(
        R, heads_here * (DN + DV)
    )
    latent_grad, grad_latent_norm = root_norm_back(
        key_grad_total[..., :R], latent_unit, latent_inverse, full_latent_norm.astype(jnp.float32)
    )
    rope_key_grad = rotate(key_grad_total[..., R:], cosine, -sine)
    latent_raw_grad = jnp.concatenate([latent_grad, rope_key_grad], axis=-1).astype(jnp.bfloat16)
    grad_down = jnp.einsum(
        "sbd,sbc->dc", input_low, latent_raw_grad, preferred_element_type=jnp.float32
    )
    input_part = input_part + lead * jnp.einsum(
        "sbc,dc->sbd", latent_raw_grad, full_down, preferred_element_type=jnp.float32
    )
    source_part, grad_norm_in = root_norm_back(
        input_part, unit_in, inverse_in, full_norm_in.astype(jnp.float32)
    )
    summed = lax.psum((source_part, grad_norm_in, grad_norm_ffn, grad_router), "wa")
    tokens_gradient = grad_hidden + summed[0]
    reduced = (
        lax.psum_scatter(summed[1], "ctx", scatter_dimension=0, tiled=True),
        lax.psum_scatter(grad_query, "ctx", scatter_dimension=0, tiled=True),
        lax.psum_scatter(grad_down, "ctx", scatter_dimension=0, tiled=True),
        lax.psum_scatter(grad_latent_norm, "ctx", scatter_dimension=0, tiled=True),
        lax.psum_scatter(grad_latent_up, "ctx", scatter_dimension=0, tiled=True),
        lax.psum_scatter(grad_output, "ctx", scatter_dimension=1, tiled=True),
        lax.psum_scatter(summed[2], "ctx", scatter_dimension=0, tiled=True),
        lax.psum_scatter(summed[3], "ctx", scatter_dimension=0, tiled=True),
        lax.psum_scatter(grad_shared_gate, "ctx", scatter_dimension=0, tiled=True),
        lax.psum_scatter(grad_shared_up, "ctx", scatter_dimension=0, tiled=True),
        lax.psum_scatter(grad_shared_down, "ctx", scatter_dimension=1, tiled=True),
    )
    return (
        output.astype(jnp.bfloat16),
        tokens_gradient,
        reduced[0],
        reduced[1],
        reduced[2],
        reduced[3],
        reduced[4],
        reduced[5],
        reduced[6],
        reduced[7],
        reduced[8],
        reduced[9],
        reduced[10],
        grad_expert_gate,
        grad_expert_up,
        grad_expert_down,
    )


VMEM_LIMIT = 60 * 1024 * 1024
TILE = 256


def local_call(body, grid, in_specs, out_specs, out_shape, operands, after=()):
    inputs = len(in_specs)

    def run(*refs):
        body(*refs[:inputs], *refs[inputs + len(after) :])

    return pl.pallas_call(
        run,
        grid=grid,
        in_specs=list(in_specs) + [pl.BlockSpec(memory_space=pl.ANY)] * len(after),
        out_specs=out_specs,
        out_shape=out_shape,
        compiler_params=pltpu.CompilerParams(vmem_limit_bytes=VMEM_LIMIT),
        cost_estimate=pl.CostEstimate(flops=1, bytes_accessed=1, transcendentals=0),
    )(*operands, *after)


def whole(array):
    return pl.BlockSpec(array.shape, lambda *_: (0,) * array.ndim)


def by_rows(array, rows=TILE):
    return pl.BlockSpec((rows, array.shape[1]), lambda i: (i, 0))


def by_first(array):
    return pl.BlockSpec((1,) + array.shape[1:], lambda i: (i,) + (0,) * (array.ndim - 1))


def shaped(shape, dtype=jnp.bfloat16):
    return jax.ShapeDtypeStruct(shape, dtype)


def mul(left, right):
    return jnp.dot(left, right, preferred_element_type=jnp.float32)


def mul_nt(left, right):
    return lax.dot_general(
        left, right, (((1,), (1,)), ((), ())), preferred_element_type=jnp.float32
    )


def mul_tn(left, right):
    return lax.dot_general(
        left, right, (((0,), (0,)), ((), ())), preferred_element_type=jnp.float32
    )


def glu_back(gate, up, grads):
    sigmoid = 1.0 / (1.0 + jnp.exp(-gate))
    silu = gate * sigmoid
    slope = sigmoid * (1.0 + gate * (1.0 - sigmoid))
    return (silu * up, grads * up * slope, grads * silu)


def feed_body(
    experts, rows, back, shared_back, gate_t, up_t, small_t, named, pick,
    act_out, shared_act_out, gate_out, up_out, shared_out, gain_out,
):
    here = rows[...]
    part = small_t.shape[0] // 3
    small = mul_nt(here, small_t[...])
    logits = small[:, 2 * part :]
    ids = lax.broadcasted_iota(jnp.int32, logits.shape, 1)
    logits = jnp.where(ids < experts, logits, -1e30)
    chances = jnp.exp(logits - jnp.max(logits, axis=1, keepdims=True))
    total = jnp.sum(chances, axis=1, keepdims=True)
    named_here = named[...]
    share = jnp.sum(chances * pick[...], axis=1, keepdims=True) / total * named_here
    act, gate_grad, up_grad = glu_back(
        small[:, :part], small[:, part : 2 * part], shared_back[...].astype(jnp.float32)
    )
    shared_act_out[...] = act.astype(jnp.bfloat16)
    shared_out[:, :part] = gate_grad.astype(jnp.bfloat16)
    shared_out[:, part:] = up_grad.astype(jnp.bfloat16)
    grads = back[...].astype(jnp.float32)
    act, gate_grad, up_grad = glu_back(mul_nt(here, gate_t[...]), mul_nt(here, up_t[...]), grads)
    gain_out[...] = jnp.sum(act * grads, axis=1, keepdims=True) * named_here
    act_out[...] = (act * share).astype(jnp.bfloat16)
    gate_out[...] = (gate_grad * share).astype(jnp.bfloat16)
    up_out[...] = (up_grad * share).astype(jnp.bfloat16)


def feed_kernel(rows, back, shared_back, gate_t, up_t, small_t, named, pick, experts):
    count = rows.shape[0]
    hidden, part = (back.shape[1], shared_back.shape[1])
    shapes = [shaped((count, s)) for s in (hidden, part, hidden, hidden, 2 * part)]
    shapes.append(shaped((count, 1), jnp.float32))
    return local_call(
        partial(feed_body, experts),
        (count // TILE,),
        [
            by_rows(rows),
            by_rows(back),
            by_rows(shared_back),
            whole(gate_t),
            whole(up_t),
            whole(small_t),
            by_rows(named),
            whole(pick),
        ],
        [by_rows(s) for s in shapes],
        shapes,
        (rows, back, shared_back, gate_t, up_t, small_t, named, pick),
    )


def input_body(gate, up, shared, gate_t, up_t, small_t, gain, pick, out):
    width = gate_t.shape[1]
    used = shared.shape[1]
    out[:, :width] = (
        mul(gate[...], gate_t[...]) + mul(up[...], up_t[...]) + mul(shared[...], small_t[:used, :])
    ).astype(jnp.bfloat16)
    out[:, width:] = (gain[...] * pick[...]).astype(jnp.bfloat16)


def input_kernel(gate, up, shared, gate_t, up_t, small_t, gain, pick, after=()):
    count = gate.shape[0]
    shape = shaped((count, gate_t.shape[1] + pick.shape[1]))
    return local_call(
        input_body,
        (count // TILE,),
        [by_rows(gate), by_rows(up), by_rows(shared)]
        + [whole(gate_t), whole(up_t), whole(small_t), by_rows(gain), whole(pick)],
        by_rows(shape),
        shape,
        (gate, up, shared, gate_t, up_t, small_t, gain, pick),
        after,
    )


def result_body(act, shared_act, down, shared_down, out):
    out[...] = (mul(act[...], down[...]) + mul(shared_act[...], shared_down[...])).astype(
        jnp.bfloat16
    )


def result_kernel(act, shared_act, down, shared_down, after=()):
    count = act.shape[0]
    shape = shaped((count, down.shape[1]))
    return local_call(
        result_body,
        (count // TILE,),
        [by_rows(act), by_rows(shared_act), whole(down), whole(shared_down)],
        by_rows(shape),
        shape,
        (act, shared_act, down, shared_down),
        after,
    )


def weight_body(left_own, left_other, more_own, more_other, own, other, out, more_out):
    here, there = (own[...], other[...])
    out[...] = mul_tn(left_own[...], here) + mul_tn(left_other[...], there)
    more_out[...] = (mul_tn(more_own[...], here) + mul_tn(more_other[...], there)).astype(
        jnp.bfloat16
    )


def weight_kernel(lefts, mores, rights, side=0, part=128, after=()):
    count, width = rights[0].shape
    columns = lambda rows: pl.BlockSpec((rows, TILE), lambda i: (0, i))
    hidden, more = (lefts[0].shape[1], part)
    return local_call(
        weight_body,
        (width // TILE,),
        [whole(a) for a in lefts]
        + [pl.BlockSpec((count, part), lambda i: (0, side))] * 2
        + [columns(count)] * 2,
        [columns(hidden), columns(more)],
        [shaped((hidden, width), jnp.float32), shaped((more, width))],
        (*lefts, *mores, *rights),
        after,
    )


def head_parts_of(query, heads, nope):
    rope = query.shape[1] // heads - nope
    return [
        (
            query[:, k * nope : (k + 1) * nope],
            query[:, heads * nope + k * rope : heads * nope + (k + 1) * rope],
        )
        for k in range(heads)
    ]


def attend_body(
    heads, scale, query, own, other, up, out_weight, spots, key_spots,
    part_out, prob_out, absorbed_out, latent_out, head_out,
):
    rank = up.shape[0]
    absorbed, ropes = ([], [])
    for k, (nope, rope) in enumerate(head_parts_of(query[...], heads, DN)):
        key_up = up[:, k * (DN + DV) : k * (DN + DV) + DN]
        absorbed.append(mul_nt(nope, key_up).astype(jnp.bfloat16))
        ropes.append(rope)
    absorbed = jnp.concatenate(absorbed, axis=0)
    rope = jnp.concatenate(ropes, axis=0)
    absorbed_out[0] = absorbed
    keys = [source[0, k] for source in (own, other) for k in range(2)]
    scores = jnp.concatenate(
        [mul_nt(absorbed, key[:, :rank]) + mul_nt(rope, key[:, rank:]) for key in keys], axis=1
    )
    allowed = spots[...] >= key_spots[...]
    allowed = jnp.concatenate([allowed] * heads, axis=0)
    scores = jnp.where(allowed, scores * scale, -1e30)
    weights = jnp.exp(scores - jnp.max(scores, axis=1, keepdims=True))
    prob = (weights / jnp.sum(weights, axis=1, keepdims=True)).astype(jnp.bfloat16)
    prob_out[0] = prob
    size = keys[0].shape[0]
    latent = sum(
        mul(prob[:, j * size : (j + 1) * size], key[:, :rank]) for j, key in enumerate(keys)
    ).astype(jnp.bfloat16)
    latent_out[0] = latent
    rows = query.shape[0]
    head = jnp.concatenate(
        [
            mul(
                latent[k * rows : (k + 1) * rows],
                up[:, k * (DN + DV) + DN : (k + 1) * (DN + DV)],
            )
            for k in range(heads)
        ],
        axis=1,
    ).astype(jnp.bfloat16)
    head_out[...] = head
    part_out[...] = mul(head, out_weight[...]).astype(jnp.bfloat16)


def attend_kernel(query, own, other, up, out_weight, spots, key_spots, heads, scale, after=()):
    sequences = own.shape[0]
    rows = query.shape[0] // sequences
    key_count = 4 * own.shape[2]
    rank = up.shape[0]
    shapes = [
        shaped((query.shape[0], out_weight.shape[1])),
        shaped((sequences, heads * rows, key_count)),
        shaped((sequences, heads * rows, rank)),
        shaped((sequences, heads * rows, rank)),
        shaped((query.shape[0], heads * DV)),
    ]
    return local_call(
        partial(attend_body, heads, scale),
        (sequences,),
        [by_rows(query, rows), by_first(own), by_first(other)]
        + [whole(a) for a in (up, out_weight, spots, key_spots)],
        [
            by_rows(shapes[0], rows),
            by_first(shapes[1]),
            by_first(shapes[2]),
            by_first(shapes[3]),
            by_rows(shapes[4], rows),
        ],
        shapes,
        (query, own, other, up, out_weight, spots, key_spots),
        after,
    )


def attend_back_body(
    heads, scale, grads, query, own, other, up, out_weight, prob, absorbed, latent,
    own_out, other_out, query_out, up_out,
):
    rank = up.shape[0]
    rows = query.shape[0]
    first = pl.program_id(0) == 0
    grads_here = grads[...]
    head_grad = mul_nt(grads_here, out_weight[...]).astype(jnp.bfloat16)
    span = lambda k: slice(k * rows, (k + 1) * rows)
    latent_grad = []
    value_parts = []
    for k in range(heads):
        mine = head_grad[:, k * DV : (k + 1) * DV]
        value_up = up[:, k * (DN + DV) + DN : (k + 1) * (DN + DV)]
        latent_grad.append(mul_nt(mine, value_up).astype(jnp.bfloat16))
        value_parts.append(mul_tn(latent[0, span(k)], mine))
    latent_grad = jnp.concatenate(latent_grad, axis=0)
    keys = [source[0, k] for source in (own, other) for k in range(2)]
    size = keys[0].shape[0]
    prob_here = prob[0]
    prob_wide = prob_here.astype(jnp.float32)
    prob_grad = jnp.concatenate([mul_nt(latent_grad, key[:, :rank]) for key in keys], axis=1)
    inner = jnp.sum(prob_wide * prob_grad, axis=1, keepdims=True)
    score_grad = (prob_wide * (prob_grad - inner)).astype(jnp.bfloat16)
    absorbed_here = absorbed[0]
    parts = head_parts_of(query[...], heads, DN)
    rope = jnp.concatenate([part[1] for part in parts], axis=0)
    wide = 0.0
    narrow = 0.0
    for j, key in enumerate(keys):
        piece = score_grad[:, j * size : (j + 1) * size]
        wide = wide + mul(piece, key[:, :rank])
        narrow = narrow + mul(piece, key[:, rank:])
        target = (own_out, other_out)[j // 2]
        value = mul_tn(prob_here[:, j * size : (j + 1) * size], latent_grad)
        target[0, j % 2, :, :rank] = (mul_tn(piece, absorbed_here) * scale + value).astype(
            jnp.bfloat16
        )
        target[0, j % 2, :, rank:] = (mul_tn(piece, rope) * scale).astype(jnp.bfloat16)
    wide = (wide * scale).astype(jnp.bfloat16)
    narrow = narrow * scale
    for k in range(heads):
        start = k * (DN + DV)
        key_part = mul_tn(wide[span(k)], parts[k][0])
        up_out[:, start : start + DN] = (
            jnp.where(first, 0.0, up_out[:, start : start + DN]) + key_part
        )
        up_out[:, start + DN : start + DN + DV] = (
            jnp.where(first, 0.0, up_out[:, start + DN : start + DN + DV]) + value_parts[k]
        )
        query_out[:, k * DN : (k + 1) * DN] = mul(wide[span(k)], up[:, start : start + DN])
        rope_size = narrow.shape[1]
        at = heads * DN + k * rope_size
        query_out[:, at : at + rope_size] = narrow[span(k)]


def attend_back_kernel(
    grads, query, own, other, up, out_weight, prob, absorbed, latent, heads, scale, after=()
):
    sequences = own.shape[0]
    rows = query.shape[0] // sequences
    shapes = [
        shaped(own.shape),
        shaped(own.shape),
        shaped(query.shape, jnp.float32),
        shaped(up.shape, jnp.float32),
    ]
    return local_call(
        partial(attend_back_body, heads, scale),
        (sequences,),
        [by_rows(grads, rows), by_rows(query, rows), by_first(own), by_first(other)]
        + [whole(up), whole(out_weight), by_first(prob), by_first(absorbed), by_first(latent)],
        [by_first(own), by_first(own), by_rows(query, rows), whole(up)],
        shapes,
        (grads, query, own, other, up, out_weight, prob, absorbed, latent),
        after,
    )


def heads_body(z, own, *refs):
    query_out, up_out, out_out = refs[-3:]
    count = (len(refs) - 3) // 2 + 1
    above, below = (refs[: count - 1], refs[count - 1 : 2 * count - 2])
    groups, rows, _ = own.shape
    query_columns = query_out.shape[1]
    up_blocks = up_out.shape[1] // 128
    up_rows = rows // up_blocks
    heads = out_out.shape[0] // rows
    for s in range(count):
        part = own[...] if s == 0 else above[s - 1][...] + below[count - s - 1][...]
        place = lax.rem(z[0] + s, count)
        for j in range(groups):
            block = place * groups + j
            start = pl.multiple_of(block * rows, rows)
            query_out[pl.ds(start, rows), :] = part[j, :, :query_columns]
            for k in range(up_blocks):
                up_out[
                    pl.ds(pl.multiple_of(block * up_rows, up_rows), up_rows),
                    k * 128 : (k + 1) * 128,
                ] = part[j, k * up_rows : (k + 1) * up_rows, query_columns : query_columns + 128]
            for k in range(heads):
                at = query_columns + 128 + k * rows
                out_out[k * rows : (k + 1) * rows, pl.ds(start, rows)] = part[j, :, at : at + rows]


def heads_kernel(z, own, above, below, query_columns, heads, up_columns):
    count = len(above) + 1
    groups, rows, _ = own.shape
    width = count * groups * rows
    up_rows = rows * 128 // up_columns
    shapes = [
        shaped((width, query_columns)),
        shaped((count * groups * up_rows, up_columns)),
        shaped((heads * rows, width)),
    ]
    return local_call(
        heads_body,
        (1,),
        [pl.BlockSpec(memory_space=pltpu.SMEM)] + [whole(own)] * (2 * count - 1),
        [whole(s) for s in shapes],
        shapes,
        (z, own, *above, *below),
    )


def out_grads_body(rows, head, grads, out):
    heads = head.shape[1] // rows
    total = mul_tn(head[...], grads[...]).astype(jnp.bfloat16)
    for i in range(out.shape[0]):
        for k in range(heads):
            out[i, :, k * rows : (k + 1) * rows] = total[
                k * rows : (k + 1) * rows, i * rows : (i + 1) * rows
            ]


def out_grads_kernel(head, grads, rows):
    shape = shaped((grads.shape[1] // rows, rows, head.shape[1]))
    return local_call(
        partial(out_grads_body, rows),
        (1,),
        [whole(head), whole(grads)],
        whole(shape),
        shape,
        (head, grads),
    )


def query_grads_body(rows, grads, source, up, out):
    columns = grads.shape[1]
    up_blocks = up.shape[1] // 128
    up_rows = rows // up_blocks
    here = grads[...]
    for i in range(out.shape[0]):
        out[i, :, :columns] = mul_tn(source[:, i * rows : (i + 1) * rows], here).astype(
            jnp.bfloat16
        )
        for k in range(up_blocks):
            out[i, k * up_rows : (k + 1) * up_rows, columns:] = up[
                i * up_rows : (i + 1) * up_rows, k * 128 : (k + 1) * 128
            ].astype(jnp.bfloat16)


def query_grads_kernel(grads, source, up, rows, after=()):
    shape = shaped((source.shape[1] // rows, rows, grads.shape[1] + 128))
    return local_call(
        partial(query_grads_body, rows),
        (1,),
        [whole(grads), whole(source), whole(up)],
        whole(shape),
        shape,
        (grads, source, up),
        after,
    )


def product_nt_body(left, right, out):
    out[...] = mul_nt(left[...], right[...]).astype(jnp.bfloat16)


def product_nt_kernel(left, right, after=()):
    shape = shaped((left.shape[0], right.shape[0]))
    return local_call(
        product_nt_body,
        (left.shape[0] // TILE,),
        [by_rows(left), whole(right)],
        by_rows(shape),
        shape,
        (left, right),
        after,
    )


CTX = ("z", "x", "c")


def swap(value, axis):
    return lax.ppermute(value, axis, [(0, 1), (1, 0)])


def from_z(value, steps):
    count = lax.axis_size("z")
    return lax.ppermute(value, "z", [((i + steps) % count, i) for i in range(count)])


def to_z(value, steps):
    count = lax.axis_size("z")
    return lax.ppermute(value, "z", [(i, (i + steps) % count) for i in range(count)])


def trade(value, axes):
    return lax.all_to_all(value, axes, split_axis=0, concat_axis=0, tiled=True)


def add(left, right):
    return left.astype(jnp.float32) + right.astype(jnp.float32)


def low(value):
    return value.astype(jnp.bfloat16)


def dot(left, right):
    return jnp.dot(left, right, preferred_element_type=jnp.float32)


def dot_nt(left, right):
    return lax.dot_general(
        left, right, (((1,), (1,)), ((), ())), preferred_element_type=jnp.float32
    )


def dot_tn(left, right):
    return lax.dot_general(
        left, right, (((0,), (0,)), ((), ())), preferred_element_type=jnp.float32
    )


def by_own(value, axis_name, dim):
    flipped = jnp.flip(value, axis=dim)
    return jnp.where(lax.axis_index(axis_name) == 0, value, flipped)


def tie(value, *others):
    if not others:
        return value
    zero = sum(other[(0,) * other.ndim].astype(jnp.float32) for other in others) * 0.0
    return value + zero.astype(value.dtype)


def rows_first(value):
    return with_layout_constraint(value, Layout(major_to_minor=tuple(range(value.ndim))))


def put(parts, places):
    whole = jnp.zeros((len(parts),) + parts[0].shape, parts[0].dtype)
    for part, place in zip(parts, places):
        whole = lax.dynamic_update_index_in_dim(whole, part, place, 0)
    return rows_first(whole)


def z_parts(value):
    return [value] + [from_z(value, s) for s in range(1, lax.axis_size("z"))]


def chain_z(value):
    count = lax.axis_size("z")
    above, below = ([value], [value])
    for r in range(1, count):
        down = [(i + 1, i) for i in range(count - r)]
        up = [(i, i + 1) for i in range(r - 1, count - 1)]
        above.append(lax.ppermute(above[-1], "z", down))
        below.append(lax.ppermute(below[-1], "z", up))
    return (above[1:], below[1:])


def put_z(parts):
    z = lax.axis_index("z")
    count = len(parts)
    return put(parts, [(z + s) % count for s in range(count)])


def gather_plane(rows, axes=("x", "y"), gates=()):
    half = rows.shape[0] // 2
    over_a = tie(swap(rows, axes[0]), *gates)
    over_b = tie(swap(rows, axes[1]), *gates)
    both = jnp.concatenate([swap(over_b[:half], axes[0]), swap(over_a[half:], axes[1])], axis=0)
    return jnp.stack([jnp.stack([rows, over_b]), jnp.stack([over_a, both])])


def plane_first(rows, axes=("x", "y"), gates=()):
    half = rows.shape[2] // 2
    lower, upper = (rows[:, :, :half], rows[:, :, half:])
    lower = low(add(lower[0], tie(swap(lower[1], axes[0]), *gates)))
    upper = low(add(upper[:, 0], tie(swap(upper[:, 1], axes[1]), *gates)))
    return (lower, upper)


def plane_second(lower, upper, axes=("x", "y"), gates=()):
    lower = add(lower[0], tie(swap(lower[1], axes[1]), *gates))
    upper = add(upper[0], tie(swap(upper[1], axes[0]), *gates))
    return jnp.concatenate([lower, upper], axis=0)


def scatter_plane(rows, axes=("x", "y")):
    return plane_second(*plane_first(rows, axes), axes)


def spread_z(rows):
    return jnp.concatenate(z_parts(rows), axis=0)


def fold_z(slabs, gates=()):
    count = lax.axis_size("z")
    block = slabs.shape[0] // count
    sent = low(slabs)
    total = slabs[:block]
    for s in range(1, count):
        part = tie(to_z(sent[s * block : (s + 1) * block], s), *gates)
        total = total + part.astype(jnp.float32)
    return total


def sum_z(value, gates=()):
    count = lax.axis_size("z")
    z = lax.axis_index("z")
    parts = [
        lax.dynamic_index_in_dim(value, (z + s) % count, 0, keepdims=False) for s in range(count)
    ]
    total = parts[0].astype(jnp.float32)
    for s in range(1, count):
        total = total + tie(to_z(parts[s], s), *gates).astype(jnp.float32)
    return total


def both_halves(rows):
    other = swap(rows, "y")
    return by_own(jnp.stack([rows, other]), "y", 0)


def dense_shards(
    tokens,
    norm_in,
    query_weight,
    latent_down,
    latent_norm,
    latent_up,
    output_weight,
    norm_ffn,
    router_weight,
    shared_gate,
    shared_up,
    shared_down,
    expert_gate,
    expert_up,
    expert_down,
    routes,
    cotangent,
):
    zs = lax.axis_size("z")
    z, x, c = (lax.axis_index("z"), lax.axis_index("x"), lax.axis_index("c"))
    me = (z * 2 + x) * 2 + c
    sequences, block, width = tokens.shape
    count = 4 * zs
    rows_here = width // count
    slab = 4 * block
    experts = router_weight.shape[1]
    shared_here = shared_gate.shape[1] // count
    part = -(-max(shared_here, experts) // 128) * 128
    heads = latent_up.shape[1] // (4 * (DN + DV))
    query_columns = heads * (DN + DR)
    rank_rows = R // count
    head_rows = heads * DV
    scale = (DN + DR) ** (-0.5)

    latent_column = jnp.pad(latent_norm, (0, rows_here - rank_rows))[:, None]
    small = jnp.concatenate(
        [
            latent_down,
            router_weight,
            norm_in[:, None],
            norm_ffn[:, None],
            latent_column,
            routes.reshape(sequences * block, TOPK).astype(jnp.bfloat16),
        ],
        axis=1,
    )
    small = put_z(z_parts(jnp.pad(small, ((0, 0), (0, -small.shape[1] % 128)))))
    at = R + DR
    down_here = small[:, :, :at]
    rest = small[:, :, at:]
    down_here = down_here.reshape(-1, R + DR)
    down_x = swap(down_here, "x")
    down_pieces = (down_here, down_x, swap(down_here, "c"), swap(down_x, "c"))
    own_gain = rest[:, :, experts].reshape(1, zs * rows_here).astype(jnp.float32)
    rest = jnp.stack([rest, swap(rest, "x")], axis=1)
    rest = jnp.stack([rest, swap(rest, "c")], axis=2)
    rest = by_own(by_own(rest, "x", 1), "c", 2).reshape(count, rows_here, -1)
    full_router = rest[:, :, :experts].reshape(width, experts)
    full_norm_in = rest[:, :, experts].reshape(width).astype(jnp.float32)
    full_norm_ffn = rest[:, :, experts + 1].reshape(width).astype(jnp.float32)
    full_latent_norm = rest[:, :rank_rows, experts + 2].reshape(R).astype(jnp.float32)
    all_routes = rest[:, :, experts + 3 : experts + 3 + TOPK]

    up_columns = heads * (DN + DV)
    up_part = jnp.transpose(
        latent_up.reshape(rank_rows, 4, up_columns // 128, 128), (1, 2, 0, 3)
    ).reshape(4, rows_here, 128)
    out_part = jnp.transpose(output_weight.reshape(4, heads, DV, rows_here), (0, 2, 1, 3)).reshape(
        4, DV, heads * rows_here
    )
    by_heads = query_weight.reshape(rows_here, 4, heads, DN + DR)
    by_heads = jnp.concatenate(
        [
            by_heads[..., :DN].reshape(rows_here, 4, heads * DN),
            by_heads[..., DN:].reshape(rows_here, 4, heads * DR),
        ],
        axis=2,
    )
    by_heads = jnp.transpose(by_heads, (1, 0, 2))
    by_heads = trade(jnp.concatenate([by_heads, up_part, out_part], axis=2), ("x", "c"))
    mine = by_own(tokens, "y", 0)
    line = jnp.stack([mine, swap(mine, "x")], axis=1)
    line = jnp.stack([line, swap(line, "c")], axis=1)
    source = line.reshape(sequences * slab, width).astype(jnp.float32)
    grad_mine = by_own(cotangent, "y", 0)[0]
    grad_parts = z_parts(tie(grad_mine, small))
    grads_own = gather_plane(jnp.concatenate(grad_parts))
    grads_other = swap(grads_own, "c").reshape(-1, width)
    grads_own = grads_own.reshape(-1, width)
    gate_t, up_t, down = (expert_gate[0].T, expert_up[0].T, expert_down[0])
    back_own = product_nt_kernel(grads_own, down)
    back_other = product_nt_kernel(grads_other, down)
    by_heads = tie(by_heads, grad_parts[-1])
    above, below = chain_z(by_heads)
    query_here, up_here, out_here = heads_kernel(
        z[None], by_heads, above, below, query_columns, heads, up_columns
    )

    def places(turns):
        two = jnp.arange(2)
        base = (
            ((z + turns[None, None, :]) % zs) * 4
            + (x ^ two[None, :, None]) * 2
            + (c ^ two[:, None, None])
        )
        return (base[..., None] * block + jnp.arange(block)).reshape(-1)

    positions = places(jnp.arange(1))
    key_positions = places(jnp.arange(zs))
    cosine, sine = rotary_tables(positions, DR)
    normed, unit_in, inverse_in = root_norm(source, full_norm_in)
    input_low = low(normed)

    own_rows = line[0].reshape(slab, width)
    own_columns = jnp.concatenate(
        [
            lax.dynamic_slice_in_dim(own_rows, (4 * k + 2 * x + c) * rows_here, rows_here, 1)
            for k in range(zs)
        ],
        axis=1,
    ).astype(jnp.float32)
    latent_part = dot(
        low(own_columns * inverse_in[:slab] * own_gain), down_here
    )
    latent_part = low(latent_part).reshape(2, 2, block, R + DR)
    latent_part = low(add(latent_part[0], swap(latent_part[1], "c")))
    latent_raw = add(latent_part[0], swap(latent_part[1], "x"))
    latent_scaled, latent_unit, latent_inverse = root_norm(latent_raw[:, :R], full_latent_norm)
    key_own = low(
        jnp.concatenate(
            [latent_scaled, rotate(latent_raw[:, R:], cosine[:block], sine[:block])], axis=-1
        )
    )
    plane = gather_plane(spread_z(key_own), ("y", "x"))
    keys_own, keys_other = (plane, swap(plane, "c"))
    query = dot(input_low, query_here)
    rope = query[:, heads * DN :].reshape(sequences, slab, heads, DR)
    rope = rotate(rope, cosine[:, None, :], sine[:, None, :]).reshape(sequences * slab, -1)
    query_low = low(jnp.concatenate([query[:, : heads * DN], rope], axis=1))

    shared_mine = jnp.concatenate(
        [
            shared_gate.T.reshape(count, shared_here, rows_here),
            shared_up.T.reshape(count, shared_here, rows_here),
            shared_down.reshape(count, shared_here, rows_here),
        ],
        axis=1,
    )
    shared_rows = trade(tie(shared_mine, query_low), CTX)
    shared_rows = jnp.transpose(shared_rows, (1, 0, 2)).reshape(3, shared_here, width)
    shared_rows = jnp.pad(shared_rows, ((0, 0), (0, part - shared_here), (0, 0)))
    small_t = jnp.concatenate(
        [
            shared_rows[0],
            shared_rows[1],
            jnp.pad(full_router.T, ((0, part - experts), (0, 0))),
        ]
    )
    shared_down_t = shared_rows[2]

    def scatter_slab(partial):
        parts = partial.reshape(2, 2, 2, block, -1)
        kept = low(add(parts[:, 0], swap(parts[:, 1], "c")))
        return scatter_plane(kept, ("y", "x"))

    def gather_slab(rows, gates=()):
        plane = gather_plane(rows, ("y", "x"), gates)
        return jnp.stack([plane, swap(plane, "c")], axis=1).reshape(sequences * slab, -1)

    attention, prob, absorbed, latent_out, head_out = attend_kernel(
        query_low,
        keys_own,
        keys_other,
        up_here,
        out_here,
        positions[:, None],
        key_positions[None, :],
        heads,
        scale,
        (back_own, back_other) + down_pieces[1:],
    )
    attention = scatter_slab(attention)
    hidden_in = mine[0].astype(jnp.float32) + attention
    normed_ffn, unit_ffn, inverse_ffn = root_norm(hidden_in, full_norm_ffn)
    ffn_low = low(normed_ffn)
    shares = jax.nn.softmax(dot(ffn_low, full_router), axis=-1)
    ffn_slabs = spread_z(ffn_low)
    ffn_own = gather_plane(ffn_slabs, gates=(small_t,))
    ffn_other = swap(ffn_own, "c").reshape(-1, width)
    ffn_own = ffn_own.reshape(-1, width)

    relative = all_routes.reshape(zs, 2, 2, sequences, block, TOPK)
    relative = by_own(by_own(by_own(relative, "x", 1), "c", 2), "y", 3)
    relative = jnp.roll(relative, -z, axis=0)
    routed = jnp.any(relative == me.astype(jnp.bfloat16), axis=-1)
    routed = jnp.transpose(routed, (2, 1, 3, 0, 4)).reshape(2, -1, 1).astype(jnp.float32)
    pick = (jnp.arange(part)[None, :] == me).astype(jnp.float32)

    def feed(rows, grads, back, named):
        shared_back = product_nt_kernel(grads, shared_down_t)
        return feed_kernel(rows, back, shared_back, gate_t, up_t, small_t, named, pick, experts)

    act_own, more_own, gate_own, up_own, pre_own, gain_own = feed(
        ffn_own, grads_own, back_own, routed[0]
    )
    act_other, more_other, gate_other, up_other, pre_other, gain_other = feed(
        ffn_other, grads_other, back_other, routed[1]
    )
    shape = (2, 2, zs * block, -1)
    grad_other = input_kernel(
        gate_other, up_other, pre_other, gate_t, up_t, small_t, gain_other, pick
    )
    grad_own = input_kernel(
        gate_own, up_own, pre_own, gate_t, up_t, small_t, gain_own, pick, (grad_other,)
    )
    grad_own = low(add(grad_own, swap(grad_other, "c"))).reshape(shape)
    sum_other = result_kernel(act_other, more_other, down, shared_down_t, (grad_own,))
    sum_own = result_kernel(act_own, more_own, down, shared_down_t, (sum_other,))
    lower, upper = plane_first(grad_own, gates=(sum_own,))
    routed_own = low(add(tie(sum_own, lower), swap(sum_other, "c"))).reshape(shape)
    grad_slab = plane_second(lower, upper, gates=(routed_own,))
    grad_expert_down, shared_down_back = weight_kernel(
        (act_own, act_other), (more_own, more_other), (grads_own, grads_other), 0, part, (grad_slab,)
    )
    ffn_grad = fold_z(grad_slab, (grad_expert_down,))
    share_grad = ffn_grad[:, width : width + experts]
    ffn_grad = ffn_grad[:, :width]
    logit_grad = shares * (share_grad - jnp.sum(shares * share_grad, axis=-1, keepdims=True))
    ffn_grad = ffn_grad + dot_nt(low(logit_grad), full_router)
    grad_router = dot_tn(ffn_low, low(logit_grad))
    hidden_part, grad_norm_ffn = root_norm_back(ffn_grad, unit_ffn, inverse_ffn, full_norm_ffn)
    grad_hidden = grad_mine.astype(jnp.float32) + hidden_part

    hidden_low = low(grad_hidden)
    grad_expert_gate, shared_gate_back = weight_kernel(
        (gate_own, gate_other), (pre_own, pre_other), (ffn_own, ffn_other), 0, part, (hidden_low,)
    )
    grad_expert_up, shared_up_back = weight_kernel(
        (up_own, up_other),
        (pre_own, pre_other),
        (ffn_own, ffn_other),
        1,
        part,
        (grad_expert_gate,),
    )
    lower, upper = plane_first(tie(routed_own, grad_slab), gates=(grad_expert_gate,))
    attention_grad = gather_slab(hidden_low, (grad_expert_gate,))
    shared_back = jnp.concatenate(
        [
            shared_gate_back[:shared_here],
            shared_up_back[:shared_here],
            shared_down_back[:shared_here],
        ]
    )
    shared_back = trade(
        jnp.transpose(shared_back.reshape(-1, count, rows_here), (1, 0, 2)), CTX
    ).astype(jnp.float32)
    grad_shared_gate = shared_back[:, :shared_here].reshape(-1, rows_here).T
    grad_shared_up = shared_back[:, shared_here : 2 * shared_here].reshape(-1, rows_here).T
    grad_shared_down = shared_back[:, 2 * shared_here :].reshape(-1, rows_here)

    grad_out_here = out_grads_kernel(head_out, attention_grad, rows_here)
    key_own, key_other, query_grad, grad_up_here = attend_back_kernel(
        attention_grad,
        query_low,
        keys_own,
        keys_other,
        up_here,
        out_here,
        prob,
        absorbed,
        latent_out,
        heads,
        scale,
        (lower, upper, grad_out_here, grad_expert_up),
    )
    routed_slab = plane_second(lower, upper, gates=(key_own,))
    key_sum = low(add(key_own, swap(key_other, "c")))
    key_sum = fold_z(scatter_plane(key_sum, ("y", "x")))
    rope = query_grad[:, heads * DN :].reshape(sequences, slab, heads, DR)
    rope = rotate(rope, cosine[:, None, :], -sine[:, None, :]).reshape(sequences * slab, -1)
    query_raw_grad = low(jnp.concatenate([query_grad[:, : heads * DN], rope], axis=1))
    input_grad = scatter_slab(product_nt_kernel(query_raw_grad, query_here))
    grad_heads = query_grads_kernel(query_raw_grad, input_low, grad_up_here, rows_here)
    output = both_halves(low(hidden_in + fold_z(routed_slab, (grad_heads,))))

    latent_back, grad_latent_norm = root_norm_back(
        key_sum[:, :R], latent_unit, latent_inverse, full_latent_norm
    )
    rope_key = rotate(key_sum[:, R:], cosine[:block], -sine[:block])
    latent_raw_grad = low(jnp.concatenate([latent_back, rope_key], axis=-1))
    latent_input = jnp.stack([dot_nt(latent_raw_grad, down) for down in down_pieces])
    latent_input = latent_input.reshape(2, 2, block, zs, rows_here)
    latent_input = by_own(by_own(latent_input, "c", 0), "x", 1)
    input_grad = input_grad + jnp.transpose(latent_input, (2, 3, 1, 0, 4)).reshape(block, width)
    source_part, grad_norm_in = root_norm_back(
        input_grad, unit_in[:block], inverse_in[:block], full_norm_in
    )
    tokens_gradient = both_halves(low(grad_hidden + source_part)).astype(jnp.float32)

    slab_latent_grad = gather_slab(latent_raw_grad)
    grad_down = low(dot_tn(input_low, slab_latent_grad)).reshape(zs, 4, rows_here, R + DR)
    grad_down = sum_z(
        lax.dynamic_index_in_dim(grad_down, x * 2 + c, 1, keepdims=False)
    )

    grad_out = trade(
        low(sum_z(grad_out_here.reshape(zs, 4, rows_here, -1), (key_own,))), ("x", "c")
    )
    grad_output = jnp.transpose(
        grad_out.reshape(4, DV, heads, rows_here), (0, 2, 1, 3)
    ).reshape(-1, rows_here).astype(jnp.float32)
    grad_heads = sum_z(
        tie(grad_heads, key_sum).reshape(zs, 4, rows_here, -1), (slab_latent_grad,)
    )
    both = trade(low(grad_heads), ("x", "c")).astype(jnp.float32)
    grad_query = jnp.transpose(both[..., :query_columns], (1, 0, 2))
    grad_query = jnp.concatenate(
        [
            grad_query[..., : heads * DN].reshape(rows_here, 4, heads, DN),
            grad_query[..., heads * DN :].reshape(rows_here, 4, heads, DR),
        ],
        axis=-1,
    ).reshape(rows_here, -1)
    grad_latent_up = jnp.transpose(
        both[..., query_columns:].reshape(4, up_columns // 128, rank_rows, 128), (2, 0, 1, 3)
    ).reshape(rank_rows, -1)

    small_grads = jnp.concatenate(
        [
            grad_router.T.reshape(experts, count, rows_here),
            grad_norm_in.reshape(1, count, rows_here),
            grad_norm_ffn.reshape(1, count, rows_here),
            jnp.pad(
                grad_latent_norm.reshape(1, count, rank_rows),
                ((0, 0), (0, 0), (0, rows_here - rank_rows)),
            ),
        ]
    )
    small_grads = trade(jnp.transpose(small_grads, (1, 0, 2)), CTX)
    small_grads = jnp.sum(small_grads, axis=0)
    small_grads = small_grads + swap(small_grads, "y")
    return (
        output,
        tokens_gradient,
        small_grads[experts],
        grad_query,
        grad_down,
        small_grads[experts + 2, :rank_rows],
        grad_latent_up,
        grad_output,
        small_grads[experts + 1],
        small_grads[:experts].T,
        grad_shared_gate,
        grad_shared_up,
        grad_shared_down,
        grad_expert_gate.T[None],
        grad_expert_up.T[None],
        grad_expert_down[None],
    )


IN_SPECS = (
    (None, "ctx", None),
    ("ctx",),
    ("ctx", "wa"),
    ("ctx", None),
    ("ctx",),
    ("ctx", "wa"),
    ("wa", "ctx"),
    ("ctx",),
    ("ctx", None),
    ("ctx", "wa"),
    ("ctx", "wa"),
    ("wa", "ctx"),
    ("ctx", None, "wa"),
    ("ctx", None, "wa"),
    ("ctx", "wa", None),
    (None, "ctx", None),
    (None, "ctx", None),
)
OUT_SPECS = ((None, "ctx", None),) * 2 + IN_SPECS[1:15]


def solution(mesh):
    count = mesh.shape["ctx"]

    def run(*arguments):
        experts = arguments[12].shape[0]
        if experts > 4 * TOPK or experts != count or mesh.shape["wa"] != 2 or count % 8:
            return jax.shard_map(
                shards,
                mesh=mesh,
                in_specs=tuple(P(*spec) for spec in IN_SPECS),
                out_specs=tuple(P(*spec) for spec in OUT_SPECS),
                check_vma=False,
            )(*arguments)
        grid = Mesh(mesh.devices.reshape(count // 4, 2, 2, 2), ("z", "x", "c", "y"))
        names = {"ctx": CTX, "wa": "y", None: None}
        return jax.shard_map(
            dense_shards,
            mesh=grid,
            in_specs=tuple(P(*[names[n] for n in spec]) for spec in IN_SPECS),
            out_specs=tuple(P(*[names[n] for n in spec]) for spec in OUT_SPECS),
            check_vma=False,
        )(*arguments)

    return run
```

```python
from functools import partial

import jax
import jax.numpy as jnp
from jax import lax
from jax.experimental import pallas as pl
from jax.experimental.layout import Layout, with_layout_constraint
from jax.experimental.pallas import tpu as pltpu
from jax.sharding import Mesh, PartitionSpec as P

DN = 128
DR = 64
DV = 128
R = 512
TOPK = 6


epsilon = 1e-06
highest = lax.Precision.HIGHEST


def shifted(value, axis, steps):
    count = lax.axis_size(axis)
    pairs = [(source, (source + steps) % count) for source in range(count)]
    return lax.ppermute(value, axis, pairs)


def root_norm(values, gain):
    inverse = lax.rsqrt(jnp.mean(values * values, axis=-1, keepdims=True) + epsilon)
    unit = values * inverse
    return (unit * gain, unit, inverse)


def root_norm_back(upstream, unit, inverse, gain):
    scaled = upstream * gain
    inner = jnp.mean(scaled * unit, axis=-1, keepdims=True)
    leading = tuple(range(upstream.ndim - 1))
    return (inverse * (scaled - unit * inner), jnp.sum(upstream * unit, axis=leading))


def rotary_tables(positions, width):
    half = width // 2
    frequency = 10000.0 ** (-jnp.arange(half, dtype=jnp.float32) * 2.0 / width)
    angle = positions.astype(jnp.float32)[:, None] * frequency[None, :]
    return (jnp.cos(angle), jnp.sin(angle))


def rotate(values, cosine, sine):
    half = values.shape[-1] // 2
    first = values[..., :half]
    second = values[..., half:]
    return jnp.concatenate(
        [first * cosine - second * sine, second * cosine + first * sine], axis=-1
    )


def silu_slope(values):
    sigmoid = jax.nn.sigmoid(values)
    return sigmoid * (1.0 + values * (1.0 - sigmoid))


def fetch_weights(
    norm_in,
    query_weight,
    latent_down,
    latent_norm,
    latent_up,
    output_weight,
    norm_ffn,
    router_weight,
    shared_gate,
    shared_up,
    shared_down,
):
    return (
        lax.all_gather(norm_in, "ctx", axis=0, tiled=True),
        lax.all_gather(query_weight, "ctx", axis=0, tiled=True),
        lax.all_gather(latent_down, "ctx", axis=0, tiled=True),
        lax.all_gather(latent_norm, "ctx", axis=0, tiled=True),
        lax.all_gather(latent_up, "ctx", axis=0, tiled=True),
        lax.all_gather(output_weight, "ctx", axis=1, tiled=True),
        lax.all_gather(norm_ffn, "ctx", axis=0, tiled=True),
        lax.all_gather(router_weight, "ctx", axis=0, tiled=True),
        lax.all_gather(shared_gate, "ctx", axis=0, tiled=True),
        lax.all_gather(shared_up, "ctx", axis=0, tiled=True),
        lax.all_gather(shared_down, "ctx", axis=1, tiled=True),
    )


def shards(
    tokens,
    norm_in,
    query_weight,
    latent_down,
    latent_norm,
    latent_up,
    output_weight,
    norm_ffn,
    router_weight,
    shared_gate,
    shared_up,
    shared_down,
    expert_gate,
    expert_up,
    expert_down,
    routes,
    cotangent,
):
    context_count = lax.axis_size("ctx")
    context_index = lax.axis_index("ctx")
    lead = (lax.axis_index("wa") == 0).astype(jnp.float32)
    sequences, block, width = tokens.shape
    local_experts = expert_gate.shape[0]
    experts = context_count * local_experts
    capacity = max(2, block * TOPK * 4 // (3 * experts))
    scale = (DN + DR) ** (-0.5)
    gathered = fetch_weights(
        norm_in,
        query_weight,
        latent_down,
        latent_norm,
        latent_up,
        output_weight,
        norm_ffn,
        router_weight,
        shared_gate,
        shared_up,
        shared_down,
    )
    (
        full_norm_in,
        full_query,
        full_down,
        full_latent_norm,
        full_up,
        full_output,
        full_norm_ffn,
        full_router,
        full_shared_gate,
        full_shared_up,
        full_shared_down,
    ) = gathered
    heads_here = full_up.shape[1] // (DN + DV)
    positions = context_index * block + jnp.arange(block)
    cosine, sine = rotary_tables(positions, DR)
    source = tokens.astype(jnp.float32)
    normed_in, unit_in, inverse_in = root_norm(source, full_norm_in.astype(jnp.float32))
    input_low = normed_in.astype(jnp.bfloat16)
    query_raw = jnp.dot(input_low, full_query, preferred_element_type=jnp.float32).reshape(
        sequences, block, heads_here, DN + DR
    )
    query_low = jnp.concatenate(
        [query_raw[..., :DN], rotate(query_raw[..., DN:], cosine[:, None, :], sine[:, None, :])],
        axis=-1,
    ).astype(jnp.bfloat16)
    up_view = full_up.reshape(R, heads_here, DN + DV)
    key_up = up_view[..., :DN]
    value_up = up_view[..., DN:]
    absorbed = jnp.einsum(
        "sbhn,rhn->shbr", query_low[..., :DN], key_up, preferred_element_type=jnp.float32
    )
    query_rows = jnp.concatenate(
        [absorbed.astype(jnp.bfloat16), jnp.transpose(query_low[..., DN:], (0, 2, 1, 3))], axis=-1
    )
    latent_raw = jnp.dot(input_low, full_down, preferred_element_type=jnp.float32)
    latent_scaled, latent_unit, latent_inverse = root_norm(
        latent_raw[..., :R], full_latent_norm.astype(jnp.float32)
    )
    key_rows = jnp.concatenate(
        [latent_scaled, rotate(latent_raw[..., R:], cosine, sine)], axis=-1
    ).astype(jnp.bfloat16)
    piece = lax.all_gather(key_rows, "ctx", axis=1, tiled=True)
    top = jnp.full((sequences, heads_here, block), -1e30, jnp.float32)
    scores = (
        jnp.einsum("shqc,skc->shqk", query_rows, piece, preferred_element_type=jnp.float32) * scale
    )
    key_positions = jnp.arange(piece.shape[1])
    allowed = positions[:, None] >= key_positions[None, :]
    scores = jnp.where(allowed, scores, -1e30)
    new_top = jnp.maximum(top, jnp.max(scores, axis=-1))
    weights = jnp.where(allowed, jnp.exp(scores - new_top[..., None]), 0.0)
    total = jnp.sum(weights, axis=-1)
    weights_high = weights.astype(jnp.bfloat16)
    weights_rest = (weights - weights_high.astype(jnp.float32)).astype(jnp.bfloat16)
    running = jnp.einsum(
        "shqk,skr->shqr", weights_high, piece[..., :R], preferred_element_type=jnp.float32
    )
    remainder = jnp.einsum(
        "shqk,skr->shqr", weights_rest, piece[..., :R], preferred_element_type=jnp.float32
    )
    top, total, running, remainder = (new_top, total, running, remainder)
    log_total = top + jnp.log(total)
    latent_out = (running / total[..., None]).astype(jnp.bfloat16)
    latent_exact = (running + remainder) / total[..., None]
    head_out = (
        jnp.einsum("shbr,rhv->sbhv", latent_out, value_up, preferred_element_type=jnp.float32)
        .astype(jnp.bfloat16)
        .reshape(sequences, block, heads_here * DV)
    )
    attention_part = jnp.dot(head_out, full_output, preferred_element_type=jnp.float32)
    hidden_in = source + lax.psum(attention_part, "wa")
    normed_ffn, unit_ffn, inverse_ffn = root_norm(hidden_in, full_norm_ffn.astype(jnp.float32))
    ffn_low = normed_ffn.astype(jnp.bfloat16)
    shares = jax.nn.softmax(
        jnp.dot(ffn_low, full_router, preferred_element_type=jnp.float32), axis=-1
    )
    shared_g = jnp.dot(ffn_low, full_shared_gate, preferred_element_type=jnp.float32)
    shared_u = jnp.dot(ffn_low, full_shared_up, preferred_element_type=jnp.float32)
    shared_silu = jax.nn.silu(shared_g)
    shared_activation = (shared_silu * shared_u).astype(jnp.bfloat16)
    shared_part = jnp.dot(shared_activation, full_shared_down, preferred_element_type=jnp.float32)
    expert_ids = jnp.arange(experts, dtype=jnp.int32)
    chosen = (
        (routes[..., None] == expert_ids)
        .astype(jnp.int32)
        .reshape(sequences, block * TOPK, experts)
    )
    earlier = jnp.cumsum(chosen, axis=1) - chosen
    slot_of = jnp.sum(earlier * chosen, axis=-1).reshape(sequences, block, TOPK)
    slot_ids = jnp.arange(capacity, dtype=jnp.int32)
    hit = (routes[None, :, :, :, None] == expert_ids[:, None, None, None, None]) & (
        slot_of[None, :, :, :, None] == slot_ids[None, None, None, None, :]
    )
    dispatch = jnp.transpose(jnp.any(hit, axis=3), (0, 1, 3, 2)).astype(jnp.float32)
    send = (
        jnp.einsum(
            "escb,sbd->escd",
            dispatch.astype(jnp.bfloat16),
            ffn_low,
            preferred_element_type=jnp.float32,
        )
        .astype(jnp.bfloat16)
        .reshape(experts, sequences * capacity, width)
    )
    slot_share = jnp.einsum("escb,sbe->esc", dispatch, shares, precision=highest)
    received = lax.all_to_all(send, "ctx", split_axis=0, concat_axis=0, tiled=True)
    count = received.shape[1]
    rows = received.reshape(context_count, local_experts, count, width)
    gate_pre = jnp.einsum("nesd,edf->nesf", rows, expert_gate, preferred_element_type=jnp.float32)
    up_pre = jnp.einsum("nesd,edf->nesf", rows, expert_up, preferred_element_type=jnp.float32)
    activation = (jax.nn.silu(gate_pre) * up_pre).astype(jnp.bfloat16)
    result = jnp.einsum(
        "nesf,efd->nesd", activation, expert_down, preferred_element_type=jnp.float32
    ).reshape(experts, count, width)
    returned = lax.all_to_all(result, "ctx", split_axis=0, concat_axis=0, tiled=True)
    hidden_units = gate_pre.shape[-1]
    returned, received, gate_keep, up_keep = (
        returned,
        received,
        gate_pre.reshape(experts, count, hidden_units),
        up_pre.reshape(experts, count, hidden_units),
    )
    returned = returned.reshape(experts, sequences, capacity, width)
    routed_part = jnp.einsum(
        "escb,escd->sbd", dispatch, returned * slot_share[..., None], precision=highest
    )
    output = hidden_in + lax.psum(shared_part + routed_part, "wa")
    gathered = fetch_weights(
        norm_in,
        query_weight,
        latent_down,
        latent_norm,
        latent_up,
        output_weight,
        norm_ffn,
        router_weight,
        shared_gate,
        shared_up,
        shared_down,
    )
    (
        full_norm_in,
        full_query,
        full_down,
        full_latent_norm,
        full_up,
        full_output,
        full_norm_ffn,
        full_router,
        full_shared_gate,
        full_shared_up,
        full_shared_down,
    ) = gathered
    up_view = full_up.reshape(R, heads_here, DN + DV)
    key_up = up_view[..., :DN]
    value_up = up_view[..., DN:]
    grad_y = cotangent.astype(jnp.float32)
    shared_grad = jnp.einsum(
        "sbd,fd->sbf", cotangent, full_shared_down, preferred_element_type=jnp.float32
    )
    shared_gate_grad = (shared_grad * shared_u * silu_slope(shared_g)).astype(jnp.bfloat16)
    shared_up_grad = (shared_grad * shared_silu).astype(jnp.bfloat16)
    grad_shared_down = jnp.einsum(
        "sbf,sbd->fd", shared_activation, cotangent, preferred_element_type=jnp.float32
    )
    grad_shared_gate = jnp.einsum(
        "sbd,sbf->df", ffn_low, shared_gate_grad, preferred_element_type=jnp.float32
    )
    grad_shared_up = jnp.einsum(
        "sbd,sbf->df", ffn_low, shared_up_grad, preferred_element_type=jnp.float32
    )
    ffn_grad = jnp.einsum(
        "sbf,df->sbd", shared_gate_grad, full_shared_gate, preferred_element_type=jnp.float32
    )
    ffn_grad = ffn_grad + jnp.einsum(
        "sbf,df->sbd", shared_up_grad, full_shared_up, preferred_element_type=jnp.float32
    )
    grad_at_slots = jnp.einsum("escb,sbd->escd", dispatch, grad_y, precision=highest)
    slot_grads = (
        (grad_at_slots * slot_share[..., None])
        .astype(jnp.bfloat16)
        .reshape(experts, sequences * capacity, width)
    )
    slot_dot = jnp.sum(returned * grad_at_slots, axis=-1)
    share_grad = jnp.einsum("escb,esc->sbe", dispatch, slot_dot, precision=highest)
    logit_grad = shares * (share_grad - jnp.sum(shares * share_grad, axis=-1, keepdims=True))
    grad_router = jnp.einsum(
        "sbd,sbe->de", ffn_low.astype(jnp.float32), logit_grad, precision=highest
    )
    ffn_grad = ffn_grad + jnp.einsum(
        "sbe,de->sbd", logit_grad, full_router.astype(jnp.float32), precision=highest
    )
    slot_back = lax.all_to_all(slot_grads, "ctx", split_axis=0, concat_axis=0, tiled=True).reshape(
        context_count, local_experts, -1, width
    )
    rows = received.reshape(context_count, local_experts, -1, width)
    gate_pre = gate_keep.reshape(context_count, local_experts, -1, gate_keep.shape[-1])
    up_pre = up_keep.reshape(context_count, local_experts, -1, up_keep.shape[-1])
    hidden_grad = jnp.einsum(
        "nesd,efd->nesf", slot_back, expert_down, preferred_element_type=jnp.float32
    )
    silu_gate = jax.nn.silu(gate_pre)
    gate_grad = (hidden_grad * up_pre * silu_slope(gate_pre)).astype(jnp.bfloat16)
    up_grad = (hidden_grad * silu_gate).astype(jnp.bfloat16)
    activation = (silu_gate * up_pre).astype(jnp.bfloat16)
    grad_expert_down = jnp.einsum(
        "nesf,nesd->efd", activation, slot_back, preferred_element_type=jnp.float32
    )
    grad_expert_gate = jnp.einsum(
        "nesd,nesf->edf", rows, gate_grad, preferred_element_type=jnp.float32
    )
    grad_expert_up = jnp.einsum("nesd,nesf->edf", rows, up_grad, preferred_element_type=jnp.float32)
    rows_grad = jnp.einsum(
        "nesf,edf->nesd", gate_grad, expert_gate, preferred_element_type=jnp.float32
    )
    rows_grad = rows_grad + jnp.einsum(
        "nesf,edf->nesd", up_grad, expert_up, preferred_element_type=jnp.float32
    )
    slot_grad = lax.all_to_all(
        rows_grad.reshape(experts, -1, width), "ctx", split_axis=0, concat_axis=0, tiled=True
    ).reshape(experts, sequences, capacity, width)
    ffn_grad = ffn_grad + jnp.einsum("escb,escd->sbd", dispatch, slot_grad, precision=highest)
    hidden_part, grad_norm_ffn = root_norm_back(
        ffn_grad, unit_ffn, inverse_ffn, full_norm_ffn.astype(jnp.float32)
    )
    grad_hidden = grad_y + lax.psum(hidden_part, "wa")
    attention_grad = grad_hidden.astype(jnp.bfloat16)
    grad_output = jnp.einsum(
        "sbk,sbd->kd", head_out, attention_grad, preferred_element_type=jnp.float32
    )
    head_grad = (
        jnp.einsum("sbd,kd->sbk", attention_grad, full_output, preferred_element_type=jnp.float32)
        .astype(jnp.bfloat16)
        .reshape(sequences, block, heads_here, DV)
    )
    grad_value_up = jnp.einsum(
        "shbr,sbhv->rhv", latent_out, head_grad, preferred_element_type=jnp.float32
    )
    latent_out_grad = jnp.einsum(
        "sbhv,rhv->shbr", head_grad, value_up, preferred_element_type=jnp.float32
    ).astype(jnp.bfloat16)
    row_dot = jnp.sum(latent_out_grad.astype(jnp.float32) * latent_exact, axis=-1)

    def turn_body(turn, carry):
        keys_here, key_grad, query_grad = carry
        source_index = (context_index + turn) % context_count
        key_positions = source_index * block + jnp.arange(block)
        allowed = positions[:, None] >= key_positions[None, :]
        scores = (
            jnp.einsum("shqc,skc->shqk", query_rows, keys_here, preferred_element_type=jnp.float32)
            * scale
        )
        weights = jnp.where(allowed[None, None], jnp.exp(scores - log_total[..., None]), 0.0)
        weight_grad = jnp.einsum(
            "shqr,skr->shqk",
            latent_out_grad,
            keys_here[..., :R],
            preferred_element_type=jnp.float32,
        )
        score_grad = (weights * (weight_grad - row_dot[..., None])).astype(jnp.bfloat16)
        query_grad = (
            query_grad
            + jnp.einsum(
                "shqk,skc->shqc", score_grad, keys_here, preferred_element_type=jnp.float32
            )
            * scale
        )
        key_part = (
            jnp.einsum("shqk,shqc->skc", score_grad, query_rows, preferred_element_type=jnp.float32)
            * scale
        )
        value_part = jnp.einsum(
            "shqk,shqr->skr",
            weights.astype(jnp.bfloat16),
            latent_out_grad,
            preferred_element_type=jnp.float32,
        )
        key_grad = key_grad + key_part + jnp.pad(value_part, ((0, 0), (0, 0), (0, DR)))
        keys_next = shifted(keys_here, "ctx", -1)
        grad_next = shifted(key_grad, "ctx", -1)
        return (keys_next, grad_next, query_grad)

    start_back = (
        key_rows,
        jnp.zeros((sequences, block, R + DR), jnp.float32),
        jnp.zeros((sequences, heads_here, block, R + DR), jnp.float32),
    )
    unused_keys, key_grad, query_grad = lax.fori_loop(0, context_count, turn_body, start_back)
    key_grad_total = lax.psum(key_grad, "wa")
    query_grad_low = query_grad.astype(jnp.bfloat16)
    absorbed_grad = query_grad_low[..., :R]
    rope_query_grad = jnp.transpose(query_grad_low[..., R:], (0, 2, 1, 3)).astype(jnp.float32)
    grad_key_up = jnp.einsum(
        "shbr,sbhn->rhn", absorbed_grad, query_low[..., :DN], preferred_element_type=jnp.float32
    )
    nope_grad = jnp.einsum(
        "shbr,rhn->sbhn", absorbed_grad, key_up, preferred_element_type=jnp.float32
    )
    rope_raw_grad = rotate(rope_query_grad, cosine[:, None, :], -sine[:, None, :])
    query_raw_grad = (
        jnp.concatenate([nope_grad, rope_raw_grad], axis=-1)
        .astype(jnp.bfloat16)
        .reshape(sequences, block, heads_here * (DN + DR))
    )
    grad_query = jnp.einsum(
        "sbd,sbk->dk", input_low, query_raw_grad, preferred_element_type=jnp.float32
    )
    input_part = jnp.einsum(
        "sbk,dk->sbd", query_raw_grad, full_query, preferred_element_type=jnp.float32
    )
    grad_latent_up = jnp.concatenate([grad_key_up, grad_value_up], axis=-1).reshape(
        R, heads_here * (DN + DV)
    )
    latent_grad, grad_latent_norm = root_norm_back(
        key_grad_total[..., :R], latent_unit, latent_inverse, full_latent_norm.astype(jnp.float32)
    )
    rope_key_grad = rotate(key_grad_total[..., R:], cosine, -sine)
    latent_raw_grad = jnp.concatenate([latent_grad, rope_key_grad], axis=-1).astype(jnp.bfloat16)
    grad_down = jnp.einsum(
        "sbd,sbc->dc", input_low, latent_raw_grad, preferred_element_type=jnp.float32
    )
    input_part = input_part + lead * jnp.einsum(
        "sbc,dc->sbd", latent_raw_grad, full_down, preferred_element_type=jnp.float32
    )
    source_part, grad_norm_in = root_norm_back(
        input_part, unit_in, inverse_in, full_norm_in.astype(jnp.float32)
    )
    summed = lax.psum((source_part, grad_norm_in, grad_norm_ffn, grad_router), "wa")
    tokens_gradient = grad_hidden + summed[0]
    reduced = (
        lax.psum_scatter(summed[1], "ctx", scatter_dimension=0, tiled=True),
        lax.psum_scatter(grad_query, "ctx", scatter_dimension=0, tiled=True),
        lax.psum_scatter(grad_down, "ctx", scatter_dimension=0, tiled=True),
        lax.psum_scatter(grad_latent_norm, "ctx", scatter_dimension=0, tiled=True),
        lax.psum_scatter(grad_latent_up, "ctx", scatter_dimension=0, tiled=True),
        lax.psum_scatter(grad_output, "ctx", scatter_dimension=1, tiled=True),
        lax.psum_scatter(summed[2], "ctx", scatter_dimension=0, tiled=True),
        lax.psum_scatter(summed[3], "ctx", scatter_dimension=0, tiled=True),
        lax.psum_scatter(grad_shared_gate, "ctx", scatter_dimension=0, tiled=True),
        lax.psum_scatter(grad_shared_up, "ctx", scatter_dimension=0, tiled=True),
        lax.psum_scatter(grad_shared_down, "ctx", scatter_dimension=1, tiled=True),
    )
    return (
        output.astype(jnp.bfloat16),
        tokens_gradient,
        reduced[0],
        reduced[1],
        reduced[2],
        reduced[3],
        reduced[4],
        reduced[5],
        reduced[6],
        reduced[7],
        reduced[8],
        reduced[9],
        reduced[10],
        grad_expert_gate,
        grad_expert_up,
        grad_expert_down,
    )


VMEM_LIMIT = 60 * 1024 * 1024
TILE = 256


def local_call(body, grid, in_specs, out_specs, out_shape, operands, after=()):
    inputs = len(in_specs)

    def run(*refs):
        body(*refs[:inputs], *refs[inputs + len(after) :])

    return pl.pallas_call(
        run,
        grid=grid,
        in_specs=list(in_specs) + [pl.BlockSpec(memory_space=pl.ANY)] * len(after),
        out_specs=out_specs,
        out_shape=out_shape,
        compiler_params=pltpu.CompilerParams(vmem_limit_bytes=VMEM_LIMIT),
        cost_estimate=pl.CostEstimate(flops=1, bytes_accessed=1, transcendentals=0),
    )(*operands, *after)


def whole(array):
    return pl.BlockSpec(array.shape, lambda *_: (0,) * array.ndim)


def by_rows(array, rows=TILE):
    return pl.BlockSpec((rows, array.shape[1]), lambda i: (i, 0))


def by_first(array):
    return pl.BlockSpec((1,) + array.shape[1:], lambda i: (i,) + (0,) * (array.ndim - 1))


def shaped(shape, dtype=jnp.bfloat16):
    return jax.ShapeDtypeStruct(shape, dtype)


def mul(left, right):
    return jnp.dot(left, right, preferred_element_type=jnp.float32)


def mul_nt(left, right):
    return lax.dot_general(
        left, right, (((1,), (1,)), ((), ())), preferred_element_type=jnp.float32
    )


def mul_tn(left, right):
    return lax.dot_general(
        left, right, (((0,), (0,)), ((), ())), preferred_element_type=jnp.float32
    )


def glu_back(gate, up, grads):
    sigmoid = 1.0 / (1.0 + jnp.exp(-gate))
    silu = gate * sigmoid
    slope = sigmoid * (1.0 + gate * (1.0 - sigmoid))
    return (silu * up, grads * up * slope, grads * silu)


def feed_body(
    experts, rows, back, shared_back, gate_t, up_t, small_t, named, pick,
    act_out, shared_act_out, gate_out, up_out, shared_out, gain_out,
):
    here = rows[...]
    part = small_t.shape[0] // 3
    small = mul_nt(here, small_t[...])
    logits = small[:, 2 * part :]
    ids = lax.broadcasted_iota(jnp.int32, logits.shape, 1)
    logits = jnp.where(ids < experts, logits, -1e30)
    chances = jnp.exp(logits - jnp.max(logits, axis=1, keepdims=True))
    total = jnp.sum(chances, axis=1, keepdims=True)
    named_here = named[...]
    share = jnp.sum(chances * pick[...], axis=1, keepdims=True) / total * named_here
    act, gate_grad, up_grad = glu_back(
        small[:, :part], small[:, part : 2 * part], shared_back[...].astype(jnp.float32)
    )
    shared_act_out[...] = act.astype(jnp.bfloat16)
    shared_out[:, :part] = gate_grad.astype(jnp.bfloat16)
    shared_out[:, part:] = up_grad.astype(jnp.bfloat16)
    grads = back[...].astype(jnp.float32)
    act, gate_grad, up_grad = glu_back(mul_nt(here, gate_t[...]), mul_nt(here, up_t[...]), grads)
    gain_out[...] = jnp.sum(act * grads, axis=1, keepdims=True) * named_here
    act_out[...] = (act * share).astype(jnp.bfloat16)
    gate_out[...] = (gate_grad * share).astype(jnp.bfloat16)
    up_out[...] = (up_grad * share).astype(jnp.bfloat16)


def feed_kernel(rows, back, shared_back, gate_t, up_t, small_t, named, pick, experts):
    count = rows.shape[0]
    hidden, part = (back.shape[1], shared_back.shape[1])
    shapes = [shaped((count, s)) for s in (hidden, part, hidden, hidden, 2 * part)]
    shapes.append(shaped((count, 1), jnp.float32))
    return local_call(
        partial(feed_body, experts),
        (count // TILE,),
        [
            by_rows(rows),
            by_rows(back),
            by_rows(shared_back),
            whole(gate_t),
            whole(up_t),
            whole(small_t),
            by_rows(named),
            whole(pick),
        ],
        [by_rows(s) for s in shapes],
        shapes,
        (rows, back, shared_back, gate_t, up_t, small_t, named, pick),
    )


def input_body(gate, up, shared, gate_t, up_t, small_t, gain, pick, out):
    width = gate_t.shape[1]
    used = shared.shape[1]
    out[:, :width] = (
        mul(gate[...], gate_t[...]) + mul(up[...], up_t[...]) + mul(shared[...], small_t[:used, :])
    ).astype(jnp.bfloat16)
    out[:, width:] = (gain[...] * pick[...]).astype(jnp.bfloat16)


def input_kernel(gate, up, shared, gate_t, up_t, small_t, gain, pick, after=()):
    count = gate.shape[0]
    shape = shaped((count, gate_t.shape[1] + pick.shape[1]))
    return local_call(
        input_body,
        (count // TILE,),
        [by_rows(gate), by_rows(up), by_rows(shared)]
        + [whole(gate_t), whole(up_t), whole(small_t), by_rows(gain), whole(pick)],
        by_rows(shape),
        shape,
        (gate, up, shared, gate_t, up_t, small_t, gain, pick),
        after,
    )


def result_body(act, shared_act, down, shared_down, out):
    out[...] = (mul(act[...], down[...]) + mul(shared_act[...], shared_down[...])).astype(
        jnp.bfloat16
    )


def result_kernel(act, shared_act, down, shared_down, after=()):
    count = act.shape[0]
    shape = shaped((count, down.shape[1]))
    return local_call(
        result_body,
        (count // TILE,),
        [by_rows(act), by_rows(shared_act), whole(down), whole(shared_down)],
        by_rows(shape),
        shape,
        (act, shared_act, down, shared_down),
        after,
    )


def weight_body(left_own, left_other, more_own, more_other, own, other, out, more_out):
    here, there = (own[...], other[...])
    out[...] = mul_tn(left_own[...], here) + mul_tn(left_other[...], there)
    more_out[...] = (mul_tn(more_own[...], here) + mul_tn(more_other[...], there)).astype(
        jnp.bfloat16
    )


def weight_kernel(lefts, mores, rights, side=0, part=128, after=()):
    count, width = rights[0].shape
    columns = lambda rows: pl.BlockSpec((rows, TILE), lambda i: (0, i))
    hidden, more = (lefts[0].shape[1], part)
    return local_call(
        weight_body,
        (width // TILE,),
        [whole(a) for a in lefts]
        + [pl.BlockSpec((count, part), lambda i: (0, side))] * 2
        + [columns(count)] * 2,
        [columns(hidden), columns(more)],
        [shaped((hidden, width), jnp.float32), shaped((more, width))],
        (*lefts, *mores, *rights),
        after,
    )


def head_parts_of(query, heads, nope):
    rope = query.shape[1] // heads - nope
    return [
        (
            query[:, k * nope : (k + 1) * nope],
            query[:, heads * nope + k * rope : heads * nope + (k + 1) * rope],
        )
        for k in range(heads)
    ]


def attend_body(
    heads, scale, query, own, other, up, out_weight, spots, key_spots,
    kept_out, sent_out, prob_out, absorbed_out, latent_out, head_out,
):
    rank = up.shape[0]
    absorbed, ropes = ([], [])
    for k, (nope, rope) in enumerate(head_parts_of(query[...], heads, DN)):
        key_up = up[:, k * (DN + DV) : k * (DN + DV) + DN]
        absorbed.append(mul_nt(nope, key_up).astype(jnp.bfloat16))
        ropes.append(rope)
    absorbed = jnp.concatenate(absorbed, axis=0)
    rope = jnp.concatenate(ropes, axis=0)
    absorbed_out[0] = absorbed
    keys = [source[0, k] for source in (own, other) for k in range(2)]
    scores = jnp.concatenate(
        [mul_nt(absorbed, key[:, :rank]) + mul_nt(rope, key[:, rank:]) for key in keys], axis=1
    )
    allowed = spots[...] >= key_spots[...]
    allowed = jnp.concatenate([allowed] * heads, axis=0)
    scores = jnp.where(allowed, scores * scale, -1e30)
    weights = jnp.exp(scores - jnp.max(scores, axis=1, keepdims=True))
    prob = (weights / jnp.sum(weights, axis=1, keepdims=True)).astype(jnp.bfloat16)
    prob_out[0] = prob
    size = keys[0].shape[0]
    latent = sum(
        mul(prob[:, j * size : (j + 1) * size], key[:, :rank]) for j, key in enumerate(keys)
    ).astype(jnp.bfloat16)
    latent_out[0] = latent
    rows = query.shape[0]
    head = jnp.concatenate(
        [
            mul(
                latent[k * rows : (k + 1) * rows],
                up[:, k * (DN + DV) + DN : (k + 1) * (DN + DV)],
            )
            for k in range(heads)
        ],
        axis=1,
    ).astype(jnp.bfloat16)
    head_out[...] = head
    total = mul(head, out_weight[...]).astype(jnp.bfloat16)
    kept_out[0] = total[: rows // 2]
    sent_out[0] = total[rows // 2 :]


def attend_kernel(query, own, other, up, out_weight, spots, key_spots, heads, scale, after=()):
    sequences = own.shape[0]
    rows = query.shape[0] // sequences
    key_count = 4 * own.shape[2]
    rank = up.shape[0]
    shapes = [
        shaped((sequences, rows // 2, out_weight.shape[1])),
        shaped((sequences, rows // 2, out_weight.shape[1])),
        shaped((sequences, heads * rows, key_count)),
        shaped((sequences, heads * rows, rank)),
        shaped((sequences, heads * rows, rank)),
        shaped((query.shape[0], heads * DV)),
    ]
    return local_call(
        partial(attend_body, heads, scale),
        (sequences,),
        [by_rows(query, rows), by_first(own), by_first(other)]
        + [whole(a) for a in (up, out_weight, spots, key_spots)],
        [by_first(shape) for shape in shapes[:5]] + [by_rows(shapes[5], rows)],
        shapes,
        (query, own, other, up, out_weight, spots, key_spots),
        after,
    )


def attend_back_body(
    heads, scale, grads, query, own, other, up, out_weight, prob, absorbed, latent,
    own_out, other_out, query_out, up_out,
):
    rank = up.shape[0]
    rows = query.shape[0]
    first = pl.program_id(0) == 0
    grads_here = grads[...]
    head_grad = mul_nt(grads_here, out_weight[...]).astype(jnp.bfloat16)
    span = lambda k: slice(k * rows, (k + 1) * rows)
    latent_grad = []
    value_parts = []
    for k in range(heads):
        mine = head_grad[:, k * DV : (k + 1) * DV]
        value_up = up[:, k * (DN + DV) + DN : (k + 1) * (DN + DV)]
        latent_grad.append(mul_nt(mine, value_up).astype(jnp.bfloat16))
        value_parts.append(mul_tn(latent[0, span(k)], mine))
    latent_grad = jnp.concatenate(latent_grad, axis=0)
    keys = [source[0, k] for source in (own, other) for k in range(2)]
    size = keys[0].shape[0]
    prob_here = prob[0]
    prob_wide = prob_here.astype(jnp.float32)
    prob_grad = jnp.concatenate([mul_nt(latent_grad, key[:, :rank]) for key in keys], axis=1)
    inner = jnp.sum(prob_wide * prob_grad, axis=1, keepdims=True)
    score_grad = (prob_wide * (prob_grad - inner)).astype(jnp.bfloat16)
    absorbed_here = absorbed[0]
    parts = head_parts_of(query[...], heads, DN)
    rope = jnp.concatenate([part[1] for part in parts], axis=0)
    wide = 0.0
    narrow = 0.0
    for j, key in enumerate(keys):
        piece = score_grad[:, j * size : (j + 1) * size]
        wide = wide + mul(piece, key[:, :rank])
        narrow = narrow + mul(piece, key[:, rank:])
        target = (own_out, other_out)[j // 2]
        value = mul_tn(prob_here[:, j * size : (j + 1) * size], latent_grad)
        target[0, j % 2, :, :rank] = (mul_tn(piece, absorbed_here) * scale + value).astype(
            jnp.bfloat16
        )
        target[0, j % 2, :, rank:] = (mul_tn(piece, rope) * scale).astype(jnp.bfloat16)
    wide = (wide * scale).astype(jnp.bfloat16)
    narrow = narrow * scale
    for k in range(heads):
        start = k * (DN + DV)
        key_part = mul_tn(wide[span(k)], parts[k][0])
        up_out[:, start : start + DN] = (
            jnp.where(first, 0.0, up_out[:, start : start + DN]) + key_part
        )
        up_out[:, start + DN : start + DN + DV] = (
            jnp.where(first, 0.0, up_out[:, start + DN : start + DN + DV]) + value_parts[k]
        )
        query_out[:, k * DN : (k + 1) * DN] = mul(wide[span(k)], up[:, start : start + DN])
        rope_size = narrow.shape[1]
        at = heads * DN + k * rope_size
        query_out[:, at : at + rope_size] = narrow[span(k)]


def attend_back_kernel(
    grads, query, own, other, up, out_weight, prob, absorbed, latent, heads, scale, after=()
):
    sequences = own.shape[0]
    rows = query.shape[0] // sequences
    shapes = [
        shaped(own.shape),
        shaped(own.shape),
        shaped(query.shape, jnp.float32),
        shaped(up.shape, jnp.float32),
    ]
    return local_call(
        partial(attend_back_body, heads, scale),
        (sequences,),
        [by_rows(grads, rows), by_rows(query, rows), by_first(own), by_first(other)]
        + [whole(up), whole(out_weight), by_first(prob), by_first(absorbed), by_first(latent)],
        [by_first(own), by_first(own), by_rows(query, rows), whole(up)],
        shapes,
        (grads, query, own, other, up, out_weight, prob, absorbed, latent),
        after,
    )


def heads_body(parts, *refs):
    query_out, up_out, out_out = refs
    count, groups, rows, _ = parts.shape
    query_columns = query_out.shape[1]
    up_blocks = up_out.shape[1] // 128
    up_rows = rows // up_blocks
    heads = out_out.shape[0] // rows
    for block in range(count * groups):
        here = parts[block // groups, block % groups]
        span = slice(block * rows, (block + 1) * rows)
        query_out[span, :] = here[:, :query_columns]
        for k in range(up_blocks):
            up_out[block * up_rows : (block + 1) * up_rows, k * 128 : (k + 1) * 128] = here[
                k * up_rows : (k + 1) * up_rows, query_columns : query_columns + 128
            ]
        for k in range(heads):
            at = query_columns + 128 + k * rows
            out_out[k * rows : (k + 1) * rows, span] = here[:, at : at + rows]


def heads_kernel(parts, query_columns, heads, up_columns, after=()):
    count, groups, rows, _ = parts.shape
    width = count * groups * rows
    up_rows = rows * 128 // up_columns
    shapes = [
        shaped((width, query_columns)),
        shaped((count * groups * up_rows, up_columns)),
        shaped((heads * rows, width)),
    ]
    return local_call(
        heads_body,
        (1,),
        [whole(parts)],
        [whole(s) for s in shapes],
        shapes,
        (parts,),
        after,
    )


SCALAR = pl.BlockSpec(memory_space=pltpu.SMEM)


def out_grads_body(rows, z, head, grads, *outs):
    heads = head.shape[1] // rows
    for s, out in enumerate(outs):
        size = out.shape[0] * rows
        start = pl.multiple_of(lax.rem(z[0] + s, len(outs)) * size, size)
        total = mul_tn(head[...], grads[:, pl.ds(start, size)]).astype(jnp.bfloat16)
        for j in range(out.shape[0]):
            for k in range(heads):
                out[j, :, k * rows : (k + 1) * rows] = total[
                    k * rows : (k + 1) * rows, j * rows : (j + 1) * rows
                ]


def out_grads_kernel(z, count, head, grads, rows):
    shapes = [shaped((grads.shape[1] // (rows * count), rows, head.shape[1]))] * count
    return local_call(
        partial(out_grads_body, rows),
        (1,),
        [SCALAR, whole(head), whole(grads)],
        [whole(s) for s in shapes],
        shapes,
        (z, head, grads),
    )


def query_grads_body(rows, z, grads, source, up, *outs):
    columns = grads.shape[1]
    up_blocks = up.shape[1] // 128
    up_rows = rows // up_blocks
    here = grads[...]
    for s, out in enumerate(outs):
        groups = out.shape[0]
        place = lax.rem(z[0] + s, len(outs))
        start = pl.multiple_of(place * groups * rows, groups * rows)
        total = mul_tn(source[:, pl.ds(start, groups * rows)], here).astype(jnp.bfloat16)
        start = pl.multiple_of(place * groups * up_rows, groups * up_rows)
        more = up[pl.ds(start, groups * up_rows), :].astype(jnp.bfloat16)
        for j in range(groups):
            out[j, :, :columns] = total[j * rows : (j + 1) * rows]
            for k in range(up_blocks):
                out[j, k * up_rows : (k + 1) * up_rows, columns:] = more[
                    j * up_rows : (j + 1) * up_rows, k * 128 : (k + 1) * 128
                ]


def query_grads_kernel(z, count, grads, source, up, rows, after=()):
    shapes = [shaped((source.shape[1] // (rows * count), rows, grads.shape[1] + 128))] * count
    return local_call(
        partial(query_grads_body, rows),
        (1,),
        [SCALAR, whole(grads), whole(source), whole(up)],
        [whole(s) for s in shapes],
        shapes,
        (z, grads, source, up),
        after,
    )


def latent_grads_body(z, place, source, grads, *outs):
    rows = outs[0].shape[0]
    here = grads[...]
    for s, out in enumerate(outs):
        block = 4 * lax.rem(z[0] + s, len(outs)) + place[0]
        start = pl.multiple_of(block * rows, rows)
        out[...] = mul_tn(source[:, pl.ds(start, rows)], here).astype(jnp.bfloat16)


def latent_grads_kernel(z, place, count, source, grads, rows):
    shapes = [shaped((rows, grads.shape[1]))] * count
    return local_call(
        latent_grads_body,
        (1,),
        [SCALAR, SCALAR, whole(source), whole(grads)],
        [whole(s) for s in shapes],
        shapes,
        (z, place, source, grads),
    )


def split_product_body(left, right, kept_out, sent_out):
    total = mul_nt(left[...], right[...]).astype(jnp.bfloat16)
    half = total.shape[0] // 2
    kept_out[0] = total[:half]
    sent_out[0] = total[half:]


def split_product_kernel(left, right, sequences):
    rows = left.shape[0] // sequences
    shapes = [shaped((sequences, rows // 2, right.shape[0]))] * 2
    return local_call(
        split_product_body,
        (sequences,),
        [by_rows(left, rows), whole(right)],
        [by_first(s) for s in shapes],
        shapes,
        (left, right),
    )


def core_fold_body(*refs):
    for k in range(4):
        total = refs[k][0, 0].astype(jnp.float32) + refs[4 + k][0, 0].astype(jnp.float32)
        refs[8 + k][0] = total.astype(jnp.bfloat16)


def core_fold_kernel(own, received, after=()):
    half, width = (own.shape[2] // 2, own.shape[3])
    block = (1, 1, half, width)
    specs = [
        pl.BlockSpec(block, lambda k: (0, k, 0, 0)),
        pl.BlockSpec(block, lambda k: (1, k, 0, 0)),
        pl.BlockSpec(block, lambda k: (k, 0, 1, 0)),
        pl.BlockSpec(block, lambda k: (k, 1, 1, 0)),
    ]
    shapes = [shaped((2, half, width))] * 4
    return local_call(
        core_fold_body,
        (2,),
        specs + specs,
        [by_first(s) for s in shapes],
        shapes,
        (own,) * 4 + (received,) * 4,
        after,
    )


def plane_fold_body(lower, lower_got, upper, upper_got, *outs):
    for k, (left, right) in enumerate(((lower, lower_got), (upper, upper_got))):
        for j in range(2):
            total = left[j].astype(jnp.float32) + right[j].astype(jnp.float32)
            outs[2 * k + j][...] = total.astype(jnp.bfloat16)


def plane_fold_kernel(lower, lower_got, upper, upper_got, after=()):
    _, rows, width = lower.shape
    tile = max(16, rows // 2)
    spec = pl.BlockSpec((2, tile, width), lambda i: (0, i, 0))
    shapes = [shaped((rows, width))] * 4
    return local_call(
        plane_fold_body,
        (rows // tile,),
        [spec] * 4,
        [by_rows(s, tile) for s in shapes],
        shapes,
        (lower, lower_got, upper, upper_got),
        after,
    )


def slab_fold_body(lower, lower_got, upper, upper_got, own_out, *outs):
    half = lower.shape[0]
    count = len(outs) + 1
    block = 2 * half // count
    for k, (left, right) in enumerate(((lower, lower_got), (upper, upper_got))):
        total = left[...].astype(jnp.float32) + right[...].astype(jnp.float32)
        if count == 1:
            own_out[k * half : (k + 1) * half, :] = total
            continue
        for j in range(half // block):
            here = total[j * block : (j + 1) * block]
            s = k * (half // block) + j
            if s == 0:
                own_out[...] = here
            else:
                outs[s - 1][...] = here.astype(jnp.bfloat16)


def slab_fold_kernel(lower, lower_got, upper, upper_got, count, after=()):
    half, width = lower.shape
    block = 2 * half // count
    shapes = [shaped((block, width), jnp.float32)] + [shaped((block, width))] * (count - 1)
    return local_call(
        slab_fold_body,
        (1,),
        [whole(lower)] * 4,
        [whole(s) for s in shapes],
        shapes,
        (lower, lower_got, upper, upper_got),
        after,
    )


def z_fold_body(*refs):
    total = refs[0][...].astype(jnp.float32)
    for ref in refs[1:-1]:
        total = total + ref[...].astype(jnp.float32)
    refs[-1][...] = total.astype(refs[-1].dtype)


def z_fold_kernel(parts, dtype, after=()):
    shape = shaped(parts[0].shape, dtype)
    return local_call(
        z_fold_body, (1,), [whole(p) for p in parts], whole(shape), shape, tuple(parts), after
    )


def product_nt_body(left, right, out):
    out[...] = mul_nt(left[...], right[...]).astype(jnp.bfloat16)


def product_nt_kernel(left, right, after=()):
    shape = shaped((left.shape[0], right.shape[0]))
    return local_call(
        product_nt_body,
        (left.shape[0] // TILE,),
        [by_rows(left), whole(right)],
        by_rows(shape),
        shape,
        (left, right),
        after,
    )


def join_body(*refs):
    out = refs[-1]
    rows = refs[0].shape[0]
    for s, ref in enumerate(refs[:-1]):
        out[s * rows : (s + 1) * rows, :] = ref[...]


def join_kernel(parts, after=()):
    rows, width = parts[0].shape
    shape = shaped((len(parts) * rows, width), parts[0].dtype)
    return local_call(
        join_body, (1,), [whole(p) for p in parts], whole(shape), shape, tuple(parts), after
    )


CTX = ("z", "x", "c")


def swap(value, axis):
    return lax.ppermute(value, axis, [(0, 1), (1, 0)])


def from_z(value, steps):
    count = lax.axis_size("z")
    return lax.ppermute(value, "z", [((i + steps) % count, i) for i in range(count)])


def to_z(value, steps):
    count = lax.axis_size("z")
    return lax.ppermute(value, "z", [(i, (i + steps) % count) for i in range(count)])


def trade(value, axes):
    return lax.all_to_all(value, axes, split_axis=0, concat_axis=0, tiled=True)


def add(left, right):
    return left.astype(jnp.float32) + right.astype(jnp.float32)


def low(value):
    return value.astype(jnp.bfloat16)


def dot(left, right):
    return jnp.dot(left, right, preferred_element_type=jnp.float32)


def dot_nt(left, right):
    return lax.dot_general(
        left, right, (((1,), (1,)), ((), ())), preferred_element_type=jnp.float32
    )


def dot_tn(left, right):
    return lax.dot_general(
        left, right, (((0,), (0,)), ((), ())), preferred_element_type=jnp.float32
    )


def by_own(value, axis_name, dim):
    flipped = jnp.flip(value, axis=dim)
    return jnp.where(lax.axis_index(axis_name) == 0, value, flipped)


def tie(value, *others):
    if not others:
        return value
    zero = sum(other[(0,) * other.ndim].astype(jnp.float32) for other in others) * 0.0
    return value + zero.astype(value.dtype)


def rows_first(value):
    return with_layout_constraint(value, Layout(major_to_minor=tuple(range(value.ndim))))


def put(parts, places):
    whole = jnp.zeros((len(parts),) + parts[0].shape, parts[0].dtype)
    for part, place in zip(parts, places):
        whole = lax.dynamic_update_index_in_dim(whole, part, place, 0)
    return rows_first(whole)


def z_parts(value):
    return [value] + [from_z(value, s) for s in range(1, lax.axis_size("z"))]


def put_z(parts):
    z = lax.axis_index("z")
    count = len(parts)
    return put(parts, [(z + s) % count for s in range(count)])


def gather_plane(rows, axes=("x", "y"), gates=()):
    half = rows.shape[0] // 2
    over_a = tie(swap(rows, axes[0]), *gates)
    over_b = tie(swap(rows, axes[1]), *gates)
    both = jnp.concatenate([swap(over_b[:half], axes[0]), swap(over_a[half:], axes[1])], axis=0)
    return jnp.stack([jnp.stack([rows, over_b]), jnp.stack([over_a, both])])


def fold_first(pieces, axes, after=()):
    lower, lower_sent, upper, upper_sent = pieces
    return plane_fold_kernel(
        lower, swap(lower_sent, axes[0]), upper, swap(upper_sent, axes[1]), after
    )


def fold_second(pieces, axes, count, after=()):
    lower, lower_sent, upper, upper_sent = pieces
    return slab_fold_kernel(
        lower, swap(lower_sent, axes[1]), upper, swap(upper_sent, axes[0]), count, after
    )


def fold_z(parts, dtype=jnp.float32, after=()):
    received = [to_z(part, s + 1) for s, part in enumerate(parts[1:])]
    return z_fold_kernel([parts[0]] + received, dtype, after)


def spread_z(rows):
    return jnp.concatenate(z_parts(rows), axis=0)


def both_halves(rows):
    other = swap(rows, "y")
    return by_own(jnp.stack([rows, other]), "y", 0)


def dense_shards(
    tokens,
    norm_in,
    query_weight,
    latent_down,
    latent_norm,
    latent_up,
    output_weight,
    norm_ffn,
    router_weight,
    shared_gate,
    shared_up,
    shared_down,
    expert_gate,
    expert_up,
    expert_down,
    routes,
    cotangent,
):
    zs = lax.axis_size("z")
    z, x, c = (lax.axis_index("z"), lax.axis_index("x"), lax.axis_index("c"))
    me = (z * 2 + x) * 2 + c
    sequences, block, width = tokens.shape
    count = 4 * zs
    rows_here = width // count
    slab = 4 * block
    experts = router_weight.shape[1]
    shared_here = shared_gate.shape[1] // count
    part = -(-max(shared_here, experts) // 128) * 128
    heads = latent_up.shape[1] // (4 * (DN + DV))
    query_columns = heads * (DN + DR)
    rank_rows = R // count
    head_rows = heads * DV
    scale = (DN + DR) ** (-0.5)

    latent_column = jnp.pad(latent_norm, (0, rows_here - rank_rows))[:, None]
    small = jnp.concatenate(
        [
            latent_down,
            router_weight,
            norm_in[:, None],
            norm_ffn[:, None],
            latent_column,
            routes.reshape(sequences * block, TOPK).astype(jnp.bfloat16),
        ],
        axis=1,
    )
    small = put_z(z_parts(jnp.pad(small, ((0, 0), (0, -small.shape[1] % 128)))))
    at = R + DR
    down_here = small[:, :, :at]
    rest = small[:, :, at:]
    down_here = down_here.reshape(-1, R + DR)
    down_x = swap(down_here, "x")
    down_pieces = (down_here, down_x, swap(down_here, "c"), swap(down_x, "c"))
    own_gain = rest[:, :, experts].reshape(1, zs * rows_here).astype(jnp.float32)
    rest = jnp.stack([rest, swap(rest, "x")], axis=1)
    rest = jnp.stack([rest, swap(rest, "c")], axis=2)
    rest = by_own(by_own(rest, "x", 1), "c", 2).reshape(count, rows_here, -1)
    full_router = rest[:, :, :experts].reshape(width, experts)
    full_norm_in = rest[:, :, experts].reshape(width).astype(jnp.float32)
    full_norm_ffn = rest[:, :, experts + 1].reshape(width).astype(jnp.float32)
    full_latent_norm = rest[:, :rank_rows, experts + 2].reshape(R).astype(jnp.float32)
    all_routes = rest[:, :, experts + 3 : experts + 3 + TOPK]

    up_columns = heads * (DN + DV)
    up_part = jnp.transpose(
        latent_up.reshape(rank_rows, 4, up_columns // 128, 128), (1, 2, 0, 3)
    ).reshape(4, rows_here, 128)
    out_part = jnp.transpose(output_weight.reshape(4, heads, DV, rows_here), (0, 2, 1, 3)).reshape(
        4, DV, heads * rows_here
    )
    by_heads = query_weight.reshape(rows_here, 4, heads, DN + DR)
    by_heads = jnp.concatenate(
        [
            by_heads[..., :DN].reshape(rows_here, 4, heads * DN),
            by_heads[..., DN:].reshape(rows_here, 4, heads * DR),
        ],
        axis=2,
    )
    by_heads = jnp.transpose(by_heads, (1, 0, 2))
    by_heads = jnp.concatenate([by_heads, up_part, out_part], axis=2)
    mine_at = 2 * x + c
    for_group = [
        lax.dynamic_index_in_dim(by_heads, mine_at ^ k, 0, keepdims=False) for k in range(4)
    ]
    by_heads = put(
        [
            for_group[0],
            swap(for_group[1], "c"),
            swap(for_group[2], "x"),
            lax.ppermute(for_group[3], ("x", "c"), [(k, 3 - k) for k in range(4)]),
        ],
        [mine_at ^ k for k in range(4)],
    )
    mine = by_own(tokens, "y", 0)
    line = jnp.stack([mine, swap(mine, "x")], axis=1)
    line = jnp.stack([line, swap(line, "c")], axis=1)
    source = line.reshape(sequences * slab, width).astype(jnp.float32)
    grad_mine = by_own(cotangent, "y", 0)[0]
    grad_parts = z_parts(grad_mine)
    gate_t, up_t, down = (expert_gate[0].T, expert_up[0].T, expert_down[0])
    shared_mine = jnp.concatenate(
        [
            shared_gate.T.reshape(count, shared_here, rows_here),
            shared_up.T.reshape(count, shared_here, rows_here),
            shared_down.reshape(count, shared_here, rows_here),
        ],
        axis=1,
    )
    shared_rows = trade(shared_mine, CTX)
    shared_rows = jnp.transpose(shared_rows, (1, 0, 2)).reshape(3, shared_here, width)
    shared_rows = jnp.pad(shared_rows, ((0, 0), (0, part - shared_here), (0, 0)))
    small_t = jnp.concatenate(
        [
            shared_rows[0],
            shared_rows[1],
            jnp.pad(full_router.T, ((0, part - experts), (0, 0))),
        ]
    )
    shared_down_t = shared_rows[2]

    query_here, up_here, out_here = heads_kernel(
        lax.all_gather(by_heads, "z", axis=0),
        query_columns,
        heads,
        up_columns,
    )

    def places(turns):
        two = jnp.arange(2)
        base = (
            ((z + turns[None, None, :]) % zs) * 4
            + (x ^ two[None, :, None]) * 2
            + (c ^ two[:, None, None])
        )
        return (base[..., None] * block + jnp.arange(block)).reshape(-1)

    positions = places(jnp.arange(1))
    key_positions = places(jnp.arange(zs))
    cosine, sine = rotary_tables(positions, DR)
    normed, unit_in, inverse_in = root_norm(source, full_norm_in)
    input_low = low(normed)

    own_rows = line[0].reshape(slab, width)
    own_columns = jnp.concatenate(
        [
            lax.dynamic_slice_in_dim(own_rows, (4 * k + 2 * x + c) * rows_here, rows_here, 1)
            for k in range(zs)
        ],
        axis=1,
    ).astype(jnp.float32)
    latent_part = dot(
        low(own_columns * inverse_in[:slab] * own_gain), down_here
    )
    latent_part = low(latent_part).reshape(2, 2, block, R + DR)
    latent_part = low(add(latent_part[0], swap(latent_part[1], "c")))
    latent_raw = add(latent_part[0], swap(latent_part[1], "x"))
    latent_scaled, latent_unit, latent_inverse = root_norm(latent_raw[:, :R], full_latent_norm)
    key_own = low(
        jnp.concatenate(
            [latent_scaled, rotate(latent_raw[:, R:], cosine[:block], sine[:block])], axis=-1
        )
    )
    plane = gather_plane(spread_z(key_own), ("y", "x"))
    keys_own, keys_other = (plane, swap(plane, "c"))
    grads_own = gather_plane(jnp.concatenate(grad_parts), gates=(plane,))
    grads_other = swap(grads_own, "c").reshape(-1, width)
    grads_own = grads_own.reshape(-1, width)
    query = dot(input_low, query_here)
    rope = query[:, heads * DN :].reshape(sequences, slab, heads, DR)
    rope = rotate(rope, cosine[:, None, :], sine[:, None, :]).reshape(sequences * slab, -1)
    query_low = low(jnp.concatenate([query[:, : heads * DN], rope], axis=1))

    def scatter_slab(kept, sent):
        shape = (2, 2, block, width)
        pieces = core_fold_kernel(kept.reshape(shape), swap(sent, "c").reshape(shape))
        return fold_second(fold_first(pieces, ("y", "x")), ("y", "x"), 1)[0]

    def gather_slab(rows):
        plane = gather_plane(rows, ("y", "x"))
        return jnp.stack([plane, swap(plane, "c")], axis=1).reshape(sequences * slab, -1)

    kept, sent, prob, absorbed, latent_out, head_out = attend_kernel(
        query_low,
        keys_own,
        keys_other,
        up_here,
        out_here,
        positions[:, None],
        key_positions[None, :],
        heads,
        scale,
        down_pieces[1:],
    )
    attention = scatter_slab(kept, sent)
    hidden_in = mine[0].astype(jnp.float32) + attention
    normed_ffn, unit_ffn, inverse_ffn = root_norm(hidden_in, full_norm_ffn)
    ffn_low = low(normed_ffn)
    shares = jax.nn.softmax(dot(ffn_low, full_router), axis=-1)
    ffn_parts = z_parts(ffn_low)
    back_own = product_nt_kernel(grads_own, down, (ffn_low,))
    back_other = product_nt_kernel(grads_other, down, (back_own,))
    shared_own = product_nt_kernel(grads_own, shared_down_t, (back_other,))
    shared_other = product_nt_kernel(grads_other, shared_down_t, (shared_own,))
    ffn_slabs = join_kernel(ffn_parts, (shared_other,))
    ffn_own = gather_plane(ffn_slabs)
    ffn_other = swap(ffn_own, "c").reshape(-1, width)
    ffn_own = ffn_own.reshape(-1, width)

    relative = all_routes.reshape(zs, 2, 2, sequences, block, TOPK)
    relative = by_own(by_own(by_own(relative, "x", 1), "c", 2), "y", 3)
    relative = jnp.roll(relative, -z, axis=0)
    routed = jnp.any(relative == me.astype(jnp.bfloat16), axis=-1)
    routed = jnp.transpose(routed, (2, 1, 3, 0, 4)).reshape(2, -1, 1).astype(jnp.float32)
    pick = (jnp.arange(part)[None, :] == me).astype(jnp.float32)

    def feed(rows, back, shared_back, named):
        return feed_kernel(rows, back, shared_back, gate_t, up_t, small_t, named, pick, experts)

    act_own, more_own, gate_own, up_own, pre_own, gain_own = feed(
        ffn_own, back_own, shared_own, routed[0]
    )
    act_other, more_other, gate_other, up_other, pre_other, gain_other = feed(
        ffn_other, back_other, shared_other, routed[1]
    )
    shape = (2, 2, zs * block, width + part)
    grad_other = input_kernel(
        gate_other, up_other, pre_other, gate_t, up_t, small_t, gain_other, pick
    )
    grad_own = input_kernel(
        gate_own, up_own, pre_own, gate_t, up_t, small_t, gain_own, pick, (grad_other,)
    )
    pieces = core_fold_kernel(grad_own.reshape(shape), swap(grad_other, "c").reshape(shape))
    both_axes = ("x", "y")
    sum_other = result_kernel(act_other, more_other, down, shared_down_t, pieces)
    sum_own = result_kernel(act_own, more_own, down, shared_down_t, (sum_other,))
    grad_expert_up, shared_up_back = weight_kernel(
        (up_own, up_other), (pre_own, pre_other), (ffn_own, ffn_other), 1, part, (sum_own,)
    )
    pieces = fold_first(pieces, both_axes, (grad_expert_up,))
    shape = (2, 2, zs * block, width)
    grad_expert_down, shared_down_back = weight_kernel(
        (act_own, act_other), (more_own, more_other), (grads_own, grads_other), 0, part, pieces
    )
    grad_slab = fold_second(pieces, both_axes, zs, (grad_expert_down,))
    routed_pieces = core_fold_kernel(
        sum_own.reshape(shape), swap(sum_other, "c").reshape(shape), grad_slab
    )
    grad_expert_gate, shared_gate_back = weight_kernel(
        (gate_own, gate_other),
        (pre_own, pre_other),
        (ffn_own, ffn_other),
        0,
        part,
        tuple(routed_pieces),
    )
    routed_pieces = fold_first(routed_pieces, both_axes, (grad_expert_gate,))
    ffn_grad = fold_z(grad_slab, jnp.float32, routed_pieces)
    share_grad = ffn_grad[:, width : width + experts]
    ffn_grad = ffn_grad[:, :width]
    logit_grad = shares * (share_grad - jnp.sum(shares * share_grad, axis=-1, keepdims=True))
    ffn_grad = ffn_grad + dot_nt(low(logit_grad), full_router)
    grad_router = dot_tn(ffn_low, low(logit_grad))
    hidden_part, grad_norm_ffn = root_norm_back(ffn_grad, unit_ffn, inverse_ffn, full_norm_ffn)
    grad_hidden = grad_mine.astype(jnp.float32) + hidden_part

    hidden_low = low(grad_hidden)
    attention_grad = gather_slab(hidden_low)
    shared_back = jnp.concatenate(
        [
            shared_gate_back[:shared_here],
            shared_up_back[:shared_here],
            shared_down_back[:shared_here],
        ]
    )
    shared_back = trade(
        jnp.transpose(shared_back.reshape(-1, count, rows_here), (1, 0, 2)), CTX
    )
    zero = jnp.zeros((1,), jnp.int32)
    (out_grads,) = out_grads_kernel(zero, 1, head_out, attention_grad, rows_here)
    grad_out = lax.psum_scatter(out_grads, "z", scatter_dimension=0, tiled=True)
    key_own, key_other, query_grad, grad_up_here = attend_back_kernel(
        attention_grad,
        query_low,
        keys_own,
        keys_other,
        up_here,
        out_here,
        prob,
        absorbed,
        latent_out,
        heads,
        scale,
        (out_grads,),
    )
    shape = (2, 2, zs * block, R + DR)
    routed_slab = fold_second(routed_pieces, both_axes, zs, (key_own,))
    key_pieces = core_fold_kernel(key_own, swap(key_other, "c"), routed_slab)
    key_slab = fold_second(fold_first(key_pieces, ("y", "x")), ("y", "x"), zs)
    key_sum = fold_z(key_slab)
    rope = query_grad[:, heads * DN :].reshape(sequences, slab, heads, DR)
    rope = rotate(rope, cosine[:, None, :], -sine[:, None, :]).reshape(sequences * slab, -1)
    query_raw_grad = low(jnp.concatenate([query_grad[:, : heads * DN], rope], axis=1))
    input_grad = scatter_slab(*split_product_kernel(query_raw_grad, query_here, sequences))
    (query_grads,) = query_grads_kernel(
        zero, 1, query_raw_grad, input_low, grad_up_here, rows_here
    )
    grad_heads = lax.psum_scatter(query_grads, "z", scatter_dimension=0, tiled=True)
    output = both_halves(low(hidden_in + fold_z(routed_slab, jnp.float32, (key_sum,))))
    shared_back = tie(shared_back, key_sum).astype(jnp.float32)
    grad_shared_gate = shared_back[:, :shared_here].reshape(-1, rows_here).T
    grad_shared_up = shared_back[:, shared_here : 2 * shared_here].reshape(-1, rows_here).T
    grad_shared_down = shared_back[:, 2 * shared_here :].reshape(-1, rows_here)


    latent_back, grad_latent_norm = root_norm_back(
        key_sum[:, :R], latent_unit, latent_inverse, full_latent_norm
    )
    rope_key = rotate(key_sum[:, R:], cosine[:block], -sine[:block])
    latent_raw_grad = low(jnp.concatenate([latent_back, rope_key], axis=-1))
    slab_latent_grad = gather_slab(latent_raw_grad)
    down_grads = latent_grads_kernel(
        z[None], (2 * x + c)[None], zs, input_low, slab_latent_grad, rows_here
    )
    grad_down = fold_z(down_grads)
    latent_raw_grad = tie(latent_raw_grad, down_grads[0])
    latent_input = jnp.stack([dot_nt(latent_raw_grad, down) for down in down_pieces])
    latent_input = latent_input.reshape(2, 2, block, zs, rows_here)
    latent_input = by_own(by_own(latent_input, "c", 0), "x", 1)
    input_grad = input_grad + jnp.transpose(latent_input, (2, 3, 1, 0, 4)).reshape(block, width)
    source_part, grad_norm_in = root_norm_back(
        input_grad, unit_in[:block], inverse_in[:block], full_norm_in
    )
    tokens_gradient = both_halves(low(grad_hidden + source_part)).astype(jnp.float32)

    both = trade(jnp.concatenate([grad_heads, grad_out], axis=2), ("x", "c")).astype(jnp.float32)
    out_at = both.shape[2] - head_rows
    grad_output = jnp.transpose(
        both[..., out_at:].reshape(4, DV, heads, rows_here), (0, 2, 1, 3)
    ).reshape(-1, rows_here)
    grad_query = jnp.transpose(both[..., :query_columns], (1, 0, 2))
    grad_query = jnp.concatenate(
        [
            grad_query[..., : heads * DN].reshape(rows_here, 4, heads, DN),
            grad_query[..., heads * DN :].reshape(rows_here, 4, heads, DR),
        ],
        axis=-1,
    ).reshape(rows_here, -1)
    grad_latent_up = jnp.transpose(
        both[..., query_columns:out_at].reshape(4, up_columns // 128, rank_rows, 128), (2, 0, 1, 3)
    ).reshape(rank_rows, -1)

    small_grads = jnp.concatenate(
        [
            grad_router.T.reshape(experts, count, rows_here),
            grad_norm_in.reshape(1, count, rows_here),
            grad_norm_ffn.reshape(1, count, rows_here),
            jnp.pad(
                grad_latent_norm.reshape(1, count, rank_rows),
                ((0, 0), (0, 0), (0, rows_here - rank_rows)),
            ),
        ]
    )
    small_grads = trade(jnp.transpose(small_grads, (1, 0, 2)), CTX)
    small_grads = jnp.sum(small_grads, axis=0)
    small_grads = small_grads + swap(small_grads, "y")
    return (
        output,
        tokens_gradient,
        small_grads[experts],
        grad_query,
        grad_down,
        small_grads[experts + 2, :rank_rows],
        grad_latent_up,
        grad_output,
        small_grads[experts + 1],
        small_grads[:experts].T,
        grad_shared_gate,
        grad_shared_up,
        grad_shared_down,
        grad_expert_gate.T[None],
        grad_expert_up.T[None],
        grad_expert_down[None],
    )


IN_SPECS = (
    (None, "ctx", None),
    ("ctx",),
    ("ctx", "wa"),
    ("ctx", None),
    ("ctx",),
    ("ctx", "wa"),
    ("wa", "ctx"),
    ("ctx",),
    ("ctx", None),
    ("ctx", "wa"),
    ("ctx", "wa"),
    ("wa", "ctx"),
    ("ctx", None, "wa"),
    ("ctx", None, "wa"),
    ("ctx", "wa", None),
    (None, "ctx", None),
    (None, "ctx", None),
)
OUT_SPECS = ((None, "ctx", None),) * 2 + IN_SPECS[1:15]


def solution(mesh):
    count = mesh.shape["ctx"]

    def run(*arguments):
        experts = arguments[12].shape[0]
        if experts > 4 * TOPK or experts != count or mesh.shape["wa"] != 2 or count % 8:
            return jax.shard_map(
                shards,
                mesh=mesh,
                in_specs=tuple(P(*spec) for spec in IN_SPECS),
                out_specs=tuple(P(*spec) for spec in OUT_SPECS),
                check_vma=False,
            )(*arguments)
        grid = Mesh(mesh.devices.reshape(count // 4, 2, 2, 2), ("z", "x", "c", "y"))
        names = {"ctx": CTX, "wa": "y", None: None}
        return jax.shard_map(
            dense_shards,
            mesh=grid,
            in_specs=tuple(P(*[names[n] for n in spec]) for spec in IN_SPECS),
            out_specs=tuple(P(*[names[n] for n in spec]) for spec in OUT_SPECS),
            check_vma=False,
        )(*arguments)

    return run
```

```python
from functools import partial

import jax
import jax.numpy as jnp
from jax import lax
from jax.experimental import pallas as pl
from jax.experimental.layout import Layout, with_layout_constraint
from jax.experimental.pallas import tpu as pltpu
from jax.sharding import Mesh, PartitionSpec as P

DN = 128
DR = 64
DV = 128
R = 512
TOPK = 6


epsilon = 1e-06
highest = lax.Precision.HIGHEST


def shifted(value, axis, steps):
    count = lax.axis_size(axis)
    pairs = [(source, (source + steps) % count) for source in range(count)]
    return lax.ppermute(value, axis, pairs)


def root_norm(values, gain):
    inverse = lax.rsqrt(jnp.mean(values * values, axis=-1, keepdims=True) + epsilon)
    unit = values * inverse
    return (unit * gain, unit, inverse)


def root_norm_back(upstream, unit, inverse, gain):
    scaled = upstream * gain
    inner = jnp.mean(scaled * unit, axis=-1, keepdims=True)
    leading = tuple(range(upstream.ndim - 1))
    return (inverse * (scaled - unit * inner), jnp.sum(upstream * unit, axis=leading))


def rotary_tables(positions, width):
    half = width // 2
    frequency = 10000.0 ** (-jnp.arange(half, dtype=jnp.float32) * 2.0 / width)
    angle = positions.astype(jnp.float32)[:, None] * frequency[None, :]
    return (jnp.cos(angle), jnp.sin(angle))


def rotate(values, cosine, sine):
    half = values.shape[-1] // 2
    first = values[..., :half]
    second = values[..., half:]
    return jnp.concatenate(
        [first * cosine - second * sine, second * cosine + first * sine], axis=-1
    )


def silu_slope(values):
    sigmoid = jax.nn.sigmoid(values)
    return sigmoid * (1.0 + values * (1.0 - sigmoid))


def fetch_weights(
    norm_in,
    query_weight,
    latent_down,
    latent_norm,
    latent_up,
    output_weight,
    norm_ffn,
    router_weight,
    shared_gate,
    shared_up,
    shared_down,
):
    return (
        lax.all_gather(norm_in, "ctx", axis=0, tiled=True),
        lax.all_gather(query_weight, "ctx", axis=0, tiled=True),
        lax.all_gather(latent_down, "ctx", axis=0, tiled=True),
        lax.all_gather(latent_norm, "ctx", axis=0, tiled=True),
        lax.all_gather(latent_up, "ctx", axis=0, tiled=True),
        lax.all_gather(output_weight, "ctx", axis=1, tiled=True),
        lax.all_gather(norm_ffn, "ctx", axis=0, tiled=True),
        lax.all_gather(router_weight, "ctx", axis=0, tiled=True),
        lax.all_gather(shared_gate, "ctx", axis=0, tiled=True),
        lax.all_gather(shared_up, "ctx", axis=0, tiled=True),
        lax.all_gather(shared_down, "ctx", axis=1, tiled=True),
    )


def shards(
    tokens,
    norm_in,
    query_weight,
    latent_down,
    latent_norm,
    latent_up,
    output_weight,
    norm_ffn,
    router_weight,
    shared_gate,
    shared_up,
    shared_down,
    expert_gate,
    expert_up,
    expert_down,
    routes,
    cotangent,
):
    context_count = lax.axis_size("ctx")
    context_index = lax.axis_index("ctx")
    lead = (lax.axis_index("wa") == 0).astype(jnp.float32)
    sequences, block, width = tokens.shape
    local_experts = expert_gate.shape[0]
    experts = context_count * local_experts
    capacity = max(2, block * TOPK * 4 // (3 * experts))
    scale = (DN + DR) ** (-0.5)
    gathered = fetch_weights(
        norm_in,
        query_weight,
        latent_down,
        latent_norm,
        latent_up,
        output_weight,
        norm_ffn,
        router_weight,
        shared_gate,
        shared_up,
        shared_down,
    )
    (
        full_norm_in,
        full_query,
        full_down,
        full_latent_norm,
        full_up,
        full_output,
        full_norm_ffn,
        full_router,
        full_shared_gate,
        full_shared_up,
        full_shared_down,
    ) = gathered
    heads_here = full_up.shape[1] // (DN + DV)
    positions = context_index * block + jnp.arange(block)
    cosine, sine = rotary_tables(positions, DR)
    source = tokens.astype(jnp.float32)
    normed_in, unit_in, inverse_in = root_norm(source, full_norm_in.astype(jnp.float32))
    input_low = normed_in.astype(jnp.bfloat16)
    query_raw = jnp.dot(input_low, full_query, preferred_element_type=jnp.float32).reshape(
        sequences, block, heads_here, DN + DR
    )
    query_low = jnp.concatenate(
        [query_raw[..., :DN], rotate(query_raw[..., DN:], cosine[:, None, :], sine[:, None, :])],
        axis=-1,
    ).astype(jnp.bfloat16)
    up_view = full_up.reshape(R, heads_here, DN + DV)
    key_up = up_view[..., :DN]
    value_up = up_view[..., DN:]
    absorbed = jnp.einsum(
        "sbhn,rhn->shbr", query_low[..., :DN], key_up, preferred_element_type=jnp.float32
    )
    query_rows = jnp.concatenate(
        [absorbed.astype(jnp.bfloat16), jnp.transpose(query_low[..., DN:], (0, 2, 1, 3))], axis=-1
    )
    latent_raw = jnp.dot(input_low, full_down, preferred_element_type=jnp.float32)
    latent_scaled, latent_unit, latent_inverse = root_norm(
        latent_raw[..., :R], full_latent_norm.astype(jnp.float32)
    )
    key_rows = jnp.concatenate(
        [latent_scaled, rotate(latent_raw[..., R:], cosine, sine)], axis=-1
    ).astype(jnp.bfloat16)
    piece = lax.all_gather(key_rows, "ctx", axis=1, tiled=True)
    top = jnp.full((sequences, heads_here, block), -1e30, jnp.float32)
    scores = (
        jnp.einsum("shqc,skc->shqk", query_rows, piece, preferred_element_type=jnp.float32) * scale
    )
    key_positions = jnp.arange(piece.shape[1])
    allowed = positions[:, None] >= key_positions[None, :]
    scores = jnp.where(allowed, scores, -1e30)
    new_top = jnp.maximum(top, jnp.max(scores, axis=-1))
    weights = jnp.where(allowed, jnp.exp(scores - new_top[..., None]), 0.0)
    total = jnp.sum(weights, axis=-1)
    weights_high = weights.astype(jnp.bfloat16)
    weights_rest = (weights - weights_high.astype(jnp.float32)).astype(jnp.bfloat16)
    running = jnp.einsum(
        "shqk,skr->shqr", weights_high, piece[..., :R], preferred_element_type=jnp.float32
    )
    remainder = jnp.einsum(
        "shqk,skr->shqr", weights_rest, piece[..., :R], preferred_element_type=jnp.float32
    )
    top, total, running, remainder = (new_top, total, running, remainder)
    log_total = top + jnp.log(total)
    latent_out = (running / total[..., None]).astype(jnp.bfloat16)
    latent_exact = (running + remainder) / total[..., None]
    head_out = (
        jnp.einsum("shbr,rhv->sbhv", latent_out, value_up, preferred_element_type=jnp.float32)
        .astype(jnp.bfloat16)
        .reshape(sequences, block, heads_here * DV)
    )
    attention_part = jnp.dot(head_out, full_output, preferred_element_type=jnp.float32)
    hidden_in = source + lax.psum(attention_part, "wa")
    normed_ffn, unit_ffn, inverse_ffn = root_norm(hidden_in, full_norm_ffn.astype(jnp.float32))
    ffn_low = normed_ffn.astype(jnp.bfloat16)
    shares = jax.nn.softmax(
        jnp.dot(ffn_low, full_router, preferred_element_type=jnp.float32), axis=-1
    )
    shared_g = jnp.dot(ffn_low, full_shared_gate, preferred_element_type=jnp.float32)
    shared_u = jnp.dot(ffn_low, full_shared_up, preferred_element_type=jnp.float32)
    shared_silu = jax.nn.silu(shared_g)
    shared_activation = (shared_silu * shared_u).astype(jnp.bfloat16)
    shared_part = jnp.dot(shared_activation, full_shared_down, preferred_element_type=jnp.float32)
    expert_ids = jnp.arange(experts, dtype=jnp.int32)
    chosen = (
        (routes[..., None] == expert_ids)
        .astype(jnp.int32)
        .reshape(sequences, block * TOPK, experts)
    )
    earlier = jnp.cumsum(chosen, axis=1) - chosen
    slot_of = jnp.sum(earlier * chosen, axis=-1).reshape(sequences, block, TOPK)
    slot_ids = jnp.arange(capacity, dtype=jnp.int32)
    hit = (routes[None, :, :, :, None] == expert_ids[:, None, None, None, None]) & (
        slot_of[None, :, :, :, None] == slot_ids[None, None, None, None, :]
    )
    dispatch = jnp.transpose(jnp.any(hit, axis=3), (0, 1, 3, 2)).astype(jnp.float32)
    send = (
        jnp.einsum(
            "escb,sbd->escd",
            dispatch.astype(jnp.bfloat16),
            ffn_low,
            preferred_element_type=jnp.float32,
        )
        .astype(jnp.bfloat16)
        .reshape(experts, sequences * capacity, width)
    )
    slot_share = jnp.einsum("escb,sbe->esc", dispatch, shares, precision=highest)
    received = lax.all_to_all(send, "ctx", split_axis=0, concat_axis=0, tiled=True)
    count = received.shape[1]
    rows = received.reshape(context_count, local_experts, count, width)
    gate_pre = jnp.einsum("nesd,edf->nesf", rows, expert_gate, preferred_element_type=jnp.float32)
    up_pre = jnp.einsum("nesd,edf->nesf", rows, expert_up, preferred_element_type=jnp.float32)
    activation = (jax.nn.silu(gate_pre) * up_pre).astype(jnp.bfloat16)
    result = jnp.einsum(
        "nesf,efd->nesd", activation, expert_down, preferred_element_type=jnp.float32
    ).reshape(experts, count, width)
    returned = lax.all_to_all(result, "ctx", split_axis=0, concat_axis=0, tiled=True)
    hidden_units = gate_pre.shape[-1]
    returned, received, gate_keep, up_keep = (
        returned,
        received,
        gate_pre.reshape(experts, count, hidden_units),
        up_pre.reshape(experts, count, hidden_units),
    )
    returned = returned.reshape(experts, sequences, capacity, width)
    routed_part = jnp.einsum(
        "escb,escd->sbd", dispatch, returned * slot_share[..., None], precision=highest
    )
    output = hidden_in + lax.psum(shared_part + routed_part, "wa")
    gathered = fetch_weights(
        norm_in,
        query_weight,
        latent_down,
        latent_norm,
        latent_up,
        output_weight,
        norm_ffn,
        router_weight,
        shared_gate,
        shared_up,
        shared_down,
    )
    (
        full_norm_in,
        full_query,
        full_down,
        full_latent_norm,
        full_up,
        full_output,
        full_norm_ffn,
        full_router,
        full_shared_gate,
        full_shared_up,
        full_shared_down,
    ) = gathered
    up_view = full_up.reshape(R, heads_here, DN + DV)
    key_up = up_view[..., :DN]
    value_up = up_view[..., DN:]
    grad_y = cotangent.astype(jnp.float32)
    shared_grad = jnp.einsum(
        "sbd,fd->sbf", cotangent, full_shared_down, preferred_element_type=jnp.float32
    )
    shared_gate_grad = (shared_grad * shared_u * silu_slope(shared_g)).astype(jnp.bfloat16)
    shared_up_grad = (shared_grad * shared_silu).astype(jnp.bfloat16)
    grad_shared_down = jnp.einsum(
        "sbf,sbd->fd", shared_activation, cotangent, preferred_element_type=jnp.float32
    )
    grad_shared_gate = jnp.einsum(
        "sbd,sbf->df", ffn_low, shared_gate_grad, preferred_element_type=jnp.float32
    )
    grad_shared_up = jnp.einsum(
        "sbd,sbf->df", ffn_low, shared_up_grad, preferred_element_type=jnp.float32
    )
    ffn_grad = jnp.einsum(
        "sbf,df->sbd", shared_gate_grad, full_shared_gate, preferred_element_type=jnp.float32
    )
    ffn_grad = ffn_grad + jnp.einsum(
        "sbf,df->sbd", shared_up_grad, full_shared_up, preferred_element_type=jnp.float32
    )
    grad_at_slots = jnp.einsum("escb,sbd->escd", dispatch, grad_y, precision=highest)
    slot_grads = (
        (grad_at_slots * slot_share[..., None])
        .astype(jnp.bfloat16)
        .reshape(experts, sequences * capacity, width)
    )
    slot_dot = jnp.sum(returned * grad_at_slots, axis=-1)
    share_grad = jnp.einsum("escb,esc->sbe", dispatch, slot_dot, precision=highest)
    logit_grad = shares * (share_grad - jnp.sum(shares * share_grad, axis=-1, keepdims=True))
    grad_router = jnp.einsum(
        "sbd,sbe->de", ffn_low.astype(jnp.float32), logit_grad, precision=highest
    )
    ffn_grad = ffn_grad + jnp.einsum(
        "sbe,de->sbd", logit_grad, full_router.astype(jnp.float32), precision=highest
    )
    slot_back = lax.all_to_all(slot_grads, "ctx", split_axis=0, concat_axis=0, tiled=True).reshape(
        context_count, local_experts, -1, width
    )
    rows = received.reshape(context_count, local_experts, -1, width)
    gate_pre = gate_keep.reshape(context_count, local_experts, -1, gate_keep.shape[-1])
    up_pre = up_keep.reshape(context_count, local_experts, -1, up_keep.shape[-1])
    hidden_grad = jnp.einsum(
        "nesd,efd->nesf", slot_back, expert_down, preferred_element_type=jnp.float32
    )
    silu_gate = jax.nn.silu(gate_pre)
    gate_grad = (hidden_grad * up_pre * silu_slope(gate_pre)).astype(jnp.bfloat16)
    up_grad = (hidden_grad * silu_gate).astype(jnp.bfloat16)
    activation = (silu_gate * up_pre).astype(jnp.bfloat16)
    grad_expert_down = jnp.einsum(
        "nesf,nesd->efd", activation, slot_back, preferred_element_type=jnp.float32
    )
    grad_expert_gate = jnp.einsum(
        "nesd,nesf->edf", rows, gate_grad, preferred_element_type=jnp.float32
    )
    grad_expert_up = jnp.einsum("nesd,nesf->edf", rows, up_grad, preferred_element_type=jnp.float32)
    rows_grad = jnp.einsum(
        "nesf,edf->nesd", gate_grad, expert_gate, preferred_element_type=jnp.float32
    )
    rows_grad = rows_grad + jnp.einsum(
        "nesf,edf->nesd", up_grad, expert_up, preferred_element_type=jnp.float32
    )
    slot_grad = lax.all_to_all(
        rows_grad.reshape(experts, -1, width), "ctx", split_axis=0, concat_axis=0, tiled=True
    ).reshape(experts, sequences, capacity, width)
    ffn_grad = ffn_grad + jnp.einsum("escb,escd->sbd", dispatch, slot_grad, precision=highest)
    hidden_part, grad_norm_ffn = root_norm_back(
        ffn_grad, unit_ffn, inverse_ffn, full_norm_ffn.astype(jnp.float32)
    )
    grad_hidden = grad_y + lax.psum(hidden_part, "wa")
    attention_grad = grad_hidden.astype(jnp.bfloat16)
    grad_output = jnp.einsum(
        "sbk,sbd->kd", head_out, attention_grad, preferred_element_type=jnp.float32
    )
    head_grad = (
        jnp.einsum("sbd,kd->sbk", attention_grad, full_output, preferred_element_type=jnp.float32)
        .astype(jnp.bfloat16)
        .reshape(sequences, block, heads_here, DV)
    )
    grad_value_up = jnp.einsum(
        "shbr,sbhv->rhv", latent_out, head_grad, preferred_element_type=jnp.float32
    )
    latent_out_grad = jnp.einsum(
        "sbhv,rhv->shbr", head_grad, value_up, preferred_element_type=jnp.float32
    ).astype(jnp.bfloat16)
    row_dot = jnp.sum(latent_out_grad.astype(jnp.float32) * latent_exact, axis=-1)

    def turn_body(turn, carry):
        keys_here, key_grad, query_grad = carry
        source_index = (context_index + turn) % context_count
        key_positions = source_index * block + jnp.arange(block)
        allowed = positions[:, None] >= key_positions[None, :]
        scores = (
            jnp.einsum("shqc,skc->shqk", query_rows, keys_here, preferred_element_type=jnp.float32)
            * scale
        )
        weights = jnp.where(allowed[None, None], jnp.exp(scores - log_total[..., None]), 0.0)
        weight_grad = jnp.einsum(
            "shqr,skr->shqk",
            latent_out_grad,
            keys_here[..., :R],
            preferred_element_type=jnp.float32,
        )
        score_grad = (weights * (weight_grad - row_dot[..., None])).astype(jnp.bfloat16)
        query_grad = (
            query_grad
            + jnp.einsum(
                "shqk,skc->shqc", score_grad, keys_here, preferred_element_type=jnp.float32
            )
            * scale
        )
        key_part = (
            jnp.einsum("shqk,shqc->skc", score_grad, query_rows, preferred_element_type=jnp.float32)
            * scale
        )
        value_part = jnp.einsum(
            "shqk,shqr->skr",
            weights.astype(jnp.bfloat16),
            latent_out_grad,
            preferred_element_type=jnp.float32,
        )
        key_grad = key_grad + key_part + jnp.pad(value_part, ((0, 0), (0, 0), (0, DR)))
        keys_next = shifted(keys_here, "ctx", -1)
        grad_next = shifted(key_grad, "ctx", -1)
        return (keys_next, grad_next, query_grad)

    start_back = (
        key_rows,
        jnp.zeros((sequences, block, R + DR), jnp.float32),
        jnp.zeros((sequences, heads_here, block, R + DR), jnp.float32),
    )
    unused_keys, key_grad, query_grad = lax.fori_loop(0, context_count, turn_body, start_back)
    key_grad_total = lax.psum(key_grad, "wa")
    query_grad_low = query_grad.astype(jnp.bfloat16)
    absorbed_grad = query_grad_low[..., :R]
    rope_query_grad = jnp.transpose(query_grad_low[..., R:], (0, 2, 1, 3)).astype(jnp.float32)
    grad_key_up = jnp.einsum(
        "shbr,sbhn->rhn", absorbed_grad, query_low[..., :DN], preferred_element_type=jnp.float32
    )
    nope_grad = jnp.einsum(
        "shbr,rhn->sbhn", absorbed_grad, key_up, preferred_element_type=jnp.float32
    )
    rope_raw_grad = rotate(rope_query_grad, cosine[:, None, :], -sine[:, None, :])
    query_raw_grad = (
        jnp.concatenate([nope_grad, rope_raw_grad], axis=-1)
        .astype(jnp.bfloat16)
        .reshape(sequences, block, heads_here * (DN + DR))
    )
    grad_query = jnp.einsum(
        "sbd,sbk->dk", input_low, query_raw_grad, preferred_element_type=jnp.float32
    )
    input_part = jnp.einsum(
        "sbk,dk->sbd", query_raw_grad, full_query, preferred_element_type=jnp.float32
    )
    grad_latent_up = jnp.concatenate([grad_key_up, grad_value_up], axis=-1).reshape(
        R, heads_here * (DN + DV)
    )
    latent_grad, grad_latent_norm = root_norm_back(
        key_grad_total[..., :R], latent_unit, latent_inverse, full_latent_norm.astype(jnp.float32)
    )
    rope_key_grad = rotate(key_grad_total[..., R:], cosine, -sine)
    latent_raw_grad = jnp.concatenate([latent_grad, rope_key_grad], axis=-1).astype(jnp.bfloat16)
    grad_down = jnp.einsum(
        "sbd,sbc->dc", input_low, latent_raw_grad, preferred_element_type=jnp.float32
    )
    input_part = input_part + lead * jnp.einsum(
        "sbc,dc->sbd", latent_raw_grad, full_down, preferred_element_type=jnp.float32
    )
    source_part, grad_norm_in = root_norm_back(
        input_part, unit_in, inverse_in, full_norm_in.astype(jnp.float32)
    )
    summed = lax.psum((source_part, grad_norm_in, grad_norm_ffn, grad_router), "wa")
    tokens_gradient = grad_hidden + summed[0]
    reduced = (
        lax.psum_scatter(summed[1], "ctx", scatter_dimension=0, tiled=True),
        lax.psum_scatter(grad_query, "ctx", scatter_dimension=0, tiled=True),
        lax.psum_scatter(grad_down, "ctx", scatter_dimension=0, tiled=True),
        lax.psum_scatter(grad_latent_norm, "ctx", scatter_dimension=0, tiled=True),
        lax.psum_scatter(grad_latent_up, "ctx", scatter_dimension=0, tiled=True),
        lax.psum_scatter(grad_output, "ctx", scatter_dimension=1, tiled=True),
        lax.psum_scatter(summed[2], "ctx", scatter_dimension=0, tiled=True),
        lax.psum_scatter(summed[3], "ctx", scatter_dimension=0, tiled=True),
        lax.psum_scatter(grad_shared_gate, "ctx", scatter_dimension=0, tiled=True),
        lax.psum_scatter(grad_shared_up, "ctx", scatter_dimension=0, tiled=True),
        lax.psum_scatter(grad_shared_down, "ctx", scatter_dimension=1, tiled=True),
    )
    return (
        output.astype(jnp.bfloat16),
        tokens_gradient,
        reduced[0],
        reduced[1],
        reduced[2],
        reduced[3],
        reduced[4],
        reduced[5],
        reduced[6],
        reduced[7],
        reduced[8],
        reduced[9],
        reduced[10],
        grad_expert_gate,
        grad_expert_up,
        grad_expert_down,
    )


VMEM_LIMIT = 60 * 1024 * 1024
TILE = 256


def local_call(body, grid, in_specs, out_specs, out_shape, operands, after=()):
    inputs = len(in_specs)

    def run(*refs):
        body(*refs[:inputs], *refs[inputs + len(after) :])

    return pl.pallas_call(
        run,
        grid=grid,
        in_specs=list(in_specs) + [pl.BlockSpec(memory_space=pl.ANY)] * len(after),
        out_specs=out_specs,
        out_shape=out_shape,
        compiler_params=pltpu.CompilerParams(vmem_limit_bytes=VMEM_LIMIT),
        cost_estimate=pl.CostEstimate(flops=1, bytes_accessed=1, transcendentals=0),
    )(*operands, *after)


def whole(array):
    return pl.BlockSpec(array.shape, lambda *_: (0,) * array.ndim)


def by_rows(array, rows=TILE):
    return pl.BlockSpec((rows, array.shape[1]), lambda i: (i, 0))


def by_first(array):
    return pl.BlockSpec((1,) + array.shape[1:], lambda i: (i,) + (0,) * (array.ndim - 1))


def shaped(shape, dtype=jnp.bfloat16):
    return jax.ShapeDtypeStruct(shape, dtype)


def mul(left, right):
    return jnp.dot(left, right, preferred_element_type=jnp.float32)


def mul_nt(left, right):
    return lax.dot_general(
        left, right, (((1,), (1,)), ((), ())), preferred_element_type=jnp.float32
    )


def mul_tn(left, right):
    return lax.dot_general(
        left, right, (((0,), (0,)), ((), ())), preferred_element_type=jnp.float32
    )


def glu_back(gate, up, grads):
    sigmoid = 1.0 / (1.0 + jnp.exp(-gate))
    silu = gate * sigmoid
    slope = sigmoid * (1.0 + gate * (1.0 - sigmoid))
    return (silu * up, grads * up * slope, grads * silu)


def feed_body(
    experts, rows, back, shared_back, gate_t, up_t, small_t, named, pick,
    act_out, shared_act_out, gate_out, up_out, shared_out, gain_out,
):
    here = rows[...]
    part = small_t.shape[0] // 3
    small = mul_nt(here, small_t[...])
    logits = small[:, 2 * part :]
    ids = lax.broadcasted_iota(jnp.int32, logits.shape, 1)
    logits = jnp.where(ids < experts, logits, -1e30)
    chances = jnp.exp(logits - jnp.max(logits, axis=1, keepdims=True))
    total = jnp.sum(chances, axis=1, keepdims=True)
    named_here = named[...]
    share = jnp.sum(chances * pick[...], axis=1, keepdims=True) / total * named_here
    act, gate_grad, up_grad = glu_back(
        small[:, :part], small[:, part : 2 * part], shared_back[...].astype(jnp.float32)
    )
    shared_act_out[...] = act.astype(jnp.bfloat16)
    shared_out[:, :part] = gate_grad.astype(jnp.bfloat16)
    shared_out[:, part:] = up_grad.astype(jnp.bfloat16)
    grads = back[...].astype(jnp.float32)
    act, gate_grad, up_grad = glu_back(mul_nt(here, gate_t[...]), mul_nt(here, up_t[...]), grads)
    gain_out[...] = jnp.sum(act * grads, axis=1, keepdims=True) * named_here
    act_out[...] = (act * share).astype(jnp.bfloat16)
    gate_out[...] = (gate_grad * share).astype(jnp.bfloat16)
    up_out[...] = (up_grad * share).astype(jnp.bfloat16)


def feed_kernel(rows, back, shared_back, gate_t, up_t, small_t, named, pick, experts):
    count = rows.shape[0]
    hidden, part = (back.shape[1], shared_back.shape[1])
    shapes = [shaped((count, s)) for s in (hidden, part, hidden, hidden, 2 * part)]
    shapes.append(shaped((count, 1), jnp.float32))
    return local_call(
        partial(feed_body, experts),
        (count // TILE,),
        [
            by_rows(rows),
            by_rows(back),
            by_rows(shared_back),
            whole(gate_t),
            whole(up_t),
            whole(small_t),
            by_rows(named),
            whole(pick),
        ],
        [by_rows(s) for s in shapes],
        shapes,
        (rows, back, shared_back, gate_t, up_t, small_t, named, pick),
    )


def input_body(gate, up, shared, gate_t, up_t, small_t, gain, pick, out):
    width = gate_t.shape[1]
    used = shared.shape[1]
    out[:, :width] = (
        mul(gate[...], gate_t[...]) + mul(up[...], up_t[...]) + mul(shared[...], small_t[:used, :])
    ).astype(jnp.bfloat16)
    out[:, width:] = (gain[...] * pick[...]).astype(jnp.bfloat16)


def input_kernel(gate, up, shared, gate_t, up_t, small_t, gain, pick, after=()):
    count = gate.shape[0]
    shape = shaped((count, gate_t.shape[1] + pick.shape[1]))
    return local_call(
        input_body,
        (count // TILE,),
        [by_rows(gate), by_rows(up), by_rows(shared)]
        + [whole(gate_t), whole(up_t), whole(small_t), by_rows(gain), whole(pick)],
        by_rows(shape),
        shape,
        (gate, up, shared, gate_t, up_t, small_t, gain, pick),
        after,
    )


def result_body(act, shared_act, down, shared_down, out):
    out[...] = (mul(act[...], down[...]) + mul(shared_act[...], shared_down[...])).astype(
        jnp.bfloat16
    )


def result_kernel(act, shared_act, down, shared_down, after=()):
    count = act.shape[0]
    shape = shaped((count, down.shape[1]))
    return local_call(
        result_body,
        (count // TILE,),
        [by_rows(act), by_rows(shared_act), whole(down), whole(shared_down)],
        by_rows(shape),
        shape,
        (act, shared_act, down, shared_down),
        after,
    )


def weight_body(left_own, left_other, more_own, more_other, own, other, out, more_out):
    here, there = (own[...], other[...])
    out[...] = mul_tn(left_own[...], here) + mul_tn(left_other[...], there)
    more_out[...] = (mul_tn(more_own[...], here) + mul_tn(more_other[...], there)).astype(
        jnp.bfloat16
    )


def weight_kernel(lefts, mores, rights, side=0, part=128, after=()):
    count, width = rights[0].shape
    columns = lambda rows: pl.BlockSpec((rows, TILE), lambda i: (0, i))
    hidden, more = (lefts[0].shape[1], part)
    return local_call(
        weight_body,
        (width // TILE,),
        [whole(a) for a in lefts]
        + [pl.BlockSpec((count, part), lambda i: (0, side))] * 2
        + [columns(count)] * 2,
        [columns(hidden), columns(more)],
        [shaped((hidden, width), jnp.float32), shaped((more, width))],
        (*lefts, *mores, *rights),
        after,
    )


def head_parts_of(query, heads, nope):
    rope = query.shape[1] // heads - nope
    return [
        (
            query[:, k * nope : (k + 1) * nope],
            query[:, heads * nope + k * rope : heads * nope + (k + 1) * rope],
        )
        for k in range(heads)
    ]


def attend_body(
    heads, scale, query, own, other, up, out_weight, spots, key_spots,
    kept_out, sent_out, prob_out, absorbed_out, latent_out, head_out,
):
    rank = up.shape[0]
    absorbed, ropes = ([], [])
    for k, (nope, rope) in enumerate(head_parts_of(query[...], heads, DN)):
        key_up = up[:, k * (DN + DV) : k * (DN + DV) + DN]
        absorbed.append(mul_nt(nope, key_up).astype(jnp.bfloat16))
        ropes.append(rope)
    absorbed = jnp.concatenate(absorbed, axis=0)
    rope = jnp.concatenate(ropes, axis=0)
    absorbed_out[0] = absorbed
    keys = [source[0, k] for source in (own, other) for k in range(2)]
    scores = jnp.concatenate(
        [mul_nt(absorbed, key[:, :rank]) + mul_nt(rope, key[:, rank:]) for key in keys], axis=1
    )
    allowed = spots[...] >= key_spots[...]
    allowed = jnp.concatenate([allowed] * heads, axis=0)
    scores = jnp.where(allowed, scores * scale, -1e30)
    weights = jnp.exp(scores - jnp.max(scores, axis=1, keepdims=True))
    prob = (weights / jnp.sum(weights, axis=1, keepdims=True)).astype(jnp.bfloat16)
    prob_out[0] = prob
    size = keys[0].shape[0]
    latent = sum(
        mul(prob[:, j * size : (j + 1) * size], key[:, :rank]) for j, key in enumerate(keys)
    ).astype(jnp.bfloat16)
    latent_out[0] = latent
    rows = query.shape[0]
    head = jnp.concatenate(
        [
            mul(
                latent[k * rows : (k + 1) * rows],
                up[:, k * (DN + DV) + DN : (k + 1) * (DN + DV)],
            )
            for k in range(heads)
        ],
        axis=1,
    ).astype(jnp.bfloat16)
    head_out[...] = head
    total = mul(head, out_weight[...]).astype(jnp.bfloat16)
    kept_out[0] = total[: rows // 2]
    sent_out[0] = total[rows // 2 :]


def attend_kernel(query, own, other, up, out_weight, spots, key_spots, heads, scale, after=()):
    sequences = own.shape[0]
    rows = query.shape[0] // sequences
    key_count = 4 * own.shape[2]
    rank = up.shape[0]
    shapes = [
        shaped((sequences, rows // 2, out_weight.shape[1])),
        shaped((sequences, rows // 2, out_weight.shape[1])),
        shaped((sequences, heads * rows, key_count)),
        shaped((sequences, heads * rows, rank)),
        shaped((sequences, heads * rows, rank)),
        shaped((query.shape[0], heads * DV)),
    ]
    return local_call(
        partial(attend_body, heads, scale),
        (sequences,),
        [by_rows(query, rows), by_first(own), by_first(other)]
        + [whole(a) for a in (up, out_weight, spots, key_spots)],
        [by_first(shape) for shape in shapes[:5]] + [by_rows(shapes[5], rows)],
        shapes,
        (query, own, other, up, out_weight, spots, key_spots),
        after,
    )


def attend_back_body(
    heads, scale, grads, query, own, other, up, out_weight, prob, absorbed, latent,
    own_out, other_out, query_out, up_out,
):
    rank = up.shape[0]
    rows = query.shape[0]
    first = pl.program_id(0) == 0
    grads_here = grads[...]
    head_grad = mul_nt(grads_here, out_weight[...]).astype(jnp.bfloat16)
    span = lambda k: slice(k * rows, (k + 1) * rows)
    latent_grad = []
    value_parts = []
    for k in range(heads):
        mine = head_grad[:, k * DV : (k + 1) * DV]
        value_up = up[:, k * (DN + DV) + DN : (k + 1) * (DN + DV)]
        latent_grad.append(mul_nt(mine, value_up).astype(jnp.bfloat16))
        value_parts.append(mul_tn(latent[0, span(k)], mine))
    latent_grad = jnp.concatenate(latent_grad, axis=0)
    keys = [source[0, k] for source in (own, other) for k in range(2)]
    size = keys[0].shape[0]
    prob_here = prob[0]
    prob_wide = prob_here.astype(jnp.float32)
    prob_grad = jnp.concatenate([mul_nt(latent_grad, key[:, :rank]) for key in keys], axis=1)
    inner = jnp.sum(prob_wide * prob_grad, axis=1, keepdims=True)
    score_grad = (prob_wide * (prob_grad - inner)).astype(jnp.bfloat16)
    absorbed_here = absorbed[0]
    parts = head_parts_of(query[...], heads, DN)
    rope = jnp.concatenate([part[1] for part in parts], axis=0)
    wide = 0.0
    narrow = 0.0
    for j, key in enumerate(keys):
        piece = score_grad[:, j * size : (j + 1) * size]
        wide = wide + mul(piece, key[:, :rank])
        narrow = narrow + mul(piece, key[:, rank:])
        target = (own_out, other_out)[j // 2]
        value = mul_tn(prob_here[:, j * size : (j + 1) * size], latent_grad)
        target[0, j % 2, :, :rank] = (mul_tn(piece, absorbed_here) * scale + value).astype(
            jnp.bfloat16
        )
        target[0, j % 2, :, rank:] = (mul_tn(piece, rope) * scale).astype(jnp.bfloat16)
    wide = (wide * scale).astype(jnp.bfloat16)
    narrow = narrow * scale
    for k in range(heads):
        start = k * (DN + DV)
        key_part = mul_tn(wide[span(k)], parts[k][0])
        up_out[:, start : start + DN] = (
            jnp.where(first, 0.0, up_out[:, start : start + DN]) + key_part
        )
        up_out[:, start + DN : start + DN + DV] = (
            jnp.where(first, 0.0, up_out[:, start + DN : start + DN + DV]) + value_parts[k]
        )
        query_out[:, k * DN : (k + 1) * DN] = mul(wide[span(k)], up[:, start : start + DN])
        rope_size = narrow.shape[1]
        at = heads * DN + k * rope_size
        query_out[:, at : at + rope_size] = narrow[span(k)]


def attend_back_kernel(
    grads, query, own, other, up, out_weight, prob, absorbed, latent, heads, scale, after=()
):
    sequences = own.shape[0]
    rows = query.shape[0] // sequences
    shapes = [
        shaped(own.shape),
        shaped(own.shape),
        shaped(query.shape, jnp.float32),
        shaped(up.shape, jnp.float32),
    ]
    return local_call(
        partial(attend_back_body, heads, scale),
        (sequences,),
        [by_rows(grads, rows), by_rows(query, rows), by_first(own), by_first(other)]
        + [whole(up), whole(out_weight), by_first(prob), by_first(absorbed), by_first(latent)],
        [by_first(own), by_first(own), by_rows(query, rows), whole(up)],
        shapes,
        (grads, query, own, other, up, out_weight, prob, absorbed, latent),
        after,
    )


def heads_body(parts, *refs):
    query_out, up_out, out_out = refs
    count, groups, rows, _ = parts.shape
    query_columns = query_out.shape[1]
    up_blocks = up_out.shape[1] // 128
    up_rows = rows // up_blocks
    heads = out_out.shape[0] // rows
    for block in range(count * groups):
        here = parts[block // groups, block % groups]
        span = slice(block * rows, (block + 1) * rows)
        query_out[span, :] = here[:, :query_columns]
        for k in range(up_blocks):
            up_out[block * up_rows : (block + 1) * up_rows, k * 128 : (k + 1) * 128] = here[
                k * up_rows : (k + 1) * up_rows, query_columns : query_columns + 128
            ]
        for k in range(heads):
            at = query_columns + 128 + k * rows
            out_out[k * rows : (k + 1) * rows, span] = here[:, at : at + rows]


def heads_kernel(parts, query_columns, heads, up_columns, after=()):
    count, groups, rows, _ = parts.shape
    width = count * groups * rows
    up_rows = rows * 128 // up_columns
    shapes = [
        shaped((width, query_columns)),
        shaped((count * groups * up_rows, up_columns)),
        shaped((heads * rows, width)),
    ]
    return local_call(
        heads_body,
        (1,),
        [whole(parts)],
        [whole(s) for s in shapes],
        shapes,
        (parts,),
        after,
    )


SCALAR = pl.BlockSpec(memory_space=pltpu.SMEM)


def out_grads_body(rows, z, head, grads, *outs):
    heads = head.shape[1] // rows
    for s, out in enumerate(outs):
        size = out.shape[0] * rows
        start = pl.multiple_of(lax.rem(z[0] + s, len(outs)) * size, size)
        total = mul_tn(head[...], grads[:, pl.ds(start, size)]).astype(jnp.bfloat16)
        for j in range(out.shape[0]):
            for k in range(heads):
                out[j, :, k * rows : (k + 1) * rows] = total[
                    k * rows : (k + 1) * rows, j * rows : (j + 1) * rows
                ]


def out_grads_kernel(z, count, head, grads, rows):
    shapes = [shaped((grads.shape[1] // (rows * count), rows, head.shape[1]))] * count
    return local_call(
        partial(out_grads_body, rows),
        (1,),
        [SCALAR, whole(head), whole(grads)],
        [whole(s) for s in shapes],
        shapes,
        (z, head, grads),
    )


def query_grads_body(rows, grads, source, up, more, out):
    columns = grads.shape[1]
    up_blocks = up.shape[1] // 128
    up_rows = rows // up_blocks
    here = grads[...]
    for i in range(out.shape[0]):
        span = slice(i * rows, (i + 1) * rows)
        out[i, :, :columns] = mul_tn(source[:, span], here).astype(jnp.bfloat16)
        for k in range(up_blocks):
            out[i, k * up_rows : (k + 1) * up_rows, columns : columns + 128] = up[
                i * up_rows : (i + 1) * up_rows, k * 128 : (k + 1) * 128
            ].astype(jnp.bfloat16)
        out[i, :, columns + 128 :] = more[i]


def query_grads_kernel(grads, source, up, more, rows):
    shape = shaped((source.shape[1] // rows, rows, grads.shape[1] + 128 + more.shape[2]))
    return local_call(
        partial(query_grads_body, rows),
        (1,),
        [whole(grads), whole(source), whole(up), whole(more)],
        whole(shape),
        shape,
        (grads, source, up, more),
    )


def latent_grads_body(z, place, source, grads, *outs):
    rows = outs[0].shape[0]
    here = grads[...]
    for s, out in enumerate(outs):
        block = 4 * lax.rem(z[0] + s, len(outs)) + place[0]
        start = pl.multiple_of(block * rows, rows)
        out[...] = mul_tn(source[:, pl.ds(start, rows)], here).astype(jnp.bfloat16)


def latent_grads_kernel(z, place, count, source, grads, rows):
    shapes = [shaped((rows, grads.shape[1]))] * count
    return local_call(
        latent_grads_body,
        (1,),
        [SCALAR, SCALAR, whole(source), whole(grads)],
        [whole(s) for s in shapes],
        shapes,
        (z, place, source, grads),
    )


def split_product_body(left, right, kept_out, sent_out):
    total = mul_nt(left[...], right[...]).astype(jnp.bfloat16)
    half = total.shape[0] // 2
    kept_out[0] = total[:half]
    sent_out[0] = total[half:]


def split_product_kernel(left, right, sequences, after=()):
    rows = left.shape[0] // sequences
    shapes = [shaped((sequences, rows // 2, right.shape[0]))] * 2
    return local_call(
        split_product_body,
        (sequences,),
        [by_rows(left, rows), whole(right)],
        [by_first(s) for s in shapes],
        shapes,
        (left, right),
        after,
    )


def core_fold_body(*refs):
    for k in range(4):
        total = refs[k][0, 0].astype(jnp.float32) + refs[4 + k][0, 0].astype(jnp.float32)
        refs[8 + k][0] = total.astype(jnp.bfloat16)


def core_fold_kernel(own, received, after=()):
    half, width = (own.shape[2] // 2, own.shape[3])
    block = (1, 1, half, width)
    specs = [
        pl.BlockSpec(block, lambda k: (0, k, 0, 0)),
        pl.BlockSpec(block, lambda k: (1, k, 0, 0)),
        pl.BlockSpec(block, lambda k: (k, 0, 1, 0)),
        pl.BlockSpec(block, lambda k: (k, 1, 1, 0)),
    ]
    shapes = [shaped((2, half, width))] * 4
    return local_call(
        core_fold_body,
        (2,),
        specs + specs,
        [by_first(s) for s in shapes],
        shapes,
        (own,) * 4 + (received,) * 4,
        after,
    )


def plane_fold_body(lower, lower_got, upper, upper_got, *outs):
    for k, (left, right) in enumerate(((lower, lower_got), (upper, upper_got))):
        for j in range(2):
            total = left[j].astype(jnp.float32) + right[j].astype(jnp.float32)
            outs[2 * k + j][...] = total.astype(jnp.bfloat16)


def plane_fold_kernel(lower, lower_got, upper, upper_got, after=()):
    _, rows, width = lower.shape
    tile = max(16, rows // 2)
    spec = pl.BlockSpec((2, tile, width), lambda i: (0, i, 0))
    shapes = [shaped((rows, width))] * 4
    return local_call(
        plane_fold_body,
        (rows // tile,),
        [spec] * 4,
        [by_rows(s, tile) for s in shapes],
        shapes,
        (lower, lower_got, upper, upper_got),
        after,
    )


def slab_fold_body(lower, lower_got, upper, upper_got, own_out, *outs):
    half = lower.shape[0]
    count = len(outs) + 1
    block = 2 * half // count
    for k, (left, right) in enumerate(((lower, lower_got), (upper, upper_got))):
        total = left[...].astype(jnp.float32) + right[...].astype(jnp.float32)
        if count == 1:
            own_out[k * half : (k + 1) * half, :] = total
            continue
        for j in range(half // block):
            here = total[j * block : (j + 1) * block]
            s = k * (half // block) + j
            if s == 0:
                own_out[...] = here
            else:
                outs[s - 1][...] = here.astype(jnp.bfloat16)


def slab_fold_kernel(lower, lower_got, upper, upper_got, count, after=()):
    half, width = lower.shape
    block = 2 * half // count
    shapes = [shaped((block, width), jnp.float32)] + [shaped((block, width))] * (count - 1)
    return local_call(
        slab_fold_body,
        (1,),
        [whole(lower)] * 4,
        [whole(s) for s in shapes],
        shapes,
        (lower, lower_got, upper, upper_got),
        after,
    )


def z_fold_body(*refs):
    total = refs[0][...].astype(jnp.float32)
    for ref in refs[1:-1]:
        total = total + ref[...].astype(jnp.float32)
    refs[-1][...] = total.astype(refs[-1].dtype)


def z_fold_kernel(parts, dtype, after=()):
    shape = shaped(parts[0].shape, dtype)
    return local_call(
        z_fold_body, (1,), [whole(p) for p in parts], whole(shape), shape, tuple(parts), after
    )


def product_nt_body(left, right, out):
    out[...] = mul_nt(left[...], right[...]).astype(jnp.bfloat16)


def product_nt_kernel(left, right, after=()):
    shape = shaped((left.shape[0], right.shape[0]))
    return local_call(
        product_nt_body,
        (left.shape[0] // TILE,),
        [by_rows(left), whole(right)],
        by_rows(shape),
        shape,
        (left, right),
        after,
    )


def join_body(*refs):
    out = refs[-1]
    at = 0
    for ref in refs[:-1]:
        out[at : at + ref.shape[0], :] = ref[...]
        at += ref.shape[0]


def join_kernel(parts, after=(), more=()):
    parts = list(parts) + list(more)
    shape = shaped((sum(p.shape[0] for p in parts), parts[0].shape[1]), parts[0].dtype)
    return local_call(
        join_body, (1,), [whole(p) for p in parts], whole(shape), shape, tuple(parts), after
    )


def reorder_body(places, *refs):
    del places
    out = refs[-1]
    rows = refs[0].shape[1]
    for s in range(4):
        out[s * rows : (s + 1) * rows, :] = refs[s][0]


def reorder_kernel(places, blocks, after):
    _, rows, width = blocks.shape
    count = places.shape[0]
    step = lambda s: pl.BlockSpec((1, rows, width), lambda i, places: (places[4 * i + s], 0, 0))
    return pl.pallas_call(
        lambda places, a, b, c, d, dep, out: reorder_body(places, a, b, c, d, out),
        grid_spec=pltpu.PrefetchScalarGridSpec(
            num_scalar_prefetch=1,
            grid=(count // 4,),
            in_specs=[step(s) for s in range(4)] + [pl.BlockSpec(memory_space=pl.ANY)],
            out_specs=pl.BlockSpec((4 * rows, width), lambda i, places: (i, 0)),
        ),
        out_shape=shaped((count * rows, width)),
        compiler_params=pltpu.CompilerParams(vmem_limit_bytes=VMEM_LIMIT),
        cost_estimate=pl.CostEstimate(flops=1, bytes_accessed=1, transcendentals=0),
    )(places, *[blocks] * 4, after)


CTX = ("z", "x", "c")


def swap(value, axis):
    return lax.ppermute(value, axis, [(0, 1), (1, 0)])


def from_z(value, steps):
    count = lax.axis_size("z")
    return lax.ppermute(value, "z", [((i + steps) % count, i) for i in range(count)])


def to_z(value, steps):
    count = lax.axis_size("z")
    return lax.ppermute(value, "z", [(i, (i + steps) % count) for i in range(count)])


def trade(value, axes):
    return lax.all_to_all(value, axes, split_axis=0, concat_axis=0, tiled=True)


def add(left, right):
    return left.astype(jnp.float32) + right.astype(jnp.float32)


def low(value):
    return value.astype(jnp.bfloat16)


def dot(left, right):
    return jnp.dot(left, right, preferred_element_type=jnp.float32)


def dot_nt(left, right):
    return lax.dot_general(
        left, right, (((1,), (1,)), ((), ())), preferred_element_type=jnp.float32
    )


def dot_tn(left, right):
    return lax.dot_general(
        left, right, (((0,), (0,)), ((), ())), preferred_element_type=jnp.float32
    )


def by_own(value, axis_name, dim):
    flipped = jnp.flip(value, axis=dim)
    return jnp.where(lax.axis_index(axis_name) == 0, value, flipped)


def tie(value, *others):
    if not others:
        return value
    zero = sum(other[(0,) * other.ndim].astype(jnp.float32) for other in others) * 0.0
    return value + zero.astype(value.dtype)


def rows_first(value):
    return with_layout_constraint(value, Layout(major_to_minor=tuple(range(value.ndim))))


def put(parts, places):
    whole = jnp.zeros((len(parts),) + parts[0].shape, parts[0].dtype)
    for part, place in zip(parts, places):
        whole = lax.dynamic_update_index_in_dim(whole, part, place, 0)
    return rows_first(whole)


def z_parts(value):
    return [value] + [from_z(value, s) for s in range(1, lax.axis_size("z"))]


def put_z(parts):
    z = lax.axis_index("z")
    count = len(parts)
    return put(parts, [(z + s) % count for s in range(count)])


def gather_plane(rows, axes=("x", "y"), gates=()):
    half = rows.shape[0] // 2
    over_a = tie(swap(rows, axes[0]), *gates)
    over_b = tie(swap(rows, axes[1]), *gates)
    both = jnp.concatenate([swap(over_b[:half], axes[0]), swap(over_a[half:], axes[1])], axis=0)
    return jnp.stack([jnp.stack([rows, over_b]), jnp.stack([over_a, both])])


def fold_first(pieces, axes, after=()):
    lower, lower_sent, upper, upper_sent = pieces
    return plane_fold_kernel(
        lower, swap(lower_sent, axes[0]), upper, swap(upper_sent, axes[1]), after
    )


def fold_second(pieces, axes, count, after=()):
    lower, lower_sent, upper, upper_sent = pieces
    return slab_fold_kernel(
        lower, swap(lower_sent, axes[1]), upper, swap(upper_sent, axes[0]), count, after
    )


def fold_z(parts, dtype=jnp.float32, after=()):
    received = [to_z(part, s + 1) for s, part in enumerate(parts[1:])]
    return z_fold_kernel([parts[0]] + received, dtype, after)


def spread_z(rows):
    return jnp.concatenate(z_parts(rows), axis=0)


def both_halves(rows):
    other = swap(rows, "y")
    return by_own(jnp.stack([rows, other]), "y", 0)


def dense_shards(
    tokens,
    norm_in,
    query_weight,
    latent_down,
    latent_norm,
    latent_up,
    output_weight,
    norm_ffn,
    router_weight,
    shared_gate,
    shared_up,
    shared_down,
    expert_gate,
    expert_up,
    expert_down,
    routes,
    cotangent,
):
    zs = lax.axis_size("z")
    z, x, c = (lax.axis_index("z"), lax.axis_index("x"), lax.axis_index("c"))
    me = (z * 2 + x) * 2 + c
    sequences, block, width = tokens.shape
    count = 4 * zs
    rows_here = width // count
    slab = 4 * block
    experts = router_weight.shape[1]
    shared_here = shared_gate.shape[1] // count
    part = -(-max(shared_here, experts) // 128) * 128
    heads = latent_up.shape[1] // (4 * (DN + DV))
    query_columns = heads * (DN + DR)
    rank_rows = R // count
    head_rows = heads * DV
    scale = (DN + DR) ** (-0.5)

    latent_column = jnp.pad(latent_norm, (0, rows_here - rank_rows))[:, None]
    small = jnp.concatenate(
        [
            latent_down,
            router_weight,
            norm_in[:, None],
            norm_ffn[:, None],
            latent_column,
            routes.reshape(sequences * block, TOPK).astype(jnp.bfloat16),
        ],
        axis=1,
    )
    small_parts = z_parts(jnp.pad(small, ((0, 0), (0, -small.shape[1] % 128))))
    up_columns = heads * (DN + DV)
    up_part = jnp.transpose(
        latent_up.reshape(rank_rows, 4, up_columns // 128, 128), (1, 2, 0, 3)
    ).reshape(4, rows_here, 128)
    out_part = jnp.transpose(output_weight.reshape(4, heads, DV, rows_here), (0, 2, 1, 3)).reshape(
        4, DV, heads * rows_here
    )
    by_heads = query_weight.reshape(rows_here, 4, heads, DN + DR)
    by_heads = jnp.concatenate(
        [
            by_heads[..., :DN].reshape(rows_here, 4, heads * DN),
            by_heads[..., DN:].reshape(rows_here, 4, heads * DR),
        ],
        axis=2,
    )
    by_heads = jnp.transpose(by_heads, (1, 0, 2))
    by_heads = jnp.concatenate([by_heads, up_part, out_part], axis=2)
    mine_at = 2 * x + c
    for_group = [
        lax.dynamic_index_in_dim(by_heads, mine_at ^ k, 0, keepdims=False) for k in range(4)
    ]
    by_heads = put(
        [
            for_group[0],
            swap(for_group[1], "c"),
            swap(for_group[2], "x"),
            lax.ppermute(for_group[3], ("x", "c"), [(k, 3 - k) for k in range(4)]),
        ],
        [mine_at ^ k for k in range(4)],
    )
    small = put_z([tie(part, by_heads) for part in small_parts])
    at = R + DR
    down_here = small[:, :, :at]
    rest = small[:, :, at:]
    down_here = down_here.reshape(-1, R + DR)
    down_x = swap(down_here, "x")
    down_pieces = (down_here, down_x, swap(down_here, "c"), swap(down_x, "c"))
    own_gain = rest[:, :, experts].reshape(1, zs * rows_here).astype(jnp.float32)
    rest = jnp.stack([rest, swap(rest, "x")], axis=1)
    rest = jnp.stack([rest, swap(rest, "c")], axis=2)
    rest = by_own(by_own(rest, "x", 1), "c", 2).reshape(count, rows_here, -1)
    full_router = rest[:, :, :experts].reshape(width, experts)
    full_norm_in = rest[:, :, experts].reshape(width).astype(jnp.float32)
    full_norm_ffn = rest[:, :, experts + 1].reshape(width).astype(jnp.float32)
    full_latent_norm = rest[:, :rank_rows, experts + 2].reshape(R).astype(jnp.float32)
    all_routes = rest[:, :, experts + 3 : experts + 3 + TOPK]

    mine = by_own(tokens, "y", 0)
    line = jnp.stack([mine, swap(mine, "x")], axis=1)
    line = jnp.stack([line, swap(line, "c")], axis=1)
    source = line.reshape(sequences * slab, width).astype(jnp.float32)
    grad_mine = by_own(cotangent, "y", 0)[0]
    all_grads = lax.all_gather(tie(grad_mine, by_heads), CTX + ("y",), axis=0)
    one = jnp.arange(2)
    order = (
        (((z + jnp.arange(zs)) % zs)[None, None, None, :] * 2 + (x ^ one)[None, :, None, None]) * 2
        + (c ^ one)[:, None, None, None]
    ) * 2 + (lax.axis_index("y") ^ one)[None, None, :, None]
    order = order.reshape(-1).astype(jnp.int32)
    gate_t, up_t, down = (expert_gate[0].T, expert_up[0].T, expert_down[0])
    query_here, up_here, out_here = heads_kernel(
        lax.all_gather(by_heads, "z", axis=0),
        query_columns,
        heads,
        up_columns,
    )

    def places(turns):
        two = jnp.arange(2)
        base = (
            ((z + turns[None, None, :]) % zs) * 4
            + (x ^ two[None, :, None]) * 2
            + (c ^ two[:, None, None])
        )
        return (base[..., None] * block + jnp.arange(block)).reshape(-1)

    positions = places(jnp.arange(1))
    key_positions = places(jnp.arange(zs))
    cosine, sine = rotary_tables(positions, DR)
    normed, unit_in, inverse_in = root_norm(source, full_norm_in)
    input_low = low(normed)

    own_rows = line[0].reshape(slab, width)
    own_columns = jnp.concatenate(
        [
            lax.dynamic_slice_in_dim(own_rows, (4 * k + 2 * x + c) * rows_here, rows_here, 1)
            for k in range(zs)
        ],
        axis=1,
    ).astype(jnp.float32)
    latent_part = dot(
        low(own_columns * inverse_in[:slab] * own_gain), down_here
    )
    latent_part = low(latent_part).reshape(2, 2, block, R + DR)
    latent_part = low(add(latent_part[0], swap(latent_part[1], "c")))
    latent_raw = add(latent_part[0], swap(latent_part[1], "x"))
    latent_scaled, latent_unit, latent_inverse = root_norm(latent_raw[:, :R], full_latent_norm)
    key_own = low(
        jnp.concatenate(
            [latent_scaled, rotate(latent_raw[:, R:], cosine[:block], sine[:block])], axis=-1
        )
    )
    plane = gather_plane(spread_z(key_own), ("y", "x"))
    keys_own, keys_other = (plane, swap(plane, "c"))
    query = dot(input_low, query_here)
    rope = query[:, heads * DN :].reshape(sequences, slab, heads, DR)
    rope = rotate(rope, cosine[:, None, :], sine[:, None, :]).reshape(sequences * slab, -1)
    query_low = low(jnp.concatenate([query[:, : heads * DN], rope], axis=1))

    shared_mine = jnp.concatenate(
        [
            shared_gate.T.reshape(count, shared_here, rows_here),
            shared_up.T.reshape(count, shared_here, rows_here),
            shared_down.reshape(count, shared_here, rows_here),
        ],
        axis=1,
    )
    shared_rows = trade(tie(shared_mine, query_low), CTX)
    shared_got = shared_rows
    shared_rows = jnp.transpose(shared_rows, (1, 0, 2)).reshape(3, shared_here, width)
    shared_rows = jnp.pad(shared_rows, ((0, 0), (0, part - shared_here), (0, 0)))
    small_t = jnp.concatenate(
        [
            shared_rows[0],
            shared_rows[1],
            jnp.pad(full_router.T, ((0, part - experts), (0, 0))),
        ]
    )
    shared_down_t = shared_rows[2]

    def scatter_slab(kept, sent, after=()):
        shape = (2, 2, block, width)
        pieces = core_fold_kernel(kept.reshape(shape), swap(sent, "c").reshape(shape))
        return fold_second(fold_first(pieces, ("y", "x"), after), ("y", "x"), 1)[0]

    def gather_slab(rows):
        plane = gather_plane(rows, ("y", "x"))
        return jnp.stack([plane, swap(plane, "c")], axis=1).reshape(sequences * slab, -1)

    kept, sent, prob, absorbed, latent_out, head_out = attend_kernel(
        query_low,
        keys_own,
        keys_other,
        up_here,
        out_here,
        positions[:, None],
        key_positions[None, :],
        heads,
        scale,
        down_pieces[1:],
    )
    attention = scatter_slab(kept, sent)
    hidden_in = mine[0].astype(jnp.float32) + attention
    normed_ffn, unit_ffn, inverse_ffn = root_norm(hidden_in, full_norm_ffn)
    ffn_low = low(normed_ffn)
    shares = jax.nn.softmax(dot(ffn_low, full_router), axis=-1)
    half_places = order.shape[0] // 2
    grads_own = reorder_kernel(order[:half_places], all_grads, ffn_low)
    grads_other = reorder_kernel(order[half_places:], all_grads, ffn_low)
    ffn_parts = z_parts(ffn_low)
    back_own = product_nt_kernel(grads_own, down)
    back_other = product_nt_kernel(grads_other, down, (back_own,))
    ffn_slabs = join_kernel(ffn_parts, (shared_got, back_other))
    shared_own = product_nt_kernel(grads_own, shared_down_t, (ffn_slabs,))
    shared_other = product_nt_kernel(grads_other, shared_down_t, (shared_own,))
    half = ffn_slabs.shape[0] // 2
    over_x, over_y = (swap(ffn_slabs, "x"), swap(ffn_slabs, "y"))
    ffn_own = join_kernel(
        [ffn_slabs, over_y, over_x],
        (shared_other,),
        [swap(over_y[:half], "x"), swap(over_x[half:], "y")],
    )
    ffn_other = swap(ffn_own, "c").reshape(-1, width)

    relative = all_routes.reshape(zs, 2, 2, sequences, block, TOPK)
    relative = by_own(by_own(by_own(relative, "x", 1), "c", 2), "y", 3)
    relative = jnp.roll(relative, -z, axis=0)
    routed = jnp.any(relative == me.astype(jnp.bfloat16), axis=-1)
    routed = jnp.transpose(routed, (2, 1, 3, 0, 4)).reshape(2, -1, 1).astype(jnp.float32)
    pick = (jnp.arange(part)[None, :] == me).astype(jnp.float32)

    def feed(rows, back, shared_back, named):
        return feed_kernel(rows, back, shared_back, gate_t, up_t, small_t, named, pick, experts)

    act_own, more_own, gate_own, up_own, pre_own, gain_own = feed(
        ffn_own, back_own, shared_own, routed[0]
    )
    act_other, more_other, gate_other, up_other, pre_other, gain_other = feed(
        ffn_other, back_other, shared_other, routed[1]
    )
    shape = (2, 2, zs * block, width + part)
    grad_other = input_kernel(
        gate_other, up_other, pre_other, gate_t, up_t, small_t, gain_other, pick
    )
    grad_own = input_kernel(
        gate_own, up_own, pre_own, gate_t, up_t, small_t, gain_own, pick, (grad_other,)
    )
    pieces = core_fold_kernel(grad_own.reshape(shape), swap(grad_other, "c").reshape(shape))
    both_axes = ("x", "y")
    sum_other = result_kernel(act_other, more_other, down, shared_down_t, pieces)
    sum_own = result_kernel(act_own, more_own, down, shared_down_t, (sum_other,))
    grad_expert_up, shared_up_back = weight_kernel(
        (up_own, up_other), (pre_own, pre_other), (ffn_own, ffn_other), 1, part, (sum_own,)
    )
    pieces = fold_first(pieces, both_axes, (grad_expert_up,))
    shape = (2, 2, zs * block, width)
    grad_expert_down, shared_down_back = weight_kernel(
        (act_own, act_other), (more_own, more_other), (grads_own, grads_other), 0, part, pieces
    )
    grad_slab = fold_second(pieces, both_axes, zs, (grad_expert_down,))
    routed_pieces = core_fold_kernel(
        sum_own.reshape(shape), swap(sum_other, "c").reshape(shape), grad_slab
    )
    grad_expert_gate, shared_gate_back = weight_kernel(
        (gate_own, gate_other),
        (pre_own, pre_other),
        (ffn_own, ffn_other),
        0,
        part,
        tuple(routed_pieces),
    )
    routed_pieces = fold_first(routed_pieces, both_axes, (grad_expert_gate,))
    ffn_grad = fold_z(grad_slab, jnp.float32, routed_pieces)
    share_grad = ffn_grad[:, width : width + experts]
    ffn_grad = ffn_grad[:, :width]
    logit_grad = shares * (share_grad - jnp.sum(shares * share_grad, axis=-1, keepdims=True))
    ffn_grad = ffn_grad + dot_nt(low(logit_grad), full_router)
    grad_router = dot_tn(ffn_low, low(logit_grad))
    hidden_part, grad_norm_ffn = root_norm_back(ffn_grad, unit_ffn, inverse_ffn, full_norm_ffn)
    grad_hidden = grad_mine.astype(jnp.float32) + hidden_part

    hidden_low = low(grad_hidden)
    attention_grad = gather_slab(hidden_low)
    shared_back = jnp.concatenate(
        [
            shared_gate_back[:shared_here],
            shared_up_back[:shared_here],
            shared_down_back[:shared_here],
        ]
    )
    shared_back = trade(
        jnp.transpose(shared_back.reshape(-1, count, rows_here), (1, 0, 2)), CTX
    )
    zero = jnp.zeros((1,), jnp.int32)
    (out_grads,) = out_grads_kernel(zero, 1, head_out, attention_grad, rows_here)
    key_own, key_other, query_grad, grad_up_here = attend_back_kernel(
        attention_grad,
        query_low,
        keys_own,
        keys_other,
        up_here,
        out_here,
        prob,
        absorbed,
        latent_out,
        heads,
        scale,
        (out_grads,),
    )
    rope = query_grad[:, heads * DN :].reshape(sequences, slab, heads, DR)
    rope = rotate(rope, cosine[:, None, :], -sine[:, None, :]).reshape(sequences * slab, -1)
    query_raw_grad = low(jnp.concatenate([query_grad[:, : heads * DN], rope], axis=1))
    query_grads = query_grads_kernel(
        query_raw_grad, input_low, grad_up_here, out_grads, rows_here
    )
    grad_heads = lax.psum_scatter(query_grads, "z", scatter_dimension=0, tiled=True)
    key_pieces = core_fold_kernel(key_own, swap(key_other, "c"), (query_grads, shared_back))
    input_grad = scatter_slab(
        *split_product_kernel(query_raw_grad, query_here, sequences, (query_grads,))
    )
    key_slab = fold_second(fold_first(key_pieces, ("y", "x")), ("y", "x"), zs)
    key_sum = fold_z(key_slab)
    routed_slab = fold_second(routed_pieces, both_axes, zs, (key_sum,))
    latent_back, grad_latent_norm = root_norm_back(
        key_sum[:, :R], latent_unit, latent_inverse, full_latent_norm
    )
    rope_key = rotate(key_sum[:, R:], cosine[:block], -sine[:block])
    latent_raw_grad = low(jnp.concatenate([latent_back, rope_key], axis=-1))
    slab_latent_grad = gather_slab(latent_raw_grad)
    down_grads = latent_grads_kernel(
        z[None], (2 * x + c)[None], zs, input_low, slab_latent_grad, rows_here
    )
    grad_down = fold_z(down_grads)
    latent_raw_grad = tie(latent_raw_grad, down_grads[0])
    shared_back = shared_back.astype(jnp.float32)
    grad_shared_gate = shared_back[:, :shared_here].reshape(-1, rows_here).T
    grad_shared_up = shared_back[:, shared_here : 2 * shared_here].reshape(-1, rows_here).T
    grad_shared_down = shared_back[:, 2 * shared_here :].reshape(-1, rows_here)


    output = both_halves(low(hidden_in + fold_z(routed_slab, jnp.float32, (grad_down,))))
    latent_input = jnp.stack([dot_nt(latent_raw_grad, down) for down in down_pieces])
    latent_input = latent_input.reshape(2, 2, block, zs, rows_here)
    latent_input = by_own(by_own(latent_input, "c", 0), "x", 1)
    input_grad = input_grad + jnp.transpose(latent_input, (2, 3, 1, 0, 4)).reshape(block, width)
    source_part, grad_norm_in = root_norm_back(
        input_grad, unit_in[:block], inverse_in[:block], full_norm_in
    )
    tokens_gradient = both_halves(low(grad_hidden + source_part)).astype(jnp.float32)

    traded = trade(grad_heads, ("x", "c"))
    both = traded.astype(jnp.float32)
    out_at = both.shape[2] - head_rows
    grad_output = jnp.transpose(
        both[..., out_at:].reshape(4, DV, heads, rows_here), (0, 2, 1, 3)
    ).reshape(-1, rows_here)
    grad_query = jnp.transpose(both[..., :query_columns], (1, 0, 2))
    grad_query = jnp.concatenate(
        [
            grad_query[..., : heads * DN].reshape(rows_here, 4, heads, DN),
            grad_query[..., heads * DN :].reshape(rows_here, 4, heads, DR),
        ],
        axis=-1,
    ).reshape(rows_here, -1)
    grad_latent_up = jnp.transpose(
        both[..., query_columns:out_at].reshape(4, up_columns // 128, rank_rows, 128), (2, 0, 1, 3)
    ).reshape(rank_rows, -1)

    small_grads = jnp.concatenate(
        [
            grad_router.T.reshape(experts, count, rows_here),
            grad_norm_in.reshape(1, count, rows_here),
            grad_norm_ffn.reshape(1, count, rows_here),
            jnp.pad(
                grad_latent_norm.reshape(1, count, rank_rows),
                ((0, 0), (0, 0), (0, rows_here - rank_rows)),
            ),
        ]
    )
    small_grads = trade(jnp.transpose(small_grads, (1, 0, 2)), CTX)
    small_grads = jnp.sum(small_grads, axis=0)
    small_grads = small_grads + swap(small_grads, "y")
    return (
        output,
        tokens_gradient,
        small_grads[experts],
        grad_query,
        grad_down,
        small_grads[experts + 2, :rank_rows],
        grad_latent_up,
        grad_output,
        small_grads[experts + 1],
        small_grads[:experts].T,
        grad_shared_gate,
        grad_shared_up,
        grad_shared_down,
        grad_expert_gate.T[None],
        grad_expert_up.T[None],
        grad_expert_down[None],
    )


IN_SPECS = (
    (None, "ctx", None),
    ("ctx",),
    ("ctx", "wa"),
    ("ctx", None),
    ("ctx",),
    ("ctx", "wa"),
    ("wa", "ctx"),
    ("ctx",),
    ("ctx", None),
    ("ctx", "wa"),
    ("ctx", "wa"),
    ("wa", "ctx"),
    ("ctx", None, "wa"),
    ("ctx", None, "wa"),
    ("ctx", "wa", None),
    (None, "ctx", None),
    (None, "ctx", None),
)
OUT_SPECS = ((None, "ctx", None),) * 2 + IN_SPECS[1:15]


def solution(mesh):
    count = mesh.shape["ctx"]

    def run(*arguments):
        experts = arguments[12].shape[0]
        if experts > 4 * TOPK or experts != count or mesh.shape["wa"] != 2 or count % 8:
            return jax.shard_map(
                shards,
                mesh=mesh,
                in_specs=tuple(P(*spec) for spec in IN_SPECS),
                out_specs=tuple(P(*spec) for spec in OUT_SPECS),
                check_vma=False,
            )(*arguments)
        grid = Mesh(mesh.devices.reshape(count // 4, 2, 2, 2), ("z", "x", "c", "y"))
        names = {"ctx": CTX, "wa": "y", None: None}
        return jax.shard_map(
            dense_shards,
            mesh=grid,
            in_specs=tuple(P(*[names[n] for n in spec]) for spec in IN_SPECS),
            out_specs=tuple(P(*[names[n] for n in spec]) for spec in OUT_SPECS),
            check_vma=False,
        )(*arguments)

    return run
```

```python
from functools import partial

import jax
import jax.numpy as jnp
from jax import lax
from jax.experimental import pallas as pl
from jax.experimental.layout import Layout, with_layout_constraint
from jax.experimental.pallas import tpu as pltpu
from jax.sharding import Mesh, PartitionSpec as P

DN = 128
DR = 64
DV = 128
R = 512
TOPK = 6


epsilon = 1e-06
highest = lax.Precision.HIGHEST


def shifted(value, axis, steps):
    count = lax.axis_size(axis)
    pairs = [(source, (source + steps) % count) for source in range(count)]
    return lax.ppermute(value, axis, pairs)


def root_norm(values, gain):
    inverse = lax.rsqrt(jnp.mean(values * values, axis=-1, keepdims=True) + epsilon)
    unit = values * inverse
    return (unit * gain, unit, inverse)


def root_norm_back(upstream, unit, inverse, gain):
    scaled = upstream * gain
    inner = jnp.mean(scaled * unit, axis=-1, keepdims=True)
    leading = tuple(range(upstream.ndim - 1))
    return (inverse * (scaled - unit * inner), jnp.sum(upstream * unit, axis=leading))


def rotary_tables(positions, width):
    half = width // 2
    frequency = 10000.0 ** (-jnp.arange(half, dtype=jnp.float32) * 2.0 / width)
    angle = positions.astype(jnp.float32)[:, None] * frequency[None, :]
    return (jnp.cos(angle), jnp.sin(angle))


def rotate(values, cosine, sine):
    half = values.shape[-1] // 2
    first = values[..., :half]
    second = values[..., half:]
    return jnp.concatenate(
        [first * cosine - second * sine, second * cosine + first * sine], axis=-1
    )


def silu_slope(values):
    sigmoid = jax.nn.sigmoid(values)
    return sigmoid * (1.0 + values * (1.0 - sigmoid))


def fetch_weights(
    norm_in,
    query_weight,
    latent_down,
    latent_norm,
    latent_up,
    output_weight,
    norm_ffn,
    router_weight,
    shared_gate,
    shared_up,
    shared_down,
):
    return (
        lax.all_gather(norm_in, "ctx", axis=0, tiled=True),
        lax.all_gather(query_weight, "ctx", axis=0, tiled=True),
        lax.all_gather(latent_down, "ctx", axis=0, tiled=True),
        lax.all_gather(latent_norm, "ctx", axis=0, tiled=True),
        lax.all_gather(latent_up, "ctx", axis=0, tiled=True),
        lax.all_gather(output_weight, "ctx", axis=1, tiled=True),
        lax.all_gather(norm_ffn, "ctx", axis=0, tiled=True),
        lax.all_gather(router_weight, "ctx", axis=0, tiled=True),
        lax.all_gather(shared_gate, "ctx", axis=0, tiled=True),
        lax.all_gather(shared_up, "ctx", axis=0, tiled=True),
        lax.all_gather(shared_down, "ctx", axis=1, tiled=True),
    )


def shards(
    tokens,
    norm_in,
    query_weight,
    latent_down,
    latent_norm,
    latent_up,
    output_weight,
    norm_ffn,
    router_weight,
    shared_gate,
    shared_up,
    shared_down,
    expert_gate,
    expert_up,
    expert_down,
    routes,
    cotangent,
):
    context_count = lax.axis_size("ctx")
    context_index = lax.axis_index("ctx")
    lead = (lax.axis_index("wa") == 0).astype(jnp.float32)
    sequences, block, width = tokens.shape
    local_experts = expert_gate.shape[0]
    experts = context_count * local_experts
    capacity = max(2, block * TOPK * 4 // (3 * experts))
    scale = (DN + DR) ** (-0.5)
    gathered = fetch_weights(
        norm_in,
        query_weight,
        latent_down,
        latent_norm,
        latent_up,
        output_weight,
        norm_ffn,
        router_weight,
        shared_gate,
        shared_up,
        shared_down,
    )
    (
        full_norm_in,
        full_query,
        full_down,
        full_latent_norm,
        full_up,
        full_output,
        full_norm_ffn,
        full_router,
        full_shared_gate,
        full_shared_up,
        full_shared_down,
    ) = gathered
    heads_here = full_up.shape[1] // (DN + DV)
    positions = context_index * block + jnp.arange(block)
    cosine, sine = rotary_tables(positions, DR)
    source = tokens.astype(jnp.float32)
    normed_in, unit_in, inverse_in = root_norm(source, full_norm_in.astype(jnp.float32))
    input_low = normed_in.astype(jnp.bfloat16)
    query_raw = jnp.dot(input_low, full_query, preferred_element_type=jnp.float32).reshape(
        sequences, block, heads_here, DN + DR
    )
    query_low = jnp.concatenate(
        [query_raw[..., :DN], rotate(query_raw[..., DN:], cosine[:, None, :], sine[:, None, :])],
        axis=-1,
    ).astype(jnp.bfloat16)
    up_view = full_up.reshape(R, heads_here, DN + DV)
    key_up = up_view[..., :DN]
    value_up = up_view[..., DN:]
    absorbed = jnp.einsum(
        "sbhn,rhn->shbr", query_low[..., :DN], key_up, preferred_element_type=jnp.float32
    )
    query_rows = jnp.concatenate(
        [absorbed.astype(jnp.bfloat16), jnp.transpose(query_low[..., DN:], (0, 2, 1, 3))], axis=-1
    )
    latent_raw = jnp.dot(input_low, full_down, preferred_element_type=jnp.float32)
    latent_scaled, latent_unit, latent_inverse = root_norm(
        latent_raw[..., :R], full_latent_norm.astype(jnp.float32)
    )
    key_rows = jnp.concatenate(
        [latent_scaled, rotate(latent_raw[..., R:], cosine, sine)], axis=-1
    ).astype(jnp.bfloat16)
    piece = lax.all_gather(key_rows, "ctx", axis=1, tiled=True)
    top = jnp.full((sequences, heads_here, block), -1e30, jnp.float32)
    scores = (
        jnp.einsum("shqc,skc->shqk", query_rows, piece, preferred_element_type=jnp.float32) * scale
    )
    key_positions = jnp.arange(piece.shape[1])
    allowed = positions[:, None] >= key_positions[None, :]
    scores = jnp.where(allowed, scores, -1e30)
    new_top = jnp.maximum(top, jnp.max(scores, axis=-1))
    weights = jnp.where(allowed, jnp.exp(scores - new_top[..., None]), 0.0)
    total = jnp.sum(weights, axis=-1)
    weights_high = weights.astype(jnp.bfloat16)
    weights_rest = (weights - weights_high.astype(jnp.float32)).astype(jnp.bfloat16)
    running = jnp.einsum(
        "shqk,skr->shqr", weights_high, piece[..., :R], preferred_element_type=jnp.float32
    )
    remainder = jnp.einsum(
        "shqk,skr->shqr", weights_rest, piece[..., :R], preferred_element_type=jnp.float32
    )
    top, total, running, remainder = (new_top, total, running, remainder)
    log_total = top + jnp.log(total)
    latent_out = (running / total[..., None]).astype(jnp.bfloat16)
    latent_exact = (running + remainder) / total[..., None]
    head_out = (
        jnp.einsum("shbr,rhv->sbhv", latent_out, value_up, preferred_element_type=jnp.float32)
        .astype(jnp.bfloat16)
        .reshape(sequences, block, heads_here * DV)
    )
    attention_part = jnp.dot(head_out, full_output, preferred_element_type=jnp.float32)
    hidden_in = source + lax.psum(attention_part, "wa")
    normed_ffn, unit_ffn, inverse_ffn = root_norm(hidden_in, full_norm_ffn.astype(jnp.float32))
    ffn_low = normed_ffn.astype(jnp.bfloat16)
    shares = jax.nn.softmax(
        jnp.dot(ffn_low, full_router, preferred_element_type=jnp.float32), axis=-1
    )
    shared_g = jnp.dot(ffn_low, full_shared_gate, preferred_element_type=jnp.float32)
    shared_u = jnp.dot(ffn_low, full_shared_up, preferred_element_type=jnp.float32)
    shared_silu = jax.nn.silu(shared_g)
    shared_activation = (shared_silu * shared_u).astype(jnp.bfloat16)
    shared_part = jnp.dot(shared_activation, full_shared_down, preferred_element_type=jnp.float32)
    expert_ids = jnp.arange(experts, dtype=jnp.int32)
    chosen = (
        (routes[..., None] == expert_ids)
        .astype(jnp.int32)
        .reshape(sequences, block * TOPK, experts)
    )
    earlier = jnp.cumsum(chosen, axis=1) - chosen
    slot_of = jnp.sum(earlier * chosen, axis=-1).reshape(sequences, block, TOPK)
    slot_ids = jnp.arange(capacity, dtype=jnp.int32)
    hit = (routes[None, :, :, :, None] == expert_ids[:, None, None, None, None]) & (
        slot_of[None, :, :, :, None] == slot_ids[None, None, None, None, :]
    )
    dispatch = jnp.transpose(jnp.any(hit, axis=3), (0, 1, 3, 2)).astype(jnp.float32)
    send = (
        jnp.einsum(
            "escb,sbd->escd",
            dispatch.astype(jnp.bfloat16),
            ffn_low,
            preferred_element_type=jnp.float32,
        )
        .astype(jnp.bfloat16)
        .reshape(experts, sequences * capacity, width)
    )
    slot_share = jnp.einsum("escb,sbe->esc", dispatch, shares, precision=highest)
    received = lax.all_to_all(send, "ctx", split_axis=0, concat_axis=0, tiled=True)
    count = received.shape[1]
    rows = received.reshape(context_count, local_experts, count, width)
    gate_pre = jnp.einsum("nesd,edf->nesf", rows, expert_gate, preferred_element_type=jnp.float32)
    up_pre = jnp.einsum("nesd,edf->nesf", rows, expert_up, preferred_element_type=jnp.float32)
    activation = (jax.nn.silu(gate_pre) * up_pre).astype(jnp.bfloat16)
    result = jnp.einsum(
        "nesf,efd->nesd", activation, expert_down, preferred_element_type=jnp.float32
    ).reshape(experts, count, width)
    returned = lax.all_to_all(result, "ctx", split_axis=0, concat_axis=0, tiled=True)
    hidden_units = gate_pre.shape[-1]
    returned, received, gate_keep, up_keep = (
        returned,
        received,
        gate_pre.reshape(experts, count, hidden_units),
        up_pre.reshape(experts, count, hidden_units),
    )
    returned = returned.reshape(experts, sequences, capacity, width)
    routed_part = jnp.einsum(
        "escb,escd->sbd", dispatch, returned * slot_share[..., None], precision=highest
    )
    output = hidden_in + lax.psum(shared_part + routed_part, "wa")
    gathered = fetch_weights(
        norm_in,
        query_weight,
        latent_down,
        latent_norm,
        latent_up,
        output_weight,
        norm_ffn,
        router_weight,
        shared_gate,
        shared_up,
        shared_down,
    )
    (
        full_norm_in,
        full_query,
        full_down,
        full_latent_norm,
        full_up,
        full_output,
        full_norm_ffn,
        full_router,
        full_shared_gate,
        full_shared_up,
        full_shared_down,
    ) = gathered
    up_view = full_up.reshape(R, heads_here, DN + DV)
    key_up = up_view[..., :DN]
    value_up = up_view[..., DN:]
    grad_y = cotangent.astype(jnp.float32)
    shared_grad = jnp.einsum(
        "sbd,fd->sbf", cotangent, full_shared_down, preferred_element_type=jnp.float32
    )
    shared_gate_grad = (shared_grad * shared_u * silu_slope(shared_g)).astype(jnp.bfloat16)
    shared_up_grad = (shared_grad * shared_silu).astype(jnp.bfloat16)
    grad_shared_down = jnp.einsum(
        "sbf,sbd->fd", shared_activation, cotangent, preferred_element_type=jnp.float32
    )
    grad_shared_gate = jnp.einsum(
        "sbd,sbf->df", ffn_low, shared_gate_grad, preferred_element_type=jnp.float32
    )
    grad_shared_up = jnp.einsum(
        "sbd,sbf->df", ffn_low, shared_up_grad, preferred_element_type=jnp.float32
    )
    ffn_grad = jnp.einsum(
        "sbf,df->sbd", shared_gate_grad, full_shared_gate, preferred_element_type=jnp.float32
    )
    ffn_grad = ffn_grad + jnp.einsum(
        "sbf,df->sbd", shared_up_grad, full_shared_up, preferred_element_type=jnp.float32
    )
    grad_at_slots = jnp.einsum("escb,sbd->escd", dispatch, grad_y, precision=highest)
    slot_grads = (
        (grad_at_slots * slot_share[..., None])
        .astype(jnp.bfloat16)
        .reshape(experts, sequences * capacity, width)
    )
    slot_dot = jnp.sum(returned * grad_at_slots, axis=-1)
    share_grad = jnp.einsum("escb,esc->sbe", dispatch, slot_dot, precision=highest)
    logit_grad = shares * (share_grad - jnp.sum(shares * share_grad, axis=-1, keepdims=True))
    grad_router = jnp.einsum(
        "sbd,sbe->de", ffn_low.astype(jnp.float32), logit_grad, precision=highest
    )
    ffn_grad = ffn_grad + jnp.einsum(
        "sbe,de->sbd", logit_grad, full_router.astype(jnp.float32), precision=highest
    )
    slot_back = lax.all_to_all(slot_grads, "ctx", split_axis=0, concat_axis=0, tiled=True).reshape(
        context_count, local_experts, -1, width
    )
    rows = received.reshape(context_count, local_experts, -1, width)
    gate_pre = gate_keep.reshape(context_count, local_experts, -1, gate_keep.shape[-1])
    up_pre = up_keep.reshape(context_count, local_experts, -1, up_keep.shape[-1])
    hidden_grad = jnp.einsum(
        "nesd,efd->nesf", slot_back, expert_down, preferred_element_type=jnp.float32
    )
    silu_gate = jax.nn.silu(gate_pre)
    gate_grad = (hidden_grad * up_pre * silu_slope(gate_pre)).astype(jnp.bfloat16)
    up_grad = (hidden_grad * silu_gate).astype(jnp.bfloat16)
    activation = (silu_gate * up_pre).astype(jnp.bfloat16)
    grad_expert_down = jnp.einsum(
        "nesf,nesd->efd", activation, slot_back, preferred_element_type=jnp.float32
    )
    grad_expert_gate = jnp.einsum(
        "nesd,nesf->edf", rows, gate_grad, preferred_element_type=jnp.float32
    )
    grad_expert_up = jnp.einsum("nesd,nesf->edf", rows, up_grad, preferred_element_type=jnp.float32)
    rows_grad = jnp.einsum(
        "nesf,edf->nesd", gate_grad, expert_gate, preferred_element_type=jnp.float32
    )
    rows_grad = rows_grad + jnp.einsum(
        "nesf,edf->nesd", up_grad, expert_up, preferred_element_type=jnp.float32
    )
    slot_grad = lax.all_to_all(
        rows_grad.reshape(experts, -1, width), "ctx", split_axis=0, concat_axis=0, tiled=True
    ).reshape(experts, sequences, capacity, width)
    ffn_grad = ffn_grad + jnp.einsum("escb,escd->sbd", dispatch, slot_grad, precision=highest)
    hidden_part, grad_norm_ffn = root_norm_back(
        ffn_grad, unit_ffn, inverse_ffn, full_norm_ffn.astype(jnp.float32)
    )
    grad_hidden = grad_y + lax.psum(hidden_part, "wa")
    attention_grad = grad_hidden.astype(jnp.bfloat16)
    grad_output = jnp.einsum(
        "sbk,sbd->kd", head_out, attention_grad, preferred_element_type=jnp.float32
    )
    head_grad = (
        jnp.einsum("sbd,kd->sbk", attention_grad, full_output, preferred_element_type=jnp.float32)
        .astype(jnp.bfloat16)
        .reshape(sequences, block, heads_here, DV)
    )
    grad_value_up = jnp.einsum(
        "shbr,sbhv->rhv", latent_out, head_grad, preferred_element_type=jnp.float32
    )
    latent_out_grad = jnp.einsum(
        "sbhv,rhv->shbr", head_grad, value_up, preferred_element_type=jnp.float32
    ).astype(jnp.bfloat16)
    row_dot = jnp.sum(latent_out_grad.astype(jnp.float32) * latent_exact, axis=-1)

    def turn_body(turn, carry):
        keys_here, key_grad, query_grad = carry
        source_index = (context_index + turn) % context_count
        key_positions = source_index * block + jnp.arange(block)
        allowed = positions[:, None] >= key_positions[None, :]
        scores = (
            jnp.einsum("shqc,skc->shqk", query_rows, keys_here, preferred_element_type=jnp.float32)
            * scale
        )
        weights = jnp.where(allowed[None, None], jnp.exp(scores - log_total[..., None]), 0.0)
        weight_grad = jnp.einsum(
            "shqr,skr->shqk",
            latent_out_grad,
            keys_here[..., :R],
            preferred_element_type=jnp.float32,
        )
        score_grad = (weights * (weight_grad - row_dot[..., None])).astype(jnp.bfloat16)
        query_grad = (
            query_grad
            + jnp.einsum(
                "shqk,skc->shqc", score_grad, keys_here, preferred_element_type=jnp.float32
            )
            * scale
        )
        key_part = (
            jnp.einsum("shqk,shqc->skc", score_grad, query_rows, preferred_element_type=jnp.float32)
            * scale
        )
        value_part = jnp.einsum(
            "shqk,shqr->skr",
            weights.astype(jnp.bfloat16),
            latent_out_grad,
            preferred_element_type=jnp.float32,
        )
        key_grad = key_grad + key_part + jnp.pad(value_part, ((0, 0), (0, 0), (0, DR)))
        keys_next = shifted(keys_here, "ctx", -1)
        grad_next = shifted(key_grad, "ctx", -1)
        return (keys_next, grad_next, query_grad)

    start_back = (
        key_rows,
        jnp.zeros((sequences, block, R + DR), jnp.float32),
        jnp.zeros((sequences, heads_here, block, R + DR), jnp.float32),
    )
    unused_keys, key_grad, query_grad = lax.fori_loop(0, context_count, turn_body, start_back)
    key_grad_total = lax.psum(key_grad, "wa")
    query_grad_low = query_grad.astype(jnp.bfloat16)
    absorbed_grad = query_grad_low[..., :R]
    rope_query_grad = jnp.transpose(query_grad_low[..., R:], (0, 2, 1, 3)).astype(jnp.float32)
    grad_key_up = jnp.einsum(
        "shbr,sbhn->rhn", absorbed_grad, query_low[..., :DN], preferred_element_type=jnp.float32
    )
    nope_grad = jnp.einsum(
        "shbr,rhn->sbhn", absorbed_grad, key_up, preferred_element_type=jnp.float32
    )
    rope_raw_grad = rotate(rope_query_grad, cosine[:, None, :], -sine[:, None, :])
    query_raw_grad = (
        jnp.concatenate([nope_grad, rope_raw_grad], axis=-1)
        .astype(jnp.bfloat16)
        .reshape(sequences, block, heads_here * (DN + DR))
    )
    grad_query = jnp.einsum(
        "sbd,sbk->dk", input_low, query_raw_grad, preferred_element_type=jnp.float32
    )
    input_part = jnp.einsum(
        "sbk,dk->sbd", query_raw_grad, full_query, preferred_element_type=jnp.float32
    )
    grad_latent_up = jnp.concatenate([grad_key_up, grad_value_up], axis=-1).reshape(
        R, heads_here * (DN + DV)
    )
    latent_grad, grad_latent_norm = root_norm_back(
        key_grad_total[..., :R], latent_unit, latent_inverse, full_latent_norm.astype(jnp.float32)
    )
    rope_key_grad = rotate(key_grad_total[..., R:], cosine, -sine)
    latent_raw_grad = jnp.concatenate([latent_grad, rope_key_grad], axis=-1).astype(jnp.bfloat16)
    grad_down = jnp.einsum(
        "sbd,sbc->dc", input_low, latent_raw_grad, preferred_element_type=jnp.float32
    )
    input_part = input_part + lead * jnp.einsum(
        "sbc,dc->sbd", latent_raw_grad, full_down, preferred_element_type=jnp.float32
    )
    source_part, grad_norm_in = root_norm_back(
        input_part, unit_in, inverse_in, full_norm_in.astype(jnp.float32)
    )
    summed = lax.psum((source_part, grad_norm_in, grad_norm_ffn, grad_router), "wa")
    tokens_gradient = grad_hidden + summed[0]
    reduced = (
        lax.psum_scatter(summed[1], "ctx", scatter_dimension=0, tiled=True),
        lax.psum_scatter(grad_query, "ctx", scatter_dimension=0, tiled=True),
        lax.psum_scatter(grad_down, "ctx", scatter_dimension=0, tiled=True),
        lax.psum_scatter(grad_latent_norm, "ctx", scatter_dimension=0, tiled=True),
        lax.psum_scatter(grad_latent_up, "ctx", scatter_dimension=0, tiled=True),
        lax.psum_scatter(grad_output, "ctx", scatter_dimension=1, tiled=True),
        lax.psum_scatter(summed[2], "ctx", scatter_dimension=0, tiled=True),
        lax.psum_scatter(summed[3], "ctx", scatter_dimension=0, tiled=True),
        lax.psum_scatter(grad_shared_gate, "ctx", scatter_dimension=0, tiled=True),
        lax.psum_scatter(grad_shared_up, "ctx", scatter_dimension=0, tiled=True),
        lax.psum_scatter(grad_shared_down, "ctx", scatter_dimension=1, tiled=True),
    )
    return (
        output.astype(jnp.bfloat16),
        tokens_gradient,
        reduced[0],
        reduced[1],
        reduced[2],
        reduced[3],
        reduced[4],
        reduced[5],
        reduced[6],
        reduced[7],
        reduced[8],
        reduced[9],
        reduced[10],
        grad_expert_gate,
        grad_expert_up,
        grad_expert_down,
    )


VMEM_LIMIT = 60 * 1024 * 1024
TILE = 256


def local_call(body, grid, in_specs, out_specs, out_shape, operands, after=()):
    inputs = len(in_specs)

    def run(*refs):
        body(*refs[:inputs], *refs[inputs + len(after) :])

    return pl.pallas_call(
        run,
        grid=grid,
        in_specs=list(in_specs) + [pl.BlockSpec(memory_space=pl.ANY)] * len(after),
        out_specs=out_specs,
        out_shape=out_shape,
        compiler_params=pltpu.CompilerParams(vmem_limit_bytes=VMEM_LIMIT),
        cost_estimate=pl.CostEstimate(flops=1, bytes_accessed=1, transcendentals=0),
    )(*operands, *after)


def whole(array):
    return pl.BlockSpec(array.shape, lambda *_: (0,) * array.ndim)


def by_rows(array, rows=TILE):
    return pl.BlockSpec((rows, array.shape[1]), lambda i: (i, 0))


def by_first(array):
    return pl.BlockSpec((1,) + array.shape[1:], lambda i: (i,) + (0,) * (array.ndim - 1))


def shaped(shape, dtype=jnp.bfloat16):
    return jax.ShapeDtypeStruct(shape, dtype)


def mul(left, right):
    return jnp.dot(left, right, preferred_element_type=jnp.float32)


def mul_nt(left, right):
    return lax.dot_general(
        left, right, (((1,), (1,)), ((), ())), preferred_element_type=jnp.float32
    )


def mul_tn(left, right):
    return lax.dot_general(
        left, right, (((0,), (0,)), ((), ())), preferred_element_type=jnp.float32
    )


def glu_back(gate, up, grads):
    sigmoid = 1.0 / (1.0 + jnp.exp(-gate))
    silu = gate * sigmoid
    slope = sigmoid * (1.0 + gate * (1.0 - sigmoid))
    return (silu * up, grads * up * slope, grads * silu)


def feed_body(
    experts, rows, back, shared_back, gate_t, up_t, small_t, named, pick,
    act_out, shared_act_out, gate_out, up_out, shared_out, gain_out,
):
    here = rows[...]
    part = small_t.shape[0] // 3
    small = mul_nt(here, small_t[...])
    logits = small[:, 2 * part :]
    ids = lax.broadcasted_iota(jnp.int32, logits.shape, 1)
    logits = jnp.where(ids < experts, logits, -1e30)
    chances = jnp.exp(logits - jnp.max(logits, axis=1, keepdims=True))
    total = jnp.sum(chances, axis=1, keepdims=True)
    named_here = named[...]
    share = jnp.sum(chances * pick[...], axis=1, keepdims=True) / total * named_here
    act, gate_grad, up_grad = glu_back(
        small[:, :part], small[:, part : 2 * part], shared_back[...].astype(jnp.float32)
    )
    shared_act_out[...] = act.astype(jnp.bfloat16)
    shared_out[:, :part] = gate_grad.astype(jnp.bfloat16)
    shared_out[:, part:] = up_grad.astype(jnp.bfloat16)
    grads = back[...].astype(jnp.float32)
    act, gate_grad, up_grad = glu_back(mul_nt(here, gate_t[...]), mul_nt(here, up_t[...]), grads)
    gain_out[...] = jnp.sum(act * grads, axis=1, keepdims=True) * named_here
    act_out[...] = (act * share).astype(jnp.bfloat16)
    gate_out[...] = (gate_grad * share).astype(jnp.bfloat16)
    up_out[...] = (up_grad * share).astype(jnp.bfloat16)


def feed_kernel(rows, back, shared_back, gate_t, up_t, small_t, named, pick, experts, after=()):
    count = rows.shape[0]
    hidden, part = (back.shape[1], shared_back.shape[1])
    shapes = [shaped((count, s)) for s in (hidden, part, hidden, hidden, 2 * part)]
    shapes.append(shaped((count, 1), jnp.float32))
    return local_call(
        partial(feed_body, experts),
        (count // TILE,),
        [
            by_rows(rows),
            by_rows(back),
            by_rows(shared_back),
            whole(gate_t),
            whole(up_t),
            whole(small_t),
            by_rows(named),
            whole(pick),
        ],
        [by_rows(s) for s in shapes],
        shapes,
        (rows, back, shared_back, gate_t, up_t, small_t, named, pick),
        after,
    )


def input_body(gate, up, shared, gate_t, up_t, small_t, gain, pick, out):
    width = gate_t.shape[1]
    used = shared.shape[1]
    out[:, :width] = (
        mul(gate[...], gate_t[...]) + mul(up[...], up_t[...]) + mul(shared[...], small_t[:used, :])
    ).astype(jnp.bfloat16)
    out[:, width:] = (gain[...] * pick[...]).astype(jnp.bfloat16)


def input_kernel(gate, up, shared, gate_t, up_t, small_t, gain, pick, after=()):
    count = gate.shape[0]
    shape = shaped((count, gate_t.shape[1] + pick.shape[1]))
    return local_call(
        input_body,
        (count // TILE,),
        [by_rows(gate), by_rows(up), by_rows(shared)]
        + [whole(gate_t), whole(up_t), whole(small_t), by_rows(gain), whole(pick)],
        by_rows(shape),
        shape,
        (gate, up, shared, gate_t, up_t, small_t, gain, pick),
        after,
    )


def result_body(act, shared_act, down, shared_down, out):
    out[...] = (mul(act[...], down[...]) + mul(shared_act[...], shared_down[...])).astype(
        jnp.bfloat16
    )


def result_kernel(act, shared_act, down, shared_down, after=()):
    count = act.shape[0]
    shape = shaped((count, down.shape[1]))
    return local_call(
        result_body,
        (count // TILE,),
        [by_rows(act), by_rows(shared_act), whole(down), whole(shared_down)],
        by_rows(shape),
        shape,
        (act, shared_act, down, shared_down),
        after,
    )


def weight_body(left_own, left_other, more_own, more_other, own, other, out, more_out):
    here, there = (own[...], other[...])
    out[...] = mul_tn(left_own[...], here) + mul_tn(left_other[...], there)
    more_out[...] = (mul_tn(more_own[...], here) + mul_tn(more_other[...], there)).astype(
        jnp.bfloat16
    )


def weight_kernel(lefts, mores, rights, side=0, part=128, after=()):
    count, width = rights[0].shape
    columns = lambda rows: pl.BlockSpec((rows, TILE), lambda i: (0, i))
    hidden, more = (lefts[0].shape[1], part)
    return local_call(
        weight_body,
        (width // TILE,),
        [whole(a) for a in lefts]
        + [pl.BlockSpec((count, part), lambda i: (0, side))] * 2
        + [columns(count)] * 2,
        [columns(hidden), columns(more)],
        [shaped((hidden, width), jnp.float32), shaped((more, width))],
        (*lefts, *mores, *rights),
        after,
    )


def head_parts_of(query, heads, nope):
    rope = query.shape[1] // heads - nope
    return [
        (
            query[:, k * nope : (k + 1) * nope],
            query[:, heads * nope + k * rope : heads * nope + (k + 1) * rope],
        )
        for k in range(heads)
    ]


def attend_body(
    heads, scale, query, own, other, up, out_weight, spots, key_spots,
    kept_out, sent_out, prob_out, absorbed_out, latent_out, head_out,
):
    rank = up.shape[0]
    absorbed, ropes = ([], [])
    for k, (nope, rope) in enumerate(head_parts_of(query[...], heads, DN)):
        key_up = up[:, k * (DN + DV) : k * (DN + DV) + DN]
        absorbed.append(mul_nt(nope, key_up).astype(jnp.bfloat16))
        ropes.append(rope)
    absorbed = jnp.concatenate(absorbed, axis=0)
    rope = jnp.concatenate(ropes, axis=0)
    absorbed_out[0] = absorbed
    keys = [source[0, k] for source in (own, other) for k in range(2)]
    scores = jnp.concatenate(
        [mul_nt(absorbed, key[:, :rank]) + mul_nt(rope, key[:, rank:]) for key in keys], axis=1
    )
    allowed = spots[...] >= key_spots[...]
    allowed = jnp.concatenate([allowed] * heads, axis=0)
    scores = jnp.where(allowed, scores * scale, -1e30)
    weights = jnp.exp(scores - jnp.max(scores, axis=1, keepdims=True))
    prob = (weights / jnp.sum(weights, axis=1, keepdims=True)).astype(jnp.bfloat16)
    prob_out[0] = prob
    size = keys[0].shape[0]
    latent = sum(
        mul(prob[:, j * size : (j + 1) * size], key[:, :rank]) for j, key in enumerate(keys)
    ).astype(jnp.bfloat16)
    latent_out[0] = latent
    rows = query.shape[0]
    head = jnp.concatenate(
        [
            mul(
                latent[k * rows : (k + 1) * rows],
                up[:, k * (DN + DV) + DN : (k + 1) * (DN + DV)],
            )
            for k in range(heads)
        ],
        axis=1,
    ).astype(jnp.bfloat16)
    head_out[...] = head
    total = mul(head, out_weight[...]).astype(jnp.bfloat16)
    kept_out[0] = total[: rows // 2]
    sent_out[0] = total[rows // 2 :]


def attend_kernel(query, own, other, up, out_weight, spots, key_spots, heads, scale, after=()):
    sequences = own.shape[0]
    rows = query.shape[0] // sequences
    key_count = 4 * own.shape[2]
    rank = up.shape[0]
    shapes = [
        shaped((sequences, rows // 2, out_weight.shape[1])),
        shaped((sequences, rows // 2, out_weight.shape[1])),
        shaped((sequences, heads * rows, key_count)),
        shaped((sequences, heads * rows, rank)),
        shaped((sequences, heads * rows, rank)),
        shaped((query.shape[0], heads * DV)),
    ]
    return local_call(
        partial(attend_body, heads, scale),
        (sequences,),
        [by_rows(query, rows), by_first(own), by_first(other)]
        + [whole(a) for a in (up, out_weight, spots, key_spots)],
        [by_first(shape) for shape in shapes[:5]] + [by_rows(shapes[5], rows)],
        shapes,
        (query, own, other, up, out_weight, spots, key_spots),
        after,
    )


def attend_back_body(
    heads, scale, grads, query, own, other, up, out_weight, prob, absorbed, latent,
    own_out, other_out, query_out, up_out,
):
    rank = up.shape[0]
    rows = query.shape[0]
    first = pl.program_id(0) == 0
    grads_here = grads[...]
    head_grad = mul_nt(grads_here, out_weight[...]).astype(jnp.bfloat16)
    span = lambda k: slice(k * rows, (k + 1) * rows)
    latent_grad = []
    value_parts = []
    for k in range(heads):
        mine = head_grad[:, k * DV : (k + 1) * DV]
        value_up = up[:, k * (DN + DV) + DN : (k + 1) * (DN + DV)]
        latent_grad.append(mul_nt(mine, value_up).astype(jnp.bfloat16))
        value_parts.append(mul_tn(latent[0, span(k)], mine))
    latent_grad = jnp.concatenate(latent_grad, axis=0)
    keys = [source[0, k] for source in (own, other) for k in range(2)]
    size = keys[0].shape[0]
    prob_here = prob[0]
    prob_wide = prob_here.astype(jnp.float32)
    prob_grad = jnp.concatenate([mul_nt(latent_grad, key[:, :rank]) for key in keys], axis=1)
    inner = jnp.sum(prob_wide * prob_grad, axis=1, keepdims=True)
    score_grad = (prob_wide * (prob_grad - inner)).astype(jnp.bfloat16)
    absorbed_here = absorbed[0]
    parts = head_parts_of(query[...], heads, DN)
    rope = jnp.concatenate([part[1] for part in parts], axis=0)
    wide = 0.0
    narrow = 0.0
    for j, key in enumerate(keys):
        piece = score_grad[:, j * size : (j + 1) * size]
        wide = wide + mul(piece, key[:, :rank])
        narrow = narrow + mul(piece, key[:, rank:])
        target = (own_out, other_out)[j // 2]
        value = mul_tn(prob_here[:, j * size : (j + 1) * size], latent_grad)
        target[0, j % 2, :, :rank] = (mul_tn(piece, absorbed_here) * scale + value).astype(
            jnp.bfloat16
        )
        target[0, j % 2, :, rank:] = (mul_tn(piece, rope) * scale).astype(jnp.bfloat16)
    wide = (wide * scale).astype(jnp.bfloat16)
    narrow = narrow * scale
    for k in range(heads):
        start = k * (DN + DV)
        key_part = mul_tn(wide[span(k)], parts[k][0])
        up_out[:, start : start + DN] = (
            jnp.where(first, 0.0, up_out[:, start : start + DN]) + key_part
        )
        up_out[:, start + DN : start + DN + DV] = (
            jnp.where(first, 0.0, up_out[:, start + DN : start + DN + DV]) + value_parts[k]
        )
        query_out[:, k * DN : (k + 1) * DN] = mul(wide[span(k)], up[:, start : start + DN])
        rope_size = narrow.shape[1]
        at = heads * DN + k * rope_size
        query_out[:, at : at + rope_size] = narrow[span(k)]


def attend_back_kernel(
    grads, query, own, other, up, out_weight, prob, absorbed, latent, heads, scale, after=()
):
    sequences = own.shape[0]
    rows = query.shape[0] // sequences
    shapes = [
        shaped(own.shape),
        shaped(own.shape),
        shaped(query.shape, jnp.float32),
        shaped(up.shape, jnp.float32),
    ]
    return local_call(
        partial(attend_back_body, heads, scale),
        (sequences,),
        [by_rows(grads, rows), by_rows(query, rows), by_first(own), by_first(other)]
        + [whole(up), whole(out_weight), by_first(prob), by_first(absorbed), by_first(latent)],
        [by_first(own), by_first(own), by_rows(query, rows), whole(up)],
        shapes,
        (grads, query, own, other, up, out_weight, prob, absorbed, latent),
        after,
    )


def heads_body(parts, *refs):
    query_out, up_out, out_out = refs
    count, groups, rows, _ = parts.shape
    query_columns = query_out.shape[1]
    up_blocks = up_out.shape[1] // 128
    up_rows = rows // up_blocks
    heads = out_out.shape[0] // rows
    for block in range(count * groups):
        here = parts[block // groups, block % groups]
        span = slice(block * rows, (block + 1) * rows)
        query_out[span, :] = here[:, :query_columns]
        for k in range(up_blocks):
            up_out[block * up_rows : (block + 1) * up_rows, k * 128 : (k + 1) * 128] = here[
                k * up_rows : (k + 1) * up_rows, query_columns : query_columns + 128
            ]
        for k in range(heads):
            at = query_columns + 128 + k * rows
            out_out[k * rows : (k + 1) * rows, span] = here[:, at : at + rows]


def heads_kernel(parts, query_columns, heads, up_columns, after=()):
    count, groups, rows, _ = parts.shape
    width = count * groups * rows
    up_rows = rows * 128 // up_columns
    shapes = [
        shaped((width, query_columns)),
        shaped((count * groups * up_rows, up_columns)),
        shaped((heads * rows, width)),
    ]
    return local_call(
        heads_body,
        (1,),
        [whole(parts)],
        [whole(s) for s in shapes],
        shapes,
        (parts,),
        after,
    )


SCALAR = pl.BlockSpec(memory_space=pltpu.SMEM)


def out_grads_body(rows, z, head, grads, *outs):
    heads = head.shape[1] // rows
    for s, out in enumerate(outs):
        size = out.shape[0] * rows
        start = pl.multiple_of(lax.rem(z[0] + s, len(outs)) * size, size)
        total = mul_tn(head[...], grads[:, pl.ds(start, size)]).astype(jnp.bfloat16)
        for j in range(out.shape[0]):
            for k in range(heads):
                out[j, :, k * rows : (k + 1) * rows] = total[
                    k * rows : (k + 1) * rows, j * rows : (j + 1) * rows
                ]


def out_grads_kernel(z, count, head, grads, rows):
    shapes = [shaped((grads.shape[1] // (rows * count), rows, head.shape[1]))] * count
    return local_call(
        partial(out_grads_body, rows),
        (1,),
        [SCALAR, whole(head), whole(grads)],
        [whole(s) for s in shapes],
        shapes,
        (z, head, grads),
    )


def query_grads_body(rows, grads, source, up, more, out):
    columns = grads.shape[1]
    up_blocks = up.shape[1] // 128
    up_rows = rows // up_blocks
    here = grads[...]
    for i in range(out.shape[0]):
        span = slice(i * rows, (i + 1) * rows)
        out[i, :, :columns] = mul_tn(source[:, span], here).astype(jnp.bfloat16)
        for k in range(up_blocks):
            out[i, k * up_rows : (k + 1) * up_rows, columns : columns + 128] = up[
                i * up_rows : (i + 1) * up_rows, k * 128 : (k + 1) * 128
            ].astype(jnp.bfloat16)
        out[i, :, columns + 128 :] = more[i]


def query_grads_kernel(grads, source, up, more, rows):
    shape = shaped((source.shape[1] // rows, rows, grads.shape[1] + 128 + more.shape[2]))
    return local_call(
        partial(query_grads_body, rows),
        (1,),
        [whole(grads), whole(source), whole(up), whole(more)],
        whole(shape),
        shape,
        (grads, source, up, more),
    )


def latent_grads_body(z, place, source, grads, *outs):
    rows = outs[0].shape[0]
    here = grads[...]
    for s, out in enumerate(outs):
        block = 4 * lax.rem(z[0] + s, len(outs)) + place[0]
        start = pl.multiple_of(block * rows, rows)
        out[...] = mul_tn(source[:, pl.ds(start, rows)], here).astype(jnp.bfloat16)


def latent_grads_kernel(z, place, count, source, grads, rows):
    shapes = [shaped((rows, grads.shape[1]))] * count
    return local_call(
        latent_grads_body,
        (1,),
        [SCALAR, SCALAR, whole(source), whole(grads)],
        [whole(s) for s in shapes],
        shapes,
        (z, place, source, grads),
    )


def split_product_body(left, right, kept_out, sent_out):
    total = mul_nt(left[...], right[...]).astype(jnp.bfloat16)
    half = total.shape[0] // 2
    kept_out[0] = total[:half]
    sent_out[0] = total[half:]


def split_product_kernel(left, right, sequences, after=()):
    rows = left.shape[0] // sequences
    shapes = [shaped((sequences, rows // 2, right.shape[0]))] * 2
    return local_call(
        split_product_body,
        (sequences,),
        [by_rows(left, rows), whole(right)],
        [by_first(s) for s in shapes],
        shapes,
        (left, right),
        after,
    )


def core_fold_body(*refs):
    for k in range(4):
        total = refs[k][0, 0].astype(jnp.float32) + refs[4 + k][0, 0].astype(jnp.float32)
        refs[8 + k][0] = total.astype(jnp.bfloat16)


def core_fold_kernel(own, received, after=()):
    half, width = (own.shape[2] // 2, own.shape[3])
    block = (1, 1, half, width)
    specs = [
        pl.BlockSpec(block, lambda k: (0, k, 0, 0)),
        pl.BlockSpec(block, lambda k: (1, k, 0, 0)),
        pl.BlockSpec(block, lambda k: (k, 0, 1, 0)),
        pl.BlockSpec(block, lambda k: (k, 1, 1, 0)),
    ]
    shapes = [shaped((2, half, width))] * 4
    return local_call(
        core_fold_body,
        (2,),
        specs + specs,
        [by_first(s) for s in shapes],
        shapes,
        (own,) * 4 + (received,) * 4,
        after,
    )


def plane_fold_body(lower, lower_got, upper, upper_got, *outs):
    for k, (left, right) in enumerate(((lower, lower_got), (upper, upper_got))):
        for j in range(2):
            total = left[j].astype(jnp.float32) + right[j].astype(jnp.float32)
            outs[2 * k + j][...] = total.astype(jnp.bfloat16)


def plane_fold_kernel(lower, lower_got, upper, upper_got, after=()):
    _, rows, width = lower.shape
    tile = max(16, rows // 2)
    spec = pl.BlockSpec((2, tile, width), lambda i: (0, i, 0))
    shapes = [shaped((rows, width))] * 4
    return local_call(
        plane_fold_body,
        (rows // tile,),
        [spec] * 4,
        [by_rows(s, tile) for s in shapes],
        shapes,
        (lower, lower_got, upper, upper_got),
        after,
    )


def slab_fold_body(lower, lower_got, upper, upper_got, own_out, *outs):
    half = lower.shape[0]
    count = len(outs) + 1
    block = 2 * half // count
    for k, (left, right) in enumerate(((lower, lower_got), (upper, upper_got))):
        total = left[...].astype(jnp.float32) + right[...].astype(jnp.float32)
        if count == 1:
            own_out[k * half : (k + 1) * half, :] = total
            continue
        for j in range(half // block):
            here = total[j * block : (j + 1) * block]
            s = k * (half // block) + j
            if s == 0:
                own_out[...] = here
            else:
                outs[s - 1][...] = here.astype(jnp.bfloat16)


def slab_fold_kernel(lower, lower_got, upper, upper_got, count, after=()):
    half, width = lower.shape
    block = 2 * half // count
    shapes = [shaped((block, width), jnp.float32)] + [shaped((block, width))] * (count - 1)
    return local_call(
        slab_fold_body,
        (1,),
        [whole(lower)] * 4,
        [whole(s) for s in shapes],
        shapes,
        (lower, lower_got, upper, upper_got),
        after,
    )


def z_fold_body(*refs):
    total = refs[0][...].astype(jnp.float32)
    for ref in refs[1:-1]:
        total = total + ref[...].astype(jnp.float32)
    refs[-1][...] = total.astype(refs[-1].dtype)


def z_fold_kernel(parts, dtype, after=()):
    shape = shaped(parts[0].shape, dtype)
    return local_call(
        z_fold_body, (1,), [whole(p) for p in parts], whole(shape), shape, tuple(parts), after
    )


def product_nt_body(left, right, out):
    out[...] = mul_nt(left[...], right[...]).astype(jnp.bfloat16)


def product_nt_kernel(left, right, after=()):
    shape = shaped((left.shape[0], right.shape[0]))
    return local_call(
        product_nt_body,
        (left.shape[0] // TILE,),
        [by_rows(left), whole(right)],
        by_rows(shape),
        shape,
        (left, right),
        after,
    )


def join_body(*refs):
    out = refs[-1]
    at = 0
    for ref in refs[:-1]:
        out[at : at + ref.shape[0], :] = ref[...]
        at += ref.shape[0]


def join_kernel(parts, after=(), more=()):
    parts = list(parts) + list(more)
    shape = shaped((sum(p.shape[0] for p in parts), parts[0].shape[1]), parts[0].dtype)
    return local_call(
        join_body, (1,), [whole(p) for p in parts], whole(shape), shape, tuple(parts), after
    )


def reorder_body(places, *refs):
    del places
    out = refs[-1]
    rows = refs[0].shape[1]
    for s in range(4):
        out[s * rows : (s + 1) * rows, :] = refs[s][0]


def reorder_kernel(places, blocks, after):
    _, rows, width = blocks.shape
    count = places.shape[0]
    step = lambda s: pl.BlockSpec((1, rows, width), lambda i, places: (places[4 * i + s], 0, 0))
    return pl.pallas_call(
        lambda places, a, b, c, d, dep, out: reorder_body(places, a, b, c, d, out),
        grid_spec=pltpu.PrefetchScalarGridSpec(
            num_scalar_prefetch=1,
            grid=(count // 4,),
            in_specs=[step(s) for s in range(4)] + [pl.BlockSpec(memory_space=pl.ANY)],
            out_specs=pl.BlockSpec((4 * rows, width), lambda i, places: (i, 0)),
        ),
        out_shape=shaped((count * rows, width)),
        compiler_params=pltpu.CompilerParams(vmem_limit_bytes=VMEM_LIMIT),
        cost_estimate=pl.CostEstimate(flops=1, bytes_accessed=1, transcendentals=0),
    )(places, *[blocks] * 4, after)


CTX = ("z", "x", "c")


def swap(value, axis):
    return lax.ppermute(value, axis, [(0, 1), (1, 0)])


def from_z(value, steps):
    count = lax.axis_size("z")
    return lax.ppermute(value, "z", [((i + steps) % count, i) for i in range(count)])


def to_z(value, steps):
    count = lax.axis_size("z")
    return lax.ppermute(value, "z", [(i, (i + steps) % count) for i in range(count)])


def trade(value, axes):
    return lax.all_to_all(value, axes, split_axis=0, concat_axis=0, tiled=True)


def add(left, right):
    return left.astype(jnp.float32) + right.astype(jnp.float32)


def low(value):
    return value.astype(jnp.bfloat16)


def dot(left, right):
    return jnp.dot(left, right, preferred_element_type=jnp.float32)


def dot_nt(left, right):
    return lax.dot_general(
        left, right, (((1,), (1,)), ((), ())), preferred_element_type=jnp.float32
    )


def dot_tn(left, right):
    return lax.dot_general(
        left, right, (((0,), (0,)), ((), ())), preferred_element_type=jnp.float32
    )


def by_own(value, axis_name, dim):
    flipped = jnp.flip(value, axis=dim)
    return jnp.where(lax.axis_index(axis_name) == 0, value, flipped)


def tie(value, *others):
    if not others:
        return value
    zero = sum(other[(0,) * other.ndim].astype(jnp.float32) for other in others) * 0.0
    return value + zero.astype(value.dtype)


def rows_first(value):
    return with_layout_constraint(value, Layout(major_to_minor=tuple(range(value.ndim))))


def put(parts, places):
    whole = jnp.zeros((len(parts),) + parts[0].shape, parts[0].dtype)
    for part, place in zip(parts, places):
        whole = lax.dynamic_update_index_in_dim(whole, part, place, 0)
    return rows_first(whole)


def z_parts(value):
    return [value] + [from_z(value, s) for s in range(1, lax.axis_size("z"))]


def put_z(parts):
    z = lax.axis_index("z")
    count = len(parts)
    return put(parts, [(z + s) % count for s in range(count)])


def gather_plane(rows, axes=("x", "y"), gates=()):
    half = rows.shape[0] // 2
    over_a = tie(swap(rows, axes[0]), *gates)
    over_b = tie(swap(rows, axes[1]), *gates)
    both = jnp.concatenate([swap(over_b[:half], axes[0]), swap(over_a[half:], axes[1])], axis=0)
    return jnp.stack([jnp.stack([rows, over_b]), jnp.stack([over_a, both])])


def fold_first(pieces, axes, after=()):
    lower, lower_sent, upper, upper_sent = pieces
    return plane_fold_kernel(
        lower, swap(lower_sent, axes[0]), upper, swap(upper_sent, axes[1]), after
    )


def fold_second(pieces, axes, count, after=()):
    lower, lower_sent, upper, upper_sent = pieces
    return slab_fold_kernel(
        lower, swap(lower_sent, axes[1]), upper, swap(upper_sent, axes[0]), count, after
    )


def fold_z(parts, dtype=jnp.float32, after=()):
    received = [to_z(part, s + 1) for s, part in enumerate(parts[1:])]
    return z_fold_kernel([parts[0]] + received, dtype, after)


def spread_z(rows):
    return jnp.concatenate(z_parts(rows), axis=0)


def both_halves(rows):
    other = swap(rows, "y")
    return by_own(jnp.stack([rows, other]), "y", 0)


def dense_shards(
    tokens,
    norm_in,
    query_weight,
    latent_down,
    latent_norm,
    latent_up,
    output_weight,
    norm_ffn,
    router_weight,
    shared_gate,
    shared_up,
    shared_down,
    expert_gate,
    expert_up,
    expert_down,
    routes,
    cotangent,
):
    zs = lax.axis_size("z")
    z, x, c = (lax.axis_index("z"), lax.axis_index("x"), lax.axis_index("c"))
    me = (z * 2 + x) * 2 + c
    sequences, block, width = tokens.shape
    count = 4 * zs
    rows_here = width // count
    slab = 4 * block
    experts = router_weight.shape[1]
    shared_here = shared_gate.shape[1] // count
    part = -(-max(shared_here, experts) // 128) * 128
    heads = latent_up.shape[1] // (4 * (DN + DV))
    query_columns = heads * (DN + DR)
    rank_rows = R // count
    head_rows = heads * DV
    scale = (DN + DR) ** (-0.5)

    latent_column = jnp.pad(latent_norm, (0, rows_here - rank_rows))[:, None]
    small = jnp.concatenate(
        [
            latent_down,
            router_weight,
            norm_in[:, None],
            norm_ffn[:, None],
            latent_column,
            routes.reshape(sequences * block, TOPK).astype(jnp.bfloat16),
        ],
        axis=1,
    )
    small_parts = z_parts(jnp.pad(small, ((0, 0), (0, -small.shape[1] % 128))))
    up_columns = heads * (DN + DV)
    up_part = jnp.transpose(
        latent_up.reshape(rank_rows, 4, up_columns // 128, 128), (1, 2, 0, 3)
    ).reshape(4, rows_here, 128)
    out_part = jnp.transpose(output_weight.reshape(4, heads, DV, rows_here), (0, 2, 1, 3)).reshape(
        4, DV, heads * rows_here
    )
    by_heads = query_weight.reshape(rows_here, 4, heads, DN + DR)
    by_heads = jnp.concatenate(
        [
            by_heads[..., :DN].reshape(rows_here, 4, heads * DN),
            by_heads[..., DN:].reshape(rows_here, 4, heads * DR),
        ],
        axis=2,
    )
    by_heads = jnp.transpose(by_heads, (1, 0, 2))
    by_heads = jnp.concatenate([by_heads, up_part, out_part], axis=2)
    mine_at = 2 * x + c
    for_group = [
        lax.dynamic_index_in_dim(by_heads, mine_at ^ k, 0, keepdims=False) for k in range(4)
    ]
    by_heads = put(
        [
            for_group[0],
            swap(for_group[1], "c"),
            swap(for_group[2], "x"),
            lax.ppermute(for_group[3], ("x", "c"), [(k, 3 - k) for k in range(4)]),
        ],
        [mine_at ^ k for k in range(4)],
    )
    small = put_z([tie(part, by_heads) for part in small_parts])
    at = R + DR
    down_here = small[:, :, :at]
    rest = small[:, :, at:]
    down_here = down_here.reshape(-1, R + DR)
    down_x = swap(down_here, "x")
    down_pieces = (down_here, down_x, swap(down_here, "c"), swap(down_x, "c"))
    own_gain = rest[:, :, experts].reshape(1, zs * rows_here).astype(jnp.float32)
    rest = jnp.stack([rest, swap(rest, "x")], axis=1)
    rest = jnp.stack([rest, swap(rest, "c")], axis=2)
    rest = by_own(by_own(rest, "x", 1), "c", 2).reshape(count, rows_here, -1)
    full_router = rest[:, :, :experts].reshape(width, experts)
    full_norm_in = rest[:, :, experts].reshape(width).astype(jnp.float32)
    full_norm_ffn = rest[:, :, experts + 1].reshape(width).astype(jnp.float32)
    full_latent_norm = rest[:, :rank_rows, experts + 2].reshape(R).astype(jnp.float32)
    all_routes = rest[:, :, experts + 3 : experts + 3 + TOPK]

    mine = by_own(tokens, "y", 0)
    line = jnp.stack([mine, swap(mine, "x")], axis=1)
    line = jnp.stack([line, swap(line, "c")], axis=1)
    source = line.reshape(sequences * slab, width).astype(jnp.float32)
    grad_mine = by_own(cotangent, "y", 0)[0]
    all_grads = lax.all_gather(tie(grad_mine, by_heads), CTX + ("y",), axis=0)
    one = jnp.arange(2)
    order = (
        (((z + jnp.arange(zs)) % zs)[None, None, None, :] * 2 + (x ^ one)[None, :, None, None]) * 2
        + (c ^ one)[:, None, None, None]
    ) * 2 + (lax.axis_index("y") ^ one)[None, None, :, None]
    order = order.reshape(-1).astype(jnp.int32)
    gate_t, up_t, down = (expert_gate[0].T, expert_up[0].T, expert_down[0])
    query_here, up_here, out_here = heads_kernel(
        lax.all_gather(by_heads, "z", axis=0),
        query_columns,
        heads,
        up_columns,
    )

    def places(turns):
        two = jnp.arange(2)
        base = (
            ((z + turns[None, None, :]) % zs) * 4
            + (x ^ two[None, :, None]) * 2
            + (c ^ two[:, None, None])
        )
        return (base[..., None] * block + jnp.arange(block)).reshape(-1)

    positions = places(jnp.arange(1))
    key_positions = places(jnp.arange(zs))
    cosine, sine = rotary_tables(positions, DR)
    normed, unit_in, inverse_in = root_norm(source, full_norm_in)
    input_low = low(normed)

    own_rows = line[0].reshape(slab, width)
    own_columns = jnp.concatenate(
        [
            lax.dynamic_slice_in_dim(own_rows, (4 * k + 2 * x + c) * rows_here, rows_here, 1)
            for k in range(zs)
        ],
        axis=1,
    ).astype(jnp.float32)
    latent_part = dot(
        low(own_columns * inverse_in[:slab] * own_gain), down_here
    )
    latent_part = low(latent_part).reshape(2, 2, block, R + DR)
    latent_part = low(add(latent_part[0], swap(latent_part[1], "c")))
    latent_raw = add(latent_part[0], swap(latent_part[1], "x"))
    latent_scaled, latent_unit, latent_inverse = root_norm(latent_raw[:, :R], full_latent_norm)
    key_own = low(
        jnp.concatenate(
            [latent_scaled, rotate(latent_raw[:, R:], cosine[:block], sine[:block])], axis=-1
        )
    )
    plane = gather_plane(spread_z(key_own), ("y", "x"))
    keys_own, keys_other = (plane, swap(plane, "c"))
    query = dot(input_low, query_here)
    rope = query[:, heads * DN :].reshape(sequences, slab, heads, DR)
    rope = rotate(rope, cosine[:, None, :], sine[:, None, :]).reshape(sequences * slab, -1)
    query_low = low(jnp.concatenate([query[:, : heads * DN], rope], axis=1))

    shared_mine = jnp.concatenate(
        [
            shared_gate.T.reshape(count, shared_here, rows_here),
            shared_up.T.reshape(count, shared_here, rows_here),
            shared_down.reshape(count, shared_here, rows_here),
        ],
        axis=1,
    )
    shared_rows = trade(tie(shared_mine, query_low), CTX)
    shared_got = shared_rows
    shared_rows = jnp.transpose(shared_rows, (1, 0, 2)).reshape(3, shared_here, width)
    shared_rows = jnp.pad(shared_rows, ((0, 0), (0, part - shared_here), (0, 0)))
    small_t = jnp.concatenate(
        [
            shared_rows[0],
            shared_rows[1],
            jnp.pad(full_router.T, ((0, part - experts), (0, 0))),
        ]
    )
    shared_down_t = shared_rows[2]

    def scatter_slab(kept, sent, after=()):
        shape = (2, 2, block, width)
        pieces = core_fold_kernel(kept.reshape(shape), swap(sent, "c").reshape(shape))
        return fold_second(fold_first(pieces, ("y", "x"), after), ("y", "x"), 1)[0]

    def gather_slab(rows):
        plane = gather_plane(rows, ("y", "x"))
        return jnp.stack([plane, swap(plane, "c")], axis=1).reshape(sequences * slab, -1)

    kept, sent, prob, absorbed, latent_out, head_out = attend_kernel(
        query_low,
        keys_own,
        keys_other,
        up_here,
        out_here,
        positions[:, None],
        key_positions[None, :],
        heads,
        scale,
        down_pieces[1:],
    )
    attention = scatter_slab(kept, sent)
    hidden_in = mine[0].astype(jnp.float32) + attention
    normed_ffn, unit_ffn, inverse_ffn = root_norm(hidden_in, full_norm_ffn)
    ffn_low = low(normed_ffn)
    shares = jax.nn.softmax(dot(ffn_low, full_router), axis=-1)
    half_places = order.shape[0] // 2
    grads_own = reorder_kernel(order[:half_places], all_grads, ffn_low)
    grads_other = reorder_kernel(order[half_places:], all_grads, ffn_low)
    ffn_parts = z_parts(ffn_low)
    back_own = product_nt_kernel(grads_own, down)
    back_other = product_nt_kernel(grads_other, down, (back_own,))
    ffn_slabs = join_kernel(ffn_parts, (shared_got, back_other))
    shared_own = product_nt_kernel(grads_own, shared_down_t, (ffn_slabs,))
    shared_other = product_nt_kernel(grads_other, shared_down_t, (shared_own,))
    half = ffn_slabs.shape[0] // 2
    over_x, over_y = (swap(ffn_slabs, "x"), swap(ffn_slabs, "y"))
    ffn_own = join_kernel(
        [ffn_slabs, over_y, over_x],
        (shared_other,),
        [swap(over_y[:half], "x"), swap(over_x[half:], "y")],
    )
    ffn_other = swap(ffn_own, "c").reshape(-1, width)

    relative = all_routes.reshape(zs, 2, 2, sequences, block, TOPK)
    relative = by_own(by_own(by_own(relative, "x", 1), "c", 2), "y", 3)
    relative = jnp.roll(relative, -z, axis=0)
    routed = jnp.any(relative == me.astype(jnp.bfloat16), axis=-1)
    routed = jnp.transpose(routed, (2, 1, 3, 0, 4)).reshape(2, -1, 1).astype(jnp.float32)
    pick = (jnp.arange(part)[None, :] == me).astype(jnp.float32)

    def feed(rows, back, shared_back, named, after=()):
        return feed_kernel(
            rows, back, shared_back, gate_t, up_t, small_t, named, pick, experts, after
        )

    act_own, more_own, gate_own, up_own, pre_own, gain_own = feed(
        ffn_own, back_own, shared_own, routed[0]
    )
    act_other, more_other, gate_other, up_other, pre_other, gain_other = feed(
        ffn_other, back_other, shared_other, routed[1], (act_own,)
    )
    shape = (2, 2, zs * block, width + part)
    grad_other = input_kernel(
        gate_other, up_other, pre_other, gate_t, up_t, small_t, gain_other, pick
    )
    grad_own = input_kernel(
        gate_own, up_own, pre_own, gate_t, up_t, small_t, gain_own, pick, (grad_other,)
    )
    pieces = core_fold_kernel(grad_own.reshape(shape), swap(grad_other, "c").reshape(shape))
    both_axes = ("x", "y")
    sum_other = result_kernel(act_other, more_other, down, shared_down_t, pieces)
    sum_own = result_kernel(act_own, more_own, down, shared_down_t, (sum_other,))
    grad_expert_up, shared_up_back = weight_kernel(
        (up_own, up_other), (pre_own, pre_other), (ffn_own, ffn_other), 1, part, (sum_own,)
    )
    pieces = fold_first(pieces, both_axes, (grad_expert_up,))
    shape = (2, 2, zs * block, width)
    grad_expert_down, shared_down_back = weight_kernel(
        (act_own, act_other), (more_own, more_other), (grads_own, grads_other), 0, part, pieces
    )
    grad_slab = fold_second(pieces, both_axes, zs, (grad_expert_down,))
    routed_pieces = core_fold_kernel(
        sum_own.reshape(shape), swap(sum_other, "c").reshape(shape), grad_slab
    )
    grad_expert_gate, shared_gate_back = weight_kernel(
        (gate_own, gate_other),
        (pre_own, pre_other),
        (ffn_own, ffn_other),
        0,
        part,
        tuple(routed_pieces),
    )
    routed_pieces = fold_first(routed_pieces, both_axes, (grad_expert_gate,))
    ffn_grad = fold_z(grad_slab, jnp.float32, routed_pieces)
    share_grad = ffn_grad[:, width : width + experts]
    ffn_grad = ffn_grad[:, :width]
    logit_grad = shares * (share_grad - jnp.sum(shares * share_grad, axis=-1, keepdims=True))
    ffn_grad = ffn_grad + dot_nt(low(logit_grad), full_router)
    grad_router = dot_tn(ffn_low, low(logit_grad))
    hidden_part, grad_norm_ffn = root_norm_back(ffn_grad, unit_ffn, inverse_ffn, full_norm_ffn)
    grad_hidden = grad_mine.astype(jnp.float32) + hidden_part

    hidden_low = low(grad_hidden)
    attention_grad = gather_slab(hidden_low)
    shared_back = jnp.concatenate(
        [
            shared_gate_back[:shared_here],
            shared_up_back[:shared_here],
            shared_down_back[:shared_here],
        ]
    )
    shared_back = trade(
        jnp.transpose(shared_back.reshape(-1, count, rows_here), (1, 0, 2)), CTX
    )
    zero = jnp.zeros((1,), jnp.int32)
    (out_grads,) = out_grads_kernel(zero, 1, head_out, attention_grad, rows_here)
    key_own, key_other, query_grad, grad_up_here = attend_back_kernel(
        attention_grad,
        query_low,
        keys_own,
        keys_other,
        up_here,
        out_here,
        prob,
        absorbed,
        latent_out,
        heads,
        scale,
        (out_grads,),
    )
    rope = query_grad[:, heads * DN :].reshape(sequences, slab, heads, DR)
    rope = rotate(rope, cosine[:, None, :], -sine[:, None, :]).reshape(sequences * slab, -1)
    query_raw_grad = low(jnp.concatenate([query_grad[:, : heads * DN], rope], axis=1))
    query_grads = query_grads_kernel(
        query_raw_grad, input_low, grad_up_here, out_grads, rows_here
    )
    grad_heads = lax.psum_scatter(query_grads, "z", scatter_dimension=0, tiled=True)
    key_pieces = core_fold_kernel(key_own, swap(key_other, "c"), (query_grads, shared_back))
    input_grad = scatter_slab(
        *split_product_kernel(query_raw_grad, query_here, sequences, (query_grads,))
    )
    key_slab = fold_second(fold_first(key_pieces, ("y", "x")), ("y", "x"), zs)
    key_sum = fold_z(key_slab)
    routed_slab = fold_second(routed_pieces, both_axes, zs, (key_sum,))
    latent_back, grad_latent_norm = root_norm_back(
        key_sum[:, :R], latent_unit, latent_inverse, full_latent_norm
    )
    rope_key = rotate(key_sum[:, R:], cosine[:block], -sine[:block])
    latent_raw_grad = low(jnp.concatenate([latent_back, rope_key], axis=-1))
    slab_latent_grad = gather_slab(latent_raw_grad)
    down_grads = latent_grads_kernel(
        z[None], (2 * x + c)[None], zs, input_low, slab_latent_grad, rows_here
    )
    latent_raw_grad = tie(latent_raw_grad, down_grads[0])
    shared_back = shared_back.astype(jnp.float32)
    grad_shared_gate = shared_back[:, :shared_here].reshape(-1, rows_here).T
    grad_shared_up = shared_back[:, shared_here : 2 * shared_here].reshape(-1, rows_here).T
    grad_shared_down = shared_back[:, 2 * shared_here :].reshape(-1, rows_here)


    output = both_halves(low(hidden_in + fold_z(routed_slab, jnp.float32, (down_grads[0],))))
    latent_input = jnp.stack([dot_nt(latent_raw_grad, down) for down in down_pieces])
    latent_input = latent_input.reshape(2, 2, block, zs, rows_here)
    latent_input = by_own(by_own(latent_input, "c", 0), "x", 1)
    input_grad = input_grad + jnp.transpose(latent_input, (2, 3, 1, 0, 4)).reshape(block, width)
    source_part, grad_norm_in = root_norm_back(
        input_grad, unit_in[:block], inverse_in[:block], full_norm_in
    )
    tokens_gradient = both_halves(low(grad_hidden + source_part)).astype(jnp.float32)

    group = by_own(by_own(grad_heads.reshape((2, 2) + grad_heads.shape[1:]), "x", 0), "c", 1)
    crossed = lax.ppermute(group[1, 1], ("x", "c"), [(k, 3 - k) for k in range(4)])
    traded = jnp.stack(
        [
            jnp.stack([group[0, 0], swap(group[0, 1], "c")]),
            jnp.stack([swap(group[1, 0], "x"), crossed]),
        ]
    )
    traded = by_own(by_own(traded, "x", 0), "c", 1).reshape(grad_heads.shape)
    both = traded.astype(jnp.float32)
    grad_down = fold_z(down_grads, jnp.float32, (traded,))
    out_at = both.shape[2] - head_rows
    grad_output = jnp.transpose(
        both[..., out_at:].reshape(4, DV, heads, rows_here), (0, 2, 1, 3)
    ).reshape(-1, rows_here)
    grad_query = jnp.transpose(both[..., :query_columns], (1, 0, 2))
    grad_query = jnp.concatenate(
        [
            grad_query[..., : heads * DN].reshape(rows_here, 4, heads, DN),
            grad_query[..., heads * DN :].reshape(rows_here, 4, heads, DR),
        ],
        axis=-1,
    ).reshape(rows_here, -1)
    grad_latent_up = jnp.transpose(
        both[..., query_columns:out_at].reshape(4, up_columns // 128, rank_rows, 128), (2, 0, 1, 3)
    ).reshape(rank_rows, -1)

    small_grads = jnp.concatenate(
        [
            grad_router.T.reshape(experts, count, rows_here),
            grad_norm_in.reshape(1, count, rows_here),
            grad_norm_ffn.reshape(1, count, rows_here),
            jnp.pad(
                grad_latent_norm.reshape(1, count, rank_rows),
                ((0, 0), (0, 0), (0, rows_here - rank_rows)),
            ),
        ]
    )
    small_grads = trade(jnp.transpose(small_grads, (1, 0, 2)), CTX)
    small_grads = jnp.sum(small_grads, axis=0)
    small_grads = small_grads + swap(small_grads, "y")
    return (
        output,
        tokens_gradient,
        small_grads[experts],
        grad_query,
        grad_down,
        small_grads[experts + 2, :rank_rows],
        grad_latent_up,
        grad_output,
        small_grads[experts + 1],
        small_grads[:experts].T,
        grad_shared_gate,
        grad_shared_up,
        grad_shared_down,
        grad_expert_gate.T[None],
        grad_expert_up.T[None],
        grad_expert_down[None],
    )


IN_SPECS = (
    (None, "ctx", None),
    ("ctx",),
    ("ctx", "wa"),
    ("ctx", None),
    ("ctx",),
    ("ctx", "wa"),
    ("wa", "ctx"),
    ("ctx",),
    ("ctx", None),
    ("ctx", "wa"),
    ("ctx", "wa"),
    ("wa", "ctx"),
    ("ctx", None, "wa"),
    ("ctx", None, "wa"),
    ("ctx", "wa", None),
    (None, "ctx", None),
    (None, "ctx", None),
)
OUT_SPECS = ((None, "ctx", None),) * 2 + IN_SPECS[1:15]


def solution(mesh):
    count = mesh.shape["ctx"]

    def run(*arguments):
        experts = arguments[12].shape[0]
        if experts > 4 * TOPK or experts != count or mesh.shape["wa"] != 2 or count % 8:
            return jax.shard_map(
                shards,
                mesh=mesh,
                in_specs=tuple(P(*spec) for spec in IN_SPECS),
                out_specs=tuple(P(*spec) for spec in OUT_SPECS),
                check_vma=False,
            )(*arguments)
        grid = Mesh(mesh.devices.reshape(count // 4, 2, 2, 2), ("z", "x", "c", "y"))
        names = {"ctx": CTX, "wa": "y", None: None}
        return jax.shard_map(
            dense_shards,
            mesh=grid,
            in_specs=tuple(P(*[names[n] for n in spec]) for spec in IN_SPECS),
            out_specs=tuple(P(*[names[n] for n in spec]) for spec in OUT_SPECS),
            check_vma=False,
        )(*arguments)

    return run
```

```python
from functools import partial

import jax
import jax.numpy as jnp
from jax import lax
from jax.experimental import pallas as pl
from jax.experimental.layout import Layout, with_layout_constraint
from jax.experimental.pallas import tpu as pltpu
from jax.sharding import Mesh, PartitionSpec as P

DN = 128
DR = 64
DV = 128
R = 512
TOPK = 6


epsilon = 1e-06
highest = lax.Precision.HIGHEST


def shifted(value, axis, steps):
    count = lax.axis_size(axis)
    pairs = [(source, (source + steps) % count) for source in range(count)]
    return lax.ppermute(value, axis, pairs)


def root_norm(values, gain):
    inverse = lax.rsqrt(jnp.mean(values * values, axis=-1, keepdims=True) + epsilon)
    unit = values * inverse
    return (unit * gain, unit, inverse)


def root_norm_back(upstream, unit, inverse, gain):
    scaled = upstream * gain
    inner = jnp.mean(scaled * unit, axis=-1, keepdims=True)
    leading = tuple(range(upstream.ndim - 1))
    return (inverse * (scaled - unit * inner), jnp.sum(upstream * unit, axis=leading))


def rotary_tables(positions, width):
    half = width // 2
    frequency = 10000.0 ** (-jnp.arange(half, dtype=jnp.float32) * 2.0 / width)
    angle = positions.astype(jnp.float32)[:, None] * frequency[None, :]
    return (jnp.cos(angle), jnp.sin(angle))


def rotate(values, cosine, sine):
    half = values.shape[-1] // 2
    first = values[..., :half]
    second = values[..., half:]
    return jnp.concatenate(
        [first * cosine - second * sine, second * cosine + first * sine], axis=-1
    )


def silu_slope(values):
    sigmoid = jax.nn.sigmoid(values)
    return sigmoid * (1.0 + values * (1.0 - sigmoid))


def fetch_weights(
    norm_in,
    query_weight,
    latent_down,
    latent_norm,
    latent_up,
    output_weight,
    norm_ffn,
    router_weight,
    shared_gate,
    shared_up,
    shared_down,
):
    return (
        lax.all_gather(norm_in, "ctx", axis=0, tiled=True),
        lax.all_gather(query_weight, "ctx", axis=0, tiled=True),
        lax.all_gather(latent_down, "ctx", axis=0, tiled=True),
        lax.all_gather(latent_norm, "ctx", axis=0, tiled=True),
        lax.all_gather(latent_up, "ctx", axis=0, tiled=True),
        lax.all_gather(output_weight, "ctx", axis=1, tiled=True),
        lax.all_gather(norm_ffn, "ctx", axis=0, tiled=True),
        lax.all_gather(router_weight, "ctx", axis=0, tiled=True),
        lax.all_gather(shared_gate, "ctx", axis=0, tiled=True),
        lax.all_gather(shared_up, "ctx", axis=0, tiled=True),
        lax.all_gather(shared_down, "ctx", axis=1, tiled=True),
    )


def shards(
    tokens,
    norm_in,
    query_weight,
    latent_down,
    latent_norm,
    latent_up,
    output_weight,
    norm_ffn,
    router_weight,
    shared_gate,
    shared_up,
    shared_down,
    expert_gate,
    expert_up,
    expert_down,
    routes,
    cotangent,
):
    context_count = lax.axis_size("ctx")
    context_index = lax.axis_index("ctx")
    lead = (lax.axis_index("wa") == 0).astype(jnp.float32)
    sequences, block, width = tokens.shape
    local_experts = expert_gate.shape[0]
    experts = context_count * local_experts
    capacity = max(2, block * TOPK * 4 // (3 * experts))
    scale = (DN + DR) ** (-0.5)
    gathered = fetch_weights(
        norm_in,
        query_weight,
        latent_down,
        latent_norm,
        latent_up,
        output_weight,
        norm_ffn,
        router_weight,
        shared_gate,
        shared_up,
        shared_down,
    )
    (
        full_norm_in,
        full_query,
        full_down,
        full_latent_norm,
        full_up,
        full_output,
        full_norm_ffn,
        full_router,
        full_shared_gate,
        full_shared_up,
        full_shared_down,
    ) = gathered
    heads_here = full_up.shape[1] // (DN + DV)
    positions = context_index * block + jnp.arange(block)
    cosine, sine = rotary_tables(positions, DR)
    source = tokens.astype(jnp.float32)
    normed_in, unit_in, inverse_in = root_norm(source, full_norm_in.astype(jnp.float32))
    input_low = normed_in.astype(jnp.bfloat16)
    query_raw = jnp.dot(input_low, full_query, preferred_element_type=jnp.float32).reshape(
        sequences, block, heads_here, DN + DR
    )
    query_low = jnp.concatenate(
        [query_raw[..., :DN], rotate(query_raw[..., DN:], cosine[:, None, :], sine[:, None, :])],
        axis=-1,
    ).astype(jnp.bfloat16)
    up_view = full_up.reshape(R, heads_here, DN + DV)
    key_up = up_view[..., :DN]
    value_up = up_view[..., DN:]
    absorbed = jnp.einsum(
        "sbhn,rhn->shbr", query_low[..., :DN], key_up, preferred_element_type=jnp.float32
    )
    query_rows = jnp.concatenate(
        [absorbed.astype(jnp.bfloat16), jnp.transpose(query_low[..., DN:], (0, 2, 1, 3))], axis=-1
    )
    latent_raw = jnp.dot(input_low, full_down, preferred_element_type=jnp.float32)
    latent_scaled, latent_unit, latent_inverse = root_norm(
        latent_raw[..., :R], full_latent_norm.astype(jnp.float32)
    )
    key_rows = jnp.concatenate(
        [latent_scaled, rotate(latent_raw[..., R:], cosine, sine)], axis=-1
    ).astype(jnp.bfloat16)
    piece = lax.all_gather(key_rows, "ctx", axis=1, tiled=True)
    top = jnp.full((sequences, heads_here, block), -1e30, jnp.float32)
    scores = (
        jnp.einsum("shqc,skc->shqk", query_rows, piece, preferred_element_type=jnp.float32) * scale
    )
    key_positions = jnp.arange(piece.shape[1])
    allowed = positions[:, None] >= key_positions[None, :]
    scores = jnp.where(allowed, scores, -1e30)
    new_top = jnp.maximum(top, jnp.max(scores, axis=-1))
    weights = jnp.where(allowed, jnp.exp(scores - new_top[..., None]), 0.0)
    total = jnp.sum(weights, axis=-1)
    weights_high = weights.astype(jnp.bfloat16)
    weights_rest = (weights - weights_high.astype(jnp.float32)).astype(jnp.bfloat16)
    running = jnp.einsum(
        "shqk,skr->shqr", weights_high, piece[..., :R], preferred_element_type=jnp.float32
    )
    remainder = jnp.einsum(
        "shqk,skr->shqr", weights_rest, piece[..., :R], preferred_element_type=jnp.float32
    )
    top, total, running, remainder = (new_top, total, running, remainder)
    log_total = top + jnp.log(total)
    latent_out = (running / total[..., None]).astype(jnp.bfloat16)
    latent_exact = (running + remainder) / total[..., None]
    head_out = (
        jnp.einsum("shbr,rhv->sbhv", latent_out, value_up, preferred_element_type=jnp.float32)
        .astype(jnp.bfloat16)
        .reshape(sequences, block, heads_here * DV)
    )
    attention_part = jnp.dot(head_out, full_output, preferred_element_type=jnp.float32)
    hidden_in = source + lax.psum(attention_part, "wa")
    normed_ffn, unit_ffn, inverse_ffn = root_norm(hidden_in, full_norm_ffn.astype(jnp.float32))
    ffn_low = normed_ffn.astype(jnp.bfloat16)
    shares = jax.nn.softmax(
        jnp.dot(ffn_low, full_router, preferred_element_type=jnp.float32), axis=-1
    )
    shared_g = jnp.dot(ffn_low, full_shared_gate, preferred_element_type=jnp.float32)
    shared_u = jnp.dot(ffn_low, full_shared_up, preferred_element_type=jnp.float32)
    shared_silu = jax.nn.silu(shared_g)
    shared_activation = (shared_silu * shared_u).astype(jnp.bfloat16)
    shared_part = jnp.dot(shared_activation, full_shared_down, preferred_element_type=jnp.float32)
    expert_ids = jnp.arange(experts, dtype=jnp.int32)
    chosen = (
        (routes[..., None] == expert_ids)
        .astype(jnp.int32)
        .reshape(sequences, block * TOPK, experts)
    )
    earlier = jnp.cumsum(chosen, axis=1) - chosen
    slot_of = jnp.sum(earlier * chosen, axis=-1).reshape(sequences, block, TOPK)
    slot_ids = jnp.arange(capacity, dtype=jnp.int32)
    hit = (routes[None, :, :, :, None] == expert_ids[:, None, None, None, None]) & (
        slot_of[None, :, :, :, None] == slot_ids[None, None, None, None, :]
    )
    dispatch = jnp.transpose(jnp.any(hit, axis=3), (0, 1, 3, 2)).astype(jnp.float32)
    send = (
        jnp.einsum(
            "escb,sbd->escd",
            dispatch.astype(jnp.bfloat16),
            ffn_low,
            preferred_element_type=jnp.float32,
        )
        .astype(jnp.bfloat16)
        .reshape(experts, sequences * capacity, width)
    )
    slot_share = jnp.einsum("escb,sbe->esc", dispatch, shares, precision=highest)
    received = lax.all_to_all(send, "ctx", split_axis=0, concat_axis=0, tiled=True)
    count = received.shape[1]
    rows = received.reshape(context_count, local_experts, count, width)
    gate_pre = jnp.einsum("nesd,edf->nesf", rows, expert_gate, preferred_element_type=jnp.float32)
    up_pre = jnp.einsum("nesd,edf->nesf", rows, expert_up, preferred_element_type=jnp.float32)
    activation = (jax.nn.silu(gate_pre) * up_pre).astype(jnp.bfloat16)
    result = jnp.einsum(
        "nesf,efd->nesd", activation, expert_down, preferred_element_type=jnp.float32
    ).reshape(experts, count, width)
    returned = lax.all_to_all(result, "ctx", split_axis=0, concat_axis=0, tiled=True)
    hidden_units = gate_pre.shape[-1]
    returned, received, gate_keep, up_keep = (
        returned,
        received,
        gate_pre.reshape(experts, count, hidden_units),
        up_pre.reshape(experts, count, hidden_units),
    )
    returned = returned.reshape(experts, sequences, capacity, width)
    routed_part = jnp.einsum(
        "escb,escd->sbd", dispatch, returned * slot_share[..., None], precision=highest
    )
    output = hidden_in + lax.psum(shared_part + routed_part, "wa")
    gathered = fetch_weights(
        norm_in,
        query_weight,
        latent_down,
        latent_norm,
        latent_up,
        output_weight,
        norm_ffn,
        router_weight,
        shared_gate,
        shared_up,
        shared_down,
    )
    (
        full_norm_in,
        full_query,
        full_down,
        full_latent_norm,
        full_up,
        full_output,
        full_norm_ffn,
        full_router,
        full_shared_gate,
        full_shared_up,
        full_shared_down,
    ) = gathered
    up_view = full_up.reshape(R, heads_here, DN + DV)
    key_up = up_view[..., :DN]
    value_up = up_view[..., DN:]
    grad_y = cotangent.astype(jnp.float32)
    shared_grad = jnp.einsum(
        "sbd,fd->sbf", cotangent, full_shared_down, preferred_element_type=jnp.float32
    )
    shared_gate_grad = (shared_grad * shared_u * silu_slope(shared_g)).astype(jnp.bfloat16)
    shared_up_grad = (shared_grad * shared_silu).astype(jnp.bfloat16)
    grad_shared_down = jnp.einsum(
        "sbf,sbd->fd", shared_activation, cotangent, preferred_element_type=jnp.float32
    )
    grad_shared_gate = jnp.einsum(
        "sbd,sbf->df", ffn_low, shared_gate_grad, preferred_element_type=jnp.float32
    )
    grad_shared_up = jnp.einsum(
        "sbd,sbf->df", ffn_low, shared_up_grad, preferred_element_type=jnp.float32
    )
    ffn_grad = jnp.einsum(
        "sbf,df->sbd", shared_gate_grad, full_shared_gate, preferred_element_type=jnp.float32
    )
    ffn_grad = ffn_grad + jnp.einsum(
        "sbf,df->sbd", shared_up_grad, full_shared_up, preferred_element_type=jnp.float32
    )
    grad_at_slots = jnp.einsum("escb,sbd->escd", dispatch, grad_y, precision=highest)
    slot_grads = (
        (grad_at_slots * slot_share[..., None])
        .astype(jnp.bfloat16)
        .reshape(experts, sequences * capacity, width)
    )
    slot_dot = jnp.sum(returned * grad_at_slots, axis=-1)
    share_grad = jnp.einsum("escb,esc->sbe", dispatch, slot_dot, precision=highest)
    logit_grad = shares * (share_grad - jnp.sum(shares * share_grad, axis=-1, keepdims=True))
    grad_router = jnp.einsum(
        "sbd,sbe->de", ffn_low.astype(jnp.float32), logit_grad, precision=highest
    )
    ffn_grad = ffn_grad + jnp.einsum(
        "sbe,de->sbd", logit_grad, full_router.astype(jnp.float32), precision=highest
    )
    slot_back = lax.all_to_all(slot_grads, "ctx", split_axis=0, concat_axis=0, tiled=True).reshape(
        context_count, local_experts, -1, width
    )
    rows = received.reshape(context_count, local_experts, -1, width)
    gate_pre = gate_keep.reshape(context_count, local_experts, -1, gate_keep.shape[-1])
    up_pre = up_keep.reshape(context_count, local_experts, -1, up_keep.shape[-1])
    hidden_grad = jnp.einsum(
        "nesd,efd->nesf", slot_back, expert_down, preferred_element_type=jnp.float32
    )
    silu_gate = jax.nn.silu(gate_pre)
    gate_grad = (hidden_grad * up_pre * silu_slope(gate_pre)).astype(jnp.bfloat16)
    up_grad = (hidden_grad * silu_gate).astype(jnp.bfloat16)
    activation = (silu_gate * up_pre).astype(jnp.bfloat16)
    grad_expert_down = jnp.einsum(
        "nesf,nesd->efd", activation, slot_back, preferred_element_type=jnp.float32
    )
    grad_expert_gate = jnp.einsum(
        "nesd,nesf->edf", rows, gate_grad, preferred_element_type=jnp.float32
    )
    grad_expert_up = jnp.einsum("nesd,nesf->edf", rows, up_grad, preferred_element_type=jnp.float32)
    rows_grad = jnp.einsum(
        "nesf,edf->nesd", gate_grad, expert_gate, preferred_element_type=jnp.float32
    )
    rows_grad = rows_grad + jnp.einsum(
        "nesf,edf->nesd", up_grad, expert_up, preferred_element_type=jnp.float32
    )
    slot_grad = lax.all_to_all(
        rows_grad.reshape(experts, -1, width), "ctx", split_axis=0, concat_axis=0, tiled=True
    ).reshape(experts, sequences, capacity, width)
    ffn_grad = ffn_grad + jnp.einsum("escb,escd->sbd", dispatch, slot_grad, precision=highest)
    hidden_part, grad_norm_ffn = root_norm_back(
        ffn_grad, unit_ffn, inverse_ffn, full_norm_ffn.astype(jnp.float32)
    )
    grad_hidden = grad_y + lax.psum(hidden_part, "wa")
    attention_grad = grad_hidden.astype(jnp.bfloat16)
    grad_output = jnp.einsum(
        "sbk,sbd->kd", head_out, attention_grad, preferred_element_type=jnp.float32
    )
    head_grad = (
        jnp.einsum("sbd,kd->sbk", attention_grad, full_output, preferred_element_type=jnp.float32)
        .astype(jnp.bfloat16)
        .reshape(sequences, block, heads_here, DV)
    )
    grad_value_up = jnp.einsum(
        "shbr,sbhv->rhv", latent_out, head_grad, preferred_element_type=jnp.float32
    )
    latent_out_grad = jnp.einsum(
        "sbhv,rhv->shbr", head_grad, value_up, preferred_element_type=jnp.float32
    ).astype(jnp.bfloat16)
    row_dot = jnp.sum(latent_out_grad.astype(jnp.float32) * latent_exact, axis=-1)

    def turn_body(turn, carry):
        keys_here, key_grad, query_grad = carry
        source_index = (context_index + turn) % context_count
        key_positions = source_index * block + jnp.arange(block)
        allowed = positions[:, None] >= key_positions[None, :]
        scores = (
            jnp.einsum("shqc,skc->shqk", query_rows, keys_here, preferred_element_type=jnp.float32)
            * scale
        )
        weights = jnp.where(allowed[None, None], jnp.exp(scores - log_total[..., None]), 0.0)
        weight_grad = jnp.einsum(
            "shqr,skr->shqk",
            latent_out_grad,
            keys_here[..., :R],
            preferred_element_type=jnp.float32,
        )
        score_grad = (weights * (weight_grad - row_dot[..., None])).astype(jnp.bfloat16)
        query_grad = (
            query_grad
            + jnp.einsum(
                "shqk,skc->shqc", score_grad, keys_here, preferred_element_type=jnp.float32
            )
            * scale
        )
        key_part = (
            jnp.einsum("shqk,shqc->skc", score_grad, query_rows, preferred_element_type=jnp.float32)
            * scale
        )
        value_part = jnp.einsum(
            "shqk,shqr->skr",
            weights.astype(jnp.bfloat16),
            latent_out_grad,
            preferred_element_type=jnp.float32,
        )
        key_grad = key_grad + key_part + jnp.pad(value_part, ((0, 0), (0, 0), (0, DR)))
        keys_next = shifted(keys_here, "ctx", -1)
        grad_next = shifted(key_grad, "ctx", -1)
        return (keys_next, grad_next, query_grad)

    start_back = (
        key_rows,
        jnp.zeros((sequences, block, R + DR), jnp.float32),
        jnp.zeros((sequences, heads_here, block, R + DR), jnp.float32),
    )
    unused_keys, key_grad, query_grad = lax.fori_loop(0, context_count, turn_body, start_back)
    key_grad_total = lax.psum(key_grad, "wa")
    query_grad_low = query_grad.astype(jnp.bfloat16)
    absorbed_grad = query_grad_low[..., :R]
    rope_query_grad = jnp.transpose(query_grad_low[..., R:], (0, 2, 1, 3)).astype(jnp.float32)
    grad_key_up = jnp.einsum(
        "shbr,sbhn->rhn", absorbed_grad, query_low[..., :DN], preferred_element_type=jnp.float32
    )
    nope_grad = jnp.einsum(
        "shbr,rhn->sbhn", absorbed_grad, key_up, preferred_element_type=jnp.float32
    )
    rope_raw_grad = rotate(rope_query_grad, cosine[:, None, :], -sine[:, None, :])
    query_raw_grad = (
        jnp.concatenate([nope_grad, rope_raw_grad], axis=-1)
        .astype(jnp.bfloat16)
        .reshape(sequences, block, heads_here * (DN + DR))
    )
    grad_query = jnp.einsum(
        "sbd,sbk->dk", input_low, query_raw_grad, preferred_element_type=jnp.float32
    )
    input_part = jnp.einsum(
        "sbk,dk->sbd", query_raw_grad, full_query, preferred_element_type=jnp.float32
    )
    grad_latent_up = jnp.concatenate([grad_key_up, grad_value_up], axis=-1).reshape(
        R, heads_here * (DN + DV)
    )
    latent_grad, grad_latent_norm = root_norm_back(
        key_grad_total[..., :R], latent_unit, latent_inverse, full_latent_norm.astype(jnp.float32)
    )
    rope_key_grad = rotate(key_grad_total[..., R:], cosine, -sine)
    latent_raw_grad = jnp.concatenate([latent_grad, rope_key_grad], axis=-1).astype(jnp.bfloat16)
    grad_down = jnp.einsum(
        "sbd,sbc->dc", input_low, latent_raw_grad, preferred_element_type=jnp.float32
    )
    input_part = input_part + lead * jnp.einsum(
        "sbc,dc->sbd", latent_raw_grad, full_down, preferred_element_type=jnp.float32
    )
    source_part, grad_norm_in = root_norm_back(
        input_part, unit_in, inverse_in, full_norm_in.astype(jnp.float32)
    )
    summed = lax.psum((source_part, grad_norm_in, grad_norm_ffn, grad_router), "wa")
    tokens_gradient = grad_hidden + summed[0]
    reduced = (
        lax.psum_scatter(summed[1], "ctx", scatter_dimension=0, tiled=True),
        lax.psum_scatter(grad_query, "ctx", scatter_dimension=0, tiled=True),
        lax.psum_scatter(grad_down, "ctx", scatter_dimension=0, tiled=True),
        lax.psum_scatter(grad_latent_norm, "ctx", scatter_dimension=0, tiled=True),
        lax.psum_scatter(grad_latent_up, "ctx", scatter_dimension=0, tiled=True),
        lax.psum_scatter(grad_output, "ctx", scatter_dimension=1, tiled=True),
        lax.psum_scatter(summed[2], "ctx", scatter_dimension=0, tiled=True),
        lax.psum_scatter(summed[3], "ctx", scatter_dimension=0, tiled=True),
        lax.psum_scatter(grad_shared_gate, "ctx", scatter_dimension=0, tiled=True),
        lax.psum_scatter(grad_shared_up, "ctx", scatter_dimension=0, tiled=True),
        lax.psum_scatter(grad_shared_down, "ctx", scatter_dimension=1, tiled=True),
    )
    return (
        output.astype(jnp.bfloat16),
        tokens_gradient,
        reduced[0],
        reduced[1],
        reduced[2],
        reduced[3],
        reduced[4],
        reduced[5],
        reduced[6],
        reduced[7],
        reduced[8],
        reduced[9],
        reduced[10],
        grad_expert_gate,
        grad_expert_up,
        grad_expert_down,
    )


VMEM_LIMIT = 60 * 1024 * 1024
TILE = 256


def local_call(body, grid, in_specs, out_specs, out_shape, operands, after=()):
    inputs = len(in_specs)

    def run(*refs):
        body(*refs[:inputs], *refs[inputs + len(after) :])

    return pl.pallas_call(
        run,
        grid=grid,
        in_specs=list(in_specs) + [pl.BlockSpec(memory_space=pl.ANY)] * len(after),
        out_specs=out_specs,
        out_shape=out_shape,
        compiler_params=pltpu.CompilerParams(vmem_limit_bytes=VMEM_LIMIT),
        cost_estimate=pl.CostEstimate(flops=1, bytes_accessed=1, transcendentals=0),
    )(*operands, *after)


def whole(array):
    return pl.BlockSpec(array.shape, lambda *_: (0,) * array.ndim)


def by_rows(array, rows=TILE):
    return pl.BlockSpec((rows, array.shape[1]), lambda i: (i, 0))


def by_first(array):
    return pl.BlockSpec((1,) + array.shape[1:], lambda i: (i,) + (0,) * (array.ndim - 1))


def shaped(shape, dtype=jnp.bfloat16):
    return jax.ShapeDtypeStruct(shape, dtype)


def mul(left, right):
    return jnp.dot(left, right, preferred_element_type=jnp.float32)


def mul_nt(left, right):
    return lax.dot_general(
        left, right, (((1,), (1,)), ((), ())), preferred_element_type=jnp.float32
    )


def mul_tn(left, right):
    return lax.dot_general(
        left, right, (((0,), (0,)), ((), ())), preferred_element_type=jnp.float32
    )


def glu_back(gate, up, grads):
    sigmoid = 1.0 / (1.0 + jnp.exp(-gate))
    silu = gate * sigmoid
    slope = sigmoid * (1.0 + gate * (1.0 - sigmoid))
    return (silu * up, grads * up * slope, grads * silu)


def feed_body(
    experts, rows, back, shared_back, gate_t, up_t, small_t, named, pick,
    act_out, shared_act_out, gate_out, up_out, shared_out, gain_out,
):
    here = rows[...]
    part = small_t.shape[0] // 3
    small = mul_nt(here, small_t[...])
    logits = small[:, 2 * part :]
    ids = lax.broadcasted_iota(jnp.int32, logits.shape, 1)
    logits = jnp.where(ids < experts, logits, -1e30)
    chances = jnp.exp(logits - jnp.max(logits, axis=1, keepdims=True))
    total = jnp.sum(chances, axis=1, keepdims=True)
    named_here = named[...]
    share = jnp.sum(chances * pick[...], axis=1, keepdims=True) / total * named_here
    act, gate_grad, up_grad = glu_back(
        small[:, :part], small[:, part : 2 * part], shared_back[...].astype(jnp.float32)
    )
    shared_act_out[...] = act.astype(jnp.bfloat16)
    shared_out[:, :part] = gate_grad.astype(jnp.bfloat16)
    shared_out[:, part:] = up_grad.astype(jnp.bfloat16)
    grads = back[...].astype(jnp.float32)
    act, gate_grad, up_grad = glu_back(mul_nt(here, gate_t[...]), mul_nt(here, up_t[...]), grads)
    gain_out[...] = jnp.sum(act * grads, axis=1, keepdims=True) * named_here
    act_out[...] = (act * share).astype(jnp.bfloat16)
    gate_out[...] = (gate_grad * share).astype(jnp.bfloat16)
    up_out[...] = (up_grad * share).astype(jnp.bfloat16)


def feed_kernel(rows, back, shared_back, gate_t, up_t, small_t, named, pick, experts, after=()):
    count = rows.shape[0]
    hidden, part = (back.shape[1], shared_back.shape[1])
    shapes = [shaped((count, s)) for s in (hidden, part, hidden, hidden, 2 * part)]
    shapes.append(shaped((count, 1), jnp.float32))
    return local_call(
        partial(feed_body, experts),
        (count // TILE,),
        [
            by_rows(rows),
            by_rows(back),
            by_rows(shared_back),
            whole(gate_t),
            whole(up_t),
            whole(small_t),
            by_rows(named),
            whole(pick),
        ],
        [by_rows(s) for s in shapes],
        shapes,
        (rows, back, shared_back, gate_t, up_t, small_t, named, pick),
        after,
    )


def input_body(gate, up, shared, gate_t, up_t, small_t, gain, pick, out):
    width = gate_t.shape[1]
    used = shared.shape[1]
    out[:, :width] = (
        mul(gate[...], gate_t[...]) + mul(up[...], up_t[...]) + mul(shared[...], small_t[:used, :])
    ).astype(jnp.bfloat16)
    out[:, width:] = (gain[...] * pick[...]).astype(jnp.bfloat16)


def input_kernel(gate, up, shared, gate_t, up_t, small_t, gain, pick, after=()):
    count = gate.shape[0]
    shape = shaped((count, gate_t.shape[1] + pick.shape[1]))
    return local_call(
        input_body,
        (count // TILE,),
        [by_rows(gate), by_rows(up), by_rows(shared)]
        + [whole(gate_t), whole(up_t), whole(small_t), by_rows(gain), whole(pick)],
        by_rows(shape),
        shape,
        (gate, up, shared, gate_t, up_t, small_t, gain, pick),
        after,
    )


def result_body(act, shared_act, down, shared_down, out):
    out[...] = (mul(act[...], down[...]) + mul(shared_act[...], shared_down[...])).astype(
        jnp.bfloat16
    )


def result_kernel(act, shared_act, down, shared_down, after=()):
    count = act.shape[0]
    shape = shaped((count, down.shape[1]))
    return local_call(
        result_body,
        (count // TILE,),
        [by_rows(act), by_rows(shared_act), whole(down), whole(shared_down)],
        by_rows(shape),
        shape,
        (act, shared_act, down, shared_down),
        after,
    )


def weight_body(left_own, left_other, more_own, more_other, own, other, out, more_out):
    here, there = (own[...], other[...])
    out[...] = mul_tn(left_own[...], here) + mul_tn(left_other[...], there)
    more_out[...] = (mul_tn(more_own[...], here) + mul_tn(more_other[...], there)).astype(
        jnp.bfloat16
    )


def weight_kernel(lefts, mores, rights, side=0, part=128, after=()):
    count, width = rights[0].shape
    columns = lambda rows: pl.BlockSpec((rows, TILE), lambda i: (0, i))
    hidden, more = (lefts[0].shape[1], part)
    return local_call(
        weight_body,
        (width // TILE,),
        [whole(a) for a in lefts]
        + [pl.BlockSpec((count, part), lambda i: (0, side))] * 2
        + [columns(count)] * 2,
        [columns(hidden), columns(more)],
        [shaped((hidden, width), jnp.float32), shaped((more, width))],
        (*lefts, *mores, *rights),
        after,
    )


def head_parts_of(query, heads, nope):
    rope = query.shape[1] // heads - nope
    return [
        (
            query[:, k * nope : (k + 1) * nope],
            query[:, heads * nope + k * rope : heads * nope + (k + 1) * rope],
        )
        for k in range(heads)
    ]


def attend_body(
    heads, scale, query, own, other, up, out_weight, spots, key_spots,
    kept_out, sent_out, prob_out, absorbed_out, latent_out, head_out,
):
    rank = up.shape[0]
    absorbed, ropes = ([], [])
    for k, (nope, rope) in enumerate(head_parts_of(query[...], heads, DN)):
        key_up = up[:, k * (DN + DV) : k * (DN + DV) + DN]
        absorbed.append(mul_nt(nope, key_up).astype(jnp.bfloat16))
        ropes.append(rope)
    absorbed = jnp.concatenate(absorbed, axis=0)
    rope = jnp.concatenate(ropes, axis=0)
    absorbed_out[0] = absorbed
    keys = [source[0, k] for source in (own, other) for k in range(2)]
    scores = jnp.concatenate(
        [mul_nt(absorbed, key[:, :rank]) + mul_nt(rope, key[:, rank:]) for key in keys], axis=1
    )
    allowed = spots[...] >= key_spots[...]
    allowed = jnp.concatenate([allowed] * heads, axis=0)
    scores = jnp.where(allowed, scores * scale, -1e30)
    weights = jnp.exp(scores - jnp.max(scores, axis=1, keepdims=True))
    prob = (weights / jnp.sum(weights, axis=1, keepdims=True)).astype(jnp.bfloat16)
    prob_out[0] = prob
    size = keys[0].shape[0]
    latent = sum(
        mul(prob[:, j * size : (j + 1) * size], key[:, :rank]) for j, key in enumerate(keys)
    ).astype(jnp.bfloat16)
    latent_out[0] = latent
    rows = query.shape[0]
    head = jnp.concatenate(
        [
            mul(
                latent[k * rows : (k + 1) * rows],
                up[:, k * (DN + DV) + DN : (k + 1) * (DN + DV)],
            )
            for k in range(heads)
        ],
        axis=1,
    ).astype(jnp.bfloat16)
    head_out[...] = head
    total = mul(head, out_weight[...]).astype(jnp.bfloat16)
    kept_out[0] = total[: rows // 2]
    sent_out[0] = total[rows // 2 :]


def attend_kernel(query, own, other, up, out_weight, spots, key_spots, heads, scale, after=()):
    sequences = own.shape[0]
    rows = query.shape[0] // sequences
    key_count = 4 * own.shape[2]
    rank = up.shape[0]
    shapes = [
        shaped((sequences, rows // 2, out_weight.shape[1])),
        shaped((sequences, rows // 2, out_weight.shape[1])),
        shaped((sequences, heads * rows, key_count)),
        shaped((sequences, heads * rows, rank)),
        shaped((sequences, heads * rows, rank)),
        shaped((query.shape[0], heads * DV)),
    ]
    return local_call(
        partial(attend_body, heads, scale),
        (sequences,),
        [by_rows(query, rows), by_first(own), by_first(other)]
        + [whole(a) for a in (up, out_weight, spots, key_spots)],
        [by_first(shape) for shape in shapes[:5]] + [by_rows(shapes[5], rows)],
        shapes,
        (query, own, other, up, out_weight, spots, key_spots),
        after,
    )


def attend_back_body(
    heads, scale, grads, query, own, other, up, out_weight, prob, absorbed, latent,
    own_out, other_out, query_out, up_out,
):
    rank = up.shape[0]
    rows = query.shape[0]
    first = pl.program_id(0) == 0
    grads_here = grads[...]
    head_grad = mul_nt(grads_here, out_weight[...]).astype(jnp.bfloat16)
    span = lambda k: slice(k * rows, (k + 1) * rows)
    latent_grad = []
    value_parts = []
    for k in range(heads):
        mine = head_grad[:, k * DV : (k + 1) * DV]
        value_up = up[:, k * (DN + DV) + DN : (k + 1) * (DN + DV)]
        latent_grad.append(mul_nt(mine, value_up).astype(jnp.bfloat16))
        value_parts.append(mul_tn(latent[0, span(k)], mine))
    latent_grad = jnp.concatenate(latent_grad, axis=0)
    keys = [source[0, k] for source in (own, other) for k in range(2)]
    size = keys[0].shape[0]
    prob_here = prob[0]
    prob_wide = prob_here.astype(jnp.float32)
    prob_grad = jnp.concatenate([mul_nt(latent_grad, key[:, :rank]) for key in keys], axis=1)
    inner = jnp.sum(prob_wide * prob_grad, axis=1, keepdims=True)
    score_grad = (prob_wide * (prob_grad - inner)).astype(jnp.bfloat16)
    absorbed_here = absorbed[0]
    parts = head_parts_of(query[...], heads, DN)
    rope = jnp.concatenate([part[1] for part in parts], axis=0)
    wide = 0.0
    narrow = 0.0
    for j, key in enumerate(keys):
        piece = score_grad[:, j * size : (j + 1) * size]
        wide = wide + mul(piece, key[:, :rank])
        narrow = narrow + mul(piece, key[:, rank:])
        target = (own_out, other_out)[j // 2]
        value = mul_tn(prob_here[:, j * size : (j + 1) * size], latent_grad)
        target[0, j % 2, :, :rank] = (mul_tn(piece, absorbed_here) * scale + value).astype(
            jnp.bfloat16
        )
        target[0, j % 2, :, rank:] = (mul_tn(piece, rope) * scale).astype(jnp.bfloat16)
    wide = (wide * scale).astype(jnp.bfloat16)
    narrow = narrow * scale
    for k in range(heads):
        start = k * (DN + DV)
        key_part = mul_tn(wide[span(k)], parts[k][0])
        up_out[:, start : start + DN] = (
            jnp.where(first, 0.0, up_out[:, start : start + DN]) + key_part
        )
        up_out[:, start + DN : start + DN + DV] = (
            jnp.where(first, 0.0, up_out[:, start + DN : start + DN + DV]) + value_parts[k]
        )
        query_out[:, k * DN : (k + 1) * DN] = mul(wide[span(k)], up[:, start : start + DN])
        rope_size = narrow.shape[1]
        at = heads * DN + k * rope_size
        query_out[:, at : at + rope_size] = narrow[span(k)]


def attend_back_kernel(
    grads, query, own, other, up, out_weight, prob, absorbed, latent, heads, scale, after=()
):
    sequences = own.shape[0]
    rows = query.shape[0] // sequences
    shapes = [
        shaped(own.shape),
        shaped(own.shape),
        shaped(query.shape, jnp.float32),
        shaped(up.shape, jnp.float32),
    ]
    return local_call(
        partial(attend_back_body, heads, scale),
        (sequences,),
        [by_rows(grads, rows), by_rows(query, rows), by_first(own), by_first(other)]
        + [whole(up), whole(out_weight), by_first(prob), by_first(absorbed), by_first(latent)],
        [by_first(own), by_first(own), by_rows(query, rows), whole(up)],
        shapes,
        (grads, query, own, other, up, out_weight, prob, absorbed, latent),
        after,
    )


def heads_body(parts, *refs):
    query_out, up_out, out_out = refs
    count, groups, rows, _ = parts.shape
    query_columns = query_out.shape[1]
    up_blocks = up_out.shape[1] // 128
    up_rows = rows // up_blocks
    heads = out_out.shape[0] // rows
    for block in range(count * groups):
        here = parts[block // groups, block % groups]
        span = slice(block * rows, (block + 1) * rows)
        query_out[span, :] = here[:, :query_columns]
        for k in range(up_blocks):
            up_out[block * up_rows : (block + 1) * up_rows, k * 128 : (k + 1) * 128] = here[
                k * up_rows : (k + 1) * up_rows, query_columns : query_columns + 128
            ]
        for k in range(heads):
            at = query_columns + 128 + k * rows
            out_out[k * rows : (k + 1) * rows, span] = here[:, at : at + rows]


def heads_kernel(parts, query_columns, heads, up_columns, after=()):
    count, groups, rows, _ = parts.shape
    width = count * groups * rows
    up_rows = rows * 128 // up_columns
    shapes = [
        shaped((width, query_columns)),
        shaped((count * groups * up_rows, up_columns)),
        shaped((heads * rows, width)),
    ]
    return local_call(
        heads_body,
        (1,),
        [whole(parts)],
        [whole(s) for s in shapes],
        shapes,
        (parts,),
        after,
    )


SCALAR = pl.BlockSpec(memory_space=pltpu.SMEM)


def out_grads_body(rows, z, head, grads, *outs):
    heads = head.shape[1] // rows
    for s, out in enumerate(outs):
        size = out.shape[0] * rows
        start = pl.multiple_of(lax.rem(z[0] + s, len(outs)) * size, size)
        total = mul_tn(head[...], grads[:, pl.ds(start, size)]).astype(jnp.bfloat16)
        for j in range(out.shape[0]):
            for k in range(heads):
                out[j, :, k * rows : (k + 1) * rows] = total[
                    k * rows : (k + 1) * rows, j * rows : (j + 1) * rows
                ]


def out_grads_kernel(z, count, head, grads, rows):
    shapes = [shaped((grads.shape[1] // (rows * count), rows, head.shape[1]))] * count
    return local_call(
        partial(out_grads_body, rows),
        (1,),
        [SCALAR, whole(head), whole(grads)],
        [whole(s) for s in shapes],
        shapes,
        (z, head, grads),
    )


def query_grads_body(rows, grads, source, up, more, out):
    columns = grads.shape[1]
    up_blocks = up.shape[1] // 128
    up_rows = rows // up_blocks
    here = grads[...]
    for i in range(out.shape[0]):
        span = slice(i * rows, (i + 1) * rows)
        out[i, :, :columns] = mul_tn(source[:, span], here).astype(jnp.bfloat16)
        for k in range(up_blocks):
            out[i, k * up_rows : (k + 1) * up_rows, columns : columns + 128] = up[
                i * up_rows : (i + 1) * up_rows, k * 128 : (k + 1) * 128
            ].astype(jnp.bfloat16)
        out[i, :, columns + 128 :] = more[i]


def query_grads_kernel(grads, source, up, more, rows):
    shape = shaped((source.shape[1] // rows, rows, grads.shape[1] + 128 + more.shape[2]))
    return local_call(
        partial(query_grads_body, rows),
        (1,),
        [whole(grads), whole(source), whole(up), whole(more)],
        whole(shape),
        shape,
        (grads, source, up, more),
    )


def latent_grads_body(z, place, source, grads, *outs):
    rows = outs[0].shape[0]
    here = grads[...]
    for s, out in enumerate(outs):
        block = 4 * lax.rem(z[0] + s, len(outs)) + place[0]
        start = pl.multiple_of(block * rows, rows)
        out[...] = mul_tn(source[:, pl.ds(start, rows)], here).astype(jnp.bfloat16)


def latent_grads_kernel(z, place, count, source, grads, rows):
    shapes = [shaped((rows, grads.shape[1]))] * count
    return local_call(
        latent_grads_body,
        (1,),
        [SCALAR, SCALAR, whole(source), whole(grads)],
        [whole(s) for s in shapes],
        shapes,
        (z, place, source, grads),
    )


def split_product_body(left, right, kept_out, sent_out):
    total = mul_nt(left[...], right[...]).astype(jnp.bfloat16)
    half = total.shape[0] // 2
    kept_out[0] = total[:half]
    sent_out[0] = total[half:]


def split_product_kernel(left, right, sequences, after=()):
    rows = left.shape[0] // sequences
    shapes = [shaped((sequences, rows // 2, right.shape[0]))] * 2
    return local_call(
        split_product_body,
        (sequences,),
        [by_rows(left, rows), whole(right)],
        [by_first(s) for s in shapes],
        shapes,
        (left, right),
        after,
    )


def core_fold_body(*refs):
    for k in range(4):
        total = refs[k][0, 0].astype(jnp.float32) + refs[4 + k][0, 0].astype(jnp.float32)
        refs[8 + k][0] = total.astype(jnp.bfloat16)


def core_fold_kernel(own, received, after=()):
    half, width = (own.shape[2] // 2, own.shape[3])
    block = (1, 1, half, width)
    specs = [
        pl.BlockSpec(block, lambda k: (0, k, 0, 0)),
        pl.BlockSpec(block, lambda k: (1, k, 0, 0)),
        pl.BlockSpec(block, lambda k: (k, 0, 1, 0)),
        pl.BlockSpec(block, lambda k: (k, 1, 1, 0)),
    ]
    shapes = [shaped((2, half, width))] * 4
    return local_call(
        core_fold_body,
        (2,),
        specs + specs,
        [by_first(s) for s in shapes],
        shapes,
        (own,) * 4 + (received,) * 4,
        after,
    )


def plane_fold_body(lower, lower_got, upper, upper_got, *outs):
    for k, (left, right) in enumerate(((lower, lower_got), (upper, upper_got))):
        for j in range(2):
            total = left[j].astype(jnp.float32) + right[j].astype(jnp.float32)
            outs[2 * k + j][...] = total.astype(jnp.bfloat16)


def plane_fold_kernel(lower, lower_got, upper, upper_got, after=()):
    _, rows, width = lower.shape
    tile = max(16, rows // 2)
    spec = pl.BlockSpec((2, tile, width), lambda i: (0, i, 0))
    shapes = [shaped((rows, width))] * 4
    return local_call(
        plane_fold_body,
        (rows // tile,),
        [spec] * 4,
        [by_rows(s, tile) for s in shapes],
        shapes,
        (lower, lower_got, upper, upper_got),
        after,
    )


def slab_fold_body(lower, lower_got, upper, upper_got, own_out, *outs):
    half = lower.shape[0]
    count = len(outs) + 1
    block = 2 * half // count
    for k, (left, right) in enumerate(((lower, lower_got), (upper, upper_got))):
        total = left[...].astype(jnp.float32) + right[...].astype(jnp.float32)
        if count == 1:
            own_out[k * half : (k + 1) * half, :] = total
            continue
        for j in range(half // block):
            here = total[j * block : (j + 1) * block]
            s = k * (half // block) + j
            if s == 0:
                own_out[...] = here
            else:
                outs[s - 1][...] = here.astype(jnp.bfloat16)


def slab_fold_kernel(lower, lower_got, upper, upper_got, count, after=()):
    half, width = lower.shape
    block = 2 * half // count
    shapes = [shaped((block, width), jnp.float32)] + [shaped((block, width))] * (count - 1)
    return local_call(
        slab_fold_body,
        (1,),
        [whole(lower)] * 4,
        [whole(s) for s in shapes],
        shapes,
        (lower, lower_got, upper, upper_got),
        after,
    )


def z_fold_body(*refs):
    total = refs[0][...].astype(jnp.float32)
    for ref in refs[1:-1]:
        total = total + ref[...].astype(jnp.float32)
    refs[-1][...] = total.astype(refs[-1].dtype)


def z_fold_kernel(parts, dtype, after=()):
    shape = shaped(parts[0].shape, dtype)
    return local_call(
        z_fold_body, (1,), [whole(p) for p in parts], whole(shape), shape, tuple(parts), after
    )


def product_nt_body(left, right, out):
    out[...] = mul_nt(left[...], right[...]).astype(jnp.bfloat16)


def product_nt_kernel(left, right, after=()):
    shape = shaped((left.shape[0], right.shape[0]))
    return local_call(
        product_nt_body,
        (left.shape[0] // TILE,),
        [by_rows(left), whole(right)],
        by_rows(shape),
        shape,
        (left, right),
        after,
    )


def join_body(*refs):
    out = refs[-1]
    at = 0
    for ref in refs[:-1]:
        out[at : at + ref.shape[0], :] = ref[...]
        at += ref.shape[0]


def join_kernel(parts, after=(), more=()):
    parts = list(parts) + list(more)
    shape = shaped((sum(p.shape[0] for p in parts), parts[0].shape[1]), parts[0].dtype)
    return local_call(
        join_body, (1,), [whole(p) for p in parts], whole(shape), shape, tuple(parts), after
    )


def reorder_body(places, *refs):
    del places
    out = refs[-1]
    rows = refs[0].shape[1]
    for s in range(4):
        out[s * rows : (s + 1) * rows, :] = refs[s][0]


def reorder_kernel(places, blocks, after):
    _, rows, width = blocks.shape
    count = places.shape[0]
    step = lambda s: pl.BlockSpec((1, rows, width), lambda i, places: (places[4 * i + s], 0, 0))
    return pl.pallas_call(
        lambda places, a, b, c, d, dep, out: reorder_body(places, a, b, c, d, out),
        grid_spec=pltpu.PrefetchScalarGridSpec(
            num_scalar_prefetch=1,
            grid=(count // 4,),
            in_specs=[step(s) for s in range(4)] + [pl.BlockSpec(memory_space=pl.ANY)],
            out_specs=pl.BlockSpec((4 * rows, width), lambda i, places: (i, 0)),
        ),
        out_shape=shaped((count * rows, width)),
        compiler_params=pltpu.CompilerParams(vmem_limit_bytes=VMEM_LIMIT),
        cost_estimate=pl.CostEstimate(flops=1, bytes_accessed=1, transcendentals=0),
    )(places, *[blocks] * 4, after)


CTX = ("z", "x", "c")


def swap(value, axis):
    return lax.ppermute(value, axis, [(0, 1), (1, 0)])


def from_z(value, steps):
    count = lax.axis_size("z")
    return lax.ppermute(value, "z", [((i + steps) % count, i) for i in range(count)])


def to_z(value, steps):
    count = lax.axis_size("z")
    return lax.ppermute(value, "z", [(i, (i + steps) % count) for i in range(count)])


def trade(value, axes):
    return lax.all_to_all(value, axes, split_axis=0, concat_axis=0, tiled=True)


def add(left, right):
    return left.astype(jnp.float32) + right.astype(jnp.float32)


def low(value):
    return value.astype(jnp.bfloat16)


def dot(left, right):
    return jnp.dot(left, right, preferred_element_type=jnp.float32)


def dot_nt(left, right):
    return lax.dot_general(
        left, right, (((1,), (1,)), ((), ())), preferred_element_type=jnp.float32
    )


def dot_tn(left, right):
    return lax.dot_general(
        left, right, (((0,), (0,)), ((), ())), preferred_element_type=jnp.float32
    )


def by_own(value, axis_name, dim):
    flipped = jnp.flip(value, axis=dim)
    return jnp.where(lax.axis_index(axis_name) == 0, value, flipped)


def tie(value, *others):
    if not others:
        return value
    zero = sum(other[(0,) * other.ndim].astype(jnp.float32) for other in others) * 0.0
    return value + zero.astype(value.dtype)


def rows_first(value):
    return with_layout_constraint(value, Layout(major_to_minor=tuple(range(value.ndim))))


def put(parts, places):
    whole = jnp.zeros((len(parts),) + parts[0].shape, parts[0].dtype)
    for part, place in zip(parts, places):
        whole = lax.dynamic_update_index_in_dim(whole, part, place, 0)
    return rows_first(whole)


def z_parts(value):
    return [value] + [from_z(value, s) for s in range(1, lax.axis_size("z"))]


def put_z(parts):
    z = lax.axis_index("z")
    count = len(parts)
    return put(parts, [(z + s) % count for s in range(count)])


def gather_plane(rows, axes=("x", "y"), gates=()):
    half = rows.shape[0] // 2
    over_a = tie(swap(rows, axes[0]), *gates)
    over_b = tie(swap(rows, axes[1]), *gates)
    both = jnp.concatenate([swap(over_b[:half], axes[0]), swap(over_a[half:], axes[1])], axis=0)
    return jnp.stack([jnp.stack([rows, over_b]), jnp.stack([over_a, both])])


def fold_first(pieces, axes, after=()):
    lower, lower_sent, upper, upper_sent = pieces
    return plane_fold_kernel(
        lower, swap(lower_sent, axes[0]), upper, swap(upper_sent, axes[1]), after
    )


def fold_second(pieces, axes, count, after=()):
    lower, lower_sent, upper, upper_sent = pieces
    return slab_fold_kernel(
        lower, swap(lower_sent, axes[1]), upper, swap(upper_sent, axes[0]), count, after
    )


def fold_z(parts, dtype=jnp.float32, after=()):
    received = [to_z(part, s + 1) for s, part in enumerate(parts[1:])]
    return z_fold_kernel([parts[0]] + received, dtype, after)


def spread_z(rows):
    return jnp.concatenate(z_parts(rows), axis=0)


def both_halves(rows):
    other = swap(rows, "y")
    return by_own(jnp.stack([rows, other]), "y", 0)


def dense_shards(
    tokens,
    norm_in,
    query_weight,
    latent_down,
    latent_norm,
    latent_up,
    output_weight,
    norm_ffn,
    router_weight,
    shared_gate,
    shared_up,
    shared_down,
    expert_gate,
    expert_up,
    expert_down,
    routes,
    cotangent,
):
    zs = lax.axis_size("z")
    z, x, c = (lax.axis_index("z"), lax.axis_index("x"), lax.axis_index("c"))
    me = (z * 2 + x) * 2 + c
    sequences, block, width = tokens.shape
    count = 4 * zs
    rows_here = width // count
    slab = 4 * block
    experts = router_weight.shape[1]
    shared_here = shared_gate.shape[1] // count
    part = -(-max(shared_here, experts) // 128) * 128
    heads = latent_up.shape[1] // (4 * (DN + DV))
    query_columns = heads * (DN + DR)
    rank_rows = R // count
    head_rows = heads * DV
    scale = (DN + DR) ** (-0.5)

    latent_column = jnp.pad(latent_norm, (0, rows_here - rank_rows))[:, None]
    small = jnp.concatenate(
        [
            latent_down,
            router_weight,
            norm_in[:, None],
            norm_ffn[:, None],
            latent_column,
            routes.reshape(sequences * block, TOPK).astype(jnp.bfloat16),
        ],
        axis=1,
    )
    small_parts = z_parts(jnp.pad(small, ((0, 0), (0, -small.shape[1] % 128))))
    up_columns = heads * (DN + DV)
    up_part = jnp.transpose(
        latent_up.reshape(rank_rows, 4, up_columns // 128, 128), (1, 2, 0, 3)
    ).reshape(4, rows_here, 128)
    out_part = jnp.transpose(output_weight.reshape(4, heads, DV, rows_here), (0, 2, 1, 3)).reshape(
        4, DV, heads * rows_here
    )
    by_heads = query_weight.reshape(rows_here, 4, heads, DN + DR)
    by_heads = jnp.concatenate(
        [
            by_heads[..., :DN].reshape(rows_here, 4, heads * DN),
            by_heads[..., DN:].reshape(rows_here, 4, heads * DR),
        ],
        axis=2,
    )
    by_heads = jnp.transpose(by_heads, (1, 0, 2))
    by_heads = jnp.concatenate([by_heads, up_part, out_part], axis=2)
    mine_at = 2 * x + c
    for_group = [
        lax.dynamic_index_in_dim(by_heads, mine_at ^ k, 0, keepdims=False) for k in range(4)
    ]
    by_heads = put(
        [
            for_group[0],
            swap(for_group[1], "c"),
            swap(for_group[2], "x"),
            lax.ppermute(for_group[3], ("x", "c"), [(k, 3 - k) for k in range(4)]),
        ],
        [mine_at ^ k for k in range(4)],
    )
    small = put_z([tie(part, by_heads) for part in small_parts])
    at = R + DR
    down_here = small[:, :, :at]
    rest = small[:, :, at:]
    down_here = down_here.reshape(-1, R + DR)
    down_x = swap(down_here, "x")
    down_pieces = (down_here, down_x, swap(down_here, "c"), swap(down_x, "c"))
    own_gain = rest[:, :, experts].reshape(1, zs * rows_here).astype(jnp.float32)
    rest = jnp.stack([rest, swap(rest, "x")], axis=1)
    rest = jnp.stack([rest, swap(rest, "c")], axis=2)
    rest = by_own(by_own(rest, "x", 1), "c", 2).reshape(count, rows_here, -1)
    full_router = rest[:, :, :experts].reshape(width, experts)
    full_norm_in = rest[:, :, experts].reshape(width).astype(jnp.float32)
    full_norm_ffn = rest[:, :, experts + 1].reshape(width).astype(jnp.float32)
    full_latent_norm = rest[:, :rank_rows, experts + 2].reshape(R).astype(jnp.float32)
    all_routes = rest[:, :, experts + 3 : experts + 3 + TOPK]

    mine = by_own(tokens, "y", 0)
    line = jnp.stack([mine, swap(mine, "x")], axis=1)
    line = jnp.stack([line, swap(line, "c")], axis=1)
    source = line.reshape(sequences * slab, width).astype(jnp.float32)
    grad_mine = by_own(cotangent, "y", 0)[0]
    all_grads = lax.all_gather(tie(grad_mine, by_heads), CTX + ("y",), axis=0)
    one = jnp.arange(2)
    order = (
        (((z + jnp.arange(zs)) % zs)[None, None, None, :] * 2 + (x ^ one)[None, :, None, None]) * 2
        + (c ^ one)[:, None, None, None]
    ) * 2 + (lax.axis_index("y") ^ one)[None, None, :, None]
    order = order.reshape(-1).astype(jnp.int32)
    gate_t, up_t, down = (expert_gate[0].T, expert_up[0].T, expert_down[0])
    query_here, up_here, out_here = heads_kernel(
        lax.all_gather(by_heads, "z", axis=0),
        query_columns,
        heads,
        up_columns,
    )

    def places(turns):
        two = jnp.arange(2)
        base = (
            ((z + turns[None, None, :]) % zs) * 4
            + (x ^ two[None, :, None]) * 2
            + (c ^ two[:, None, None])
        )
        return (base[..., None] * block + jnp.arange(block)).reshape(-1)

    positions = places(jnp.arange(1))
    key_positions = places(jnp.arange(zs))
    cosine, sine = rotary_tables(positions, DR)
    normed, unit_in, inverse_in = root_norm(source, full_norm_in)
    input_low = low(normed)

    own_rows = line[0].reshape(slab, width)
    own_columns = jnp.concatenate(
        [
            lax.dynamic_slice_in_dim(own_rows, (4 * k + 2 * x + c) * rows_here, rows_here, 1)
            for k in range(zs)
        ],
        axis=1,
    ).astype(jnp.float32)
    latent_part = dot(
        low(own_columns * inverse_in[:slab] * own_gain), down_here
    )
    latent_part = low(latent_part).reshape(2, 2, block, R + DR)
    latent_part = low(add(latent_part[0], swap(latent_part[1], "c")))
    latent_raw = add(latent_part[0], swap(latent_part[1], "x"))
    latent_scaled, latent_unit, latent_inverse = root_norm(latent_raw[:, :R], full_latent_norm)
    key_own = low(
        jnp.concatenate(
            [latent_scaled, rotate(latent_raw[:, R:], cosine[:block], sine[:block])], axis=-1
        )
    )
    plane = gather_plane(spread_z(key_own), ("y", "x"))
    keys_own, keys_other = (plane, swap(plane, "c"))
    query = dot(input_low, query_here)
    rope = query[:, heads * DN :].reshape(sequences, slab, heads, DR)
    rope = rotate(rope, cosine[:, None, :], sine[:, None, :]).reshape(sequences * slab, -1)
    query_low = low(jnp.concatenate([query[:, : heads * DN], rope], axis=1))

    shared_mine = jnp.concatenate(
        [
            shared_gate.T.reshape(count, shared_here, rows_here),
            shared_up.T.reshape(count, shared_here, rows_here),
            shared_down.reshape(count, shared_here, rows_here),
        ],
        axis=1,
    )
    shared_rows = trade(tie(shared_mine, query_low), CTX)
    shared_got = shared_rows
    shared_rows = jnp.transpose(shared_rows, (1, 0, 2)).reshape(3, shared_here, width)
    shared_rows = jnp.pad(shared_rows, ((0, 0), (0, part - shared_here), (0, 0)))
    small_t = jnp.concatenate(
        [
            shared_rows[0],
            shared_rows[1],
            jnp.pad(full_router.T, ((0, part - experts), (0, 0))),
        ]
    )
    shared_down_t = shared_rows[2]

    def scatter_slab(kept, sent, after=()):
        shape = (2, 2, block, width)
        pieces = core_fold_kernel(kept.reshape(shape), swap(sent, "c").reshape(shape))
        return fold_second(fold_first(pieces, ("y", "x"), after), ("y", "x"), 1)[0]

    def gather_slab(rows):
        plane = gather_plane(rows, ("y", "x"))
        return jnp.stack([plane, swap(plane, "c")], axis=1).reshape(sequences * slab, -1)

    kept, sent, prob, absorbed, latent_out, head_out = attend_kernel(
        query_low,
        keys_own,
        keys_other,
        up_here,
        out_here,
        positions[:, None],
        key_positions[None, :],
        heads,
        scale,
        down_pieces[1:],
    )
    attention = scatter_slab(kept, sent)
    hidden_in = mine[0].astype(jnp.float32) + attention
    normed_ffn, unit_ffn, inverse_ffn = root_norm(hidden_in, full_norm_ffn)
    ffn_low = low(normed_ffn)
    shares = jax.nn.softmax(dot(ffn_low, full_router), axis=-1)
    half_places = order.shape[0] // 2
    grads_own = reorder_kernel(order[:half_places], all_grads, ffn_low)
    grads_other = reorder_kernel(order[half_places:], all_grads, ffn_low)
    ffn_parts = z_parts(ffn_low)
    back_own = product_nt_kernel(grads_own, down)
    back_other = product_nt_kernel(grads_other, down, (back_own,))
    ffn_slabs = join_kernel(ffn_parts, (shared_got, back_other))
    shared_own = product_nt_kernel(grads_own, shared_down_t, (ffn_slabs,))
    shared_other = product_nt_kernel(grads_other, shared_down_t, (shared_own,))
    half = ffn_slabs.shape[0] // 2
    over_x, over_y = (swap(ffn_slabs, "x"), swap(ffn_slabs, "y"))
    ffn_own = join_kernel(
        [ffn_slabs, over_y, over_x],
        (shared_other,),
        [swap(over_y[:half], "x"), swap(over_x[half:], "y")],
    )
    ffn_other = swap(ffn_own, "c").reshape(-1, width)

    relative = all_routes.reshape(zs, 2, 2, sequences, block, TOPK)
    relative = by_own(by_own(by_own(relative, "x", 1), "c", 2), "y", 3)
    relative = jnp.roll(relative, -z, axis=0)
    routed = jnp.any(relative == me.astype(jnp.bfloat16), axis=-1)
    routed = jnp.transpose(routed, (2, 1, 3, 0, 4)).reshape(2, -1, 1).astype(jnp.float32)
    pick = (jnp.arange(part)[None, :] == me).astype(jnp.float32)

    def feed(rows, back, shared_back, named, after=()):
        return feed_kernel(
            rows, back, shared_back, gate_t, up_t, small_t, named, pick, experts, after
        )

    act_own, more_own, gate_own, up_own, pre_own, gain_own = feed(
        ffn_own, back_own, shared_own, routed[0]
    )
    act_other, more_other, gate_other, up_other, pre_other, gain_other = feed(
        ffn_other, back_other, shared_other, routed[1], (act_own,)
    )
    shape = (2, 2, zs * block, width + part)
    grad_other = input_kernel(
        gate_other, up_other, pre_other, gate_t, up_t, small_t, gain_other, pick
    )
    grad_own = input_kernel(
        gate_own, up_own, pre_own, gate_t, up_t, small_t, gain_own, pick, (grad_other,)
    )
    pieces = core_fold_kernel(grad_own.reshape(shape), swap(grad_other, "c").reshape(shape))
    both_axes = ("x", "y")
    sum_other = result_kernel(act_other, more_other, down, shared_down_t, pieces)
    sum_own = result_kernel(act_own, more_own, down, shared_down_t, (sum_other,))
    grad_expert_up, shared_up_back = weight_kernel(
        (up_own, up_other), (pre_own, pre_other), (ffn_own, ffn_other), 1, part, (sum_own,)
    )
    pieces = fold_first(pieces, both_axes, (grad_expert_up,))
    shape = (2, 2, zs * block, width)
    grad_expert_down, shared_down_back = weight_kernel(
        (act_own, act_other), (more_own, more_other), (grads_own, grads_other), 0, part, pieces
    )
    grad_slab = fold_second(pieces, both_axes, zs, (grad_expert_down,))
    routed_pieces = core_fold_kernel(
        sum_own.reshape(shape), swap(sum_other, "c").reshape(shape), grad_slab
    )
    grad_expert_gate, shared_gate_back = weight_kernel(
        (gate_own, gate_other),
        (pre_own, pre_other),
        (ffn_own, ffn_other),
        0,
        part,
        tuple(routed_pieces),
    )
    routed_pieces = fold_first(routed_pieces, both_axes, (grad_expert_gate,))
    ffn_grad = fold_z(grad_slab, jnp.float32, routed_pieces)
    share_grad = ffn_grad[:, width : width + experts]
    ffn_grad = ffn_grad[:, :width]
    logit_grad = shares * (share_grad - jnp.sum(shares * share_grad, axis=-1, keepdims=True))
    ffn_grad = ffn_grad + dot_nt(low(logit_grad), full_router)
    grad_router = dot_tn(ffn_low, low(logit_grad))
    hidden_part, grad_norm_ffn = root_norm_back(ffn_grad, unit_ffn, inverse_ffn, full_norm_ffn)
    grad_hidden = grad_mine.astype(jnp.float32) + hidden_part

    hidden_low = low(grad_hidden)
    attention_grad = gather_slab(hidden_low)
    shared_back = jnp.concatenate(
        [
            shared_gate_back[:shared_here],
            shared_up_back[:shared_here],
            shared_down_back[:shared_here],
        ]
    )
    shared_back = trade(
        jnp.transpose(shared_back.reshape(-1, count, rows_here), (1, 0, 2)), CTX
    )
    zero = jnp.zeros((1,), jnp.int32)
    (out_grads,) = out_grads_kernel(zero, 1, head_out, attention_grad, rows_here)
    key_own, key_other, query_grad, grad_up_here = attend_back_kernel(
        attention_grad,
        query_low,
        keys_own,
        keys_other,
        up_here,
        out_here,
        prob,
        absorbed,
        latent_out,
        heads,
        scale,
        (out_grads,),
    )
    rope = query_grad[:, heads * DN :].reshape(sequences, slab, heads, DR)
    rope = rotate(rope, cosine[:, None, :], -sine[:, None, :]).reshape(sequences * slab, -1)
    query_raw_grad = low(jnp.concatenate([query_grad[:, : heads * DN], rope], axis=1))
    query_grads = query_grads_kernel(
        query_raw_grad, input_low, grad_up_here, out_grads, rows_here
    )
    grad_heads = lax.psum_scatter(query_grads, "z", scatter_dimension=0, tiled=True)
    key_pieces = core_fold_kernel(key_own, swap(key_other, "c"), (query_grads, shared_back))
    input_grad = scatter_slab(
        *split_product_kernel(query_raw_grad, query_here, sequences, (query_grads,))
    )
    key_slab = fold_second(fold_first(key_pieces, ("y", "x")), ("y", "x"), zs)
    key_sum = fold_z(key_slab)
    routed_slab = fold_second(routed_pieces, both_axes, zs, (key_sum,))
    latent_back, grad_latent_norm = root_norm_back(
        key_sum[:, :R], latent_unit, latent_inverse, full_latent_norm
    )
    rope_key = rotate(key_sum[:, R:], cosine[:block], -sine[:block])
    latent_raw_grad = low(jnp.concatenate([latent_back, rope_key], axis=-1))
    slab_latent_grad = gather_slab(latent_raw_grad)
    down_grads = latent_grads_kernel(
        z[None], (2 * x + c)[None], zs, input_low, slab_latent_grad, rows_here
    )
    latent_raw_grad = tie(latent_raw_grad, down_grads[0])
    shared_back = shared_back.astype(jnp.float32)
    grad_shared_gate = shared_back[:, :shared_here].reshape(-1, rows_here).T
    grad_shared_up = shared_back[:, shared_here : 2 * shared_here].reshape(-1, rows_here).T
    grad_shared_down = shared_back[:, 2 * shared_here :].reshape(-1, rows_here)


    latent_input = jnp.stack([dot_nt(latent_raw_grad, down) for down in down_pieces])
    latent_input = latent_input.reshape(2, 2, block, zs, rows_here)
    latent_input = by_own(by_own(latent_input, "c", 0), "x", 1)
    input_grad = input_grad + jnp.transpose(latent_input, (2, 3, 1, 0, 4)).reshape(block, width)
    source_part, grad_norm_in = root_norm_back(
        input_grad, unit_in[:block], inverse_in[:block], full_norm_in
    )
    tokens_gradient = both_halves(low(grad_hidden + source_part)).astype(jnp.float32)

    group = by_own(by_own(grad_heads.reshape((2, 2) + grad_heads.shape[1:]), "x", 0), "c", 1)
    crossed = lax.ppermute(group[1, 1], ("x", "c"), [(k, 3 - k) for k in range(4)])
    traded = jnp.stack(
        [
            jnp.stack([group[0, 0], swap(group[0, 1], "c")]),
            jnp.stack([swap(group[1, 0], "x"), crossed]),
        ]
    )
    traded = by_own(by_own(traded, "x", 0), "c", 1).reshape(grad_heads.shape)
    both = traded.astype(jnp.float32)
    output = both_halves(low(hidden_in + fold_z(routed_slab, jnp.float32, (traded,))))
    grad_down = fold_z(down_grads, jnp.float32, (traded,))
    out_at = both.shape[2] - head_rows
    grad_output = jnp.transpose(
        both[..., out_at:].reshape(4, DV, heads, rows_here), (0, 2, 1, 3)
    ).reshape(-1, rows_here)
    grad_query = jnp.transpose(both[..., :query_columns], (1, 0, 2))
    grad_query = jnp.concatenate(
        [
            grad_query[..., : heads * DN].reshape(rows_here, 4, heads, DN),
            grad_query[..., heads * DN :].reshape(rows_here, 4, heads, DR),
        ],
        axis=-1,
    ).reshape(rows_here, -1)
    grad_latent_up = jnp.transpose(
        both[..., query_columns:out_at].reshape(4, up_columns // 128, rank_rows, 128), (2, 0, 1, 3)
    ).reshape(rank_rows, -1)

    small_grads = jnp.concatenate(
        [
            grad_router.T.reshape(experts, count, rows_here),
            grad_norm_in.reshape(1, count, rows_here),
            grad_norm_ffn.reshape(1, count, rows_here),
            jnp.pad(
                grad_latent_norm.reshape(1, count, rank_rows),
                ((0, 0), (0, 0), (0, rows_here - rank_rows)),
            ),
        ]
    )
    small_grads = trade(jnp.transpose(small_grads, (1, 0, 2)), CTX)
    small_grads = jnp.sum(small_grads, axis=0)
    small_grads = small_grads + swap(small_grads, "y")
    return (
        output,
        tokens_gradient,
        small_grads[experts],
        grad_query,
        grad_down,
        small_grads[experts + 2, :rank_rows],
        grad_latent_up,
        grad_output,
        small_grads[experts + 1],
        small_grads[:experts].T,
        grad_shared_gate,
        grad_shared_up,
        grad_shared_down,
        grad_expert_gate.T[None],
        grad_expert_up.T[None],
        grad_expert_down[None],
    )


IN_SPECS = (
    (None, "ctx", None),
    ("ctx",),
    ("ctx", "wa"),
    ("ctx", None),
    ("ctx",),
    ("ctx", "wa"),
    ("wa", "ctx"),
    ("ctx",),
    ("ctx", None),
    ("ctx", "wa"),
    ("ctx", "wa"),
    ("wa", "ctx"),
    ("ctx", None, "wa"),
    ("ctx", None, "wa"),
    ("ctx", "wa", None),
    (None, "ctx", None),
    (None, "ctx", None),
)
OUT_SPECS = ((None, "ctx", None),) * 2 + IN_SPECS[1:15]


def solution(mesh):
    count = mesh.shape["ctx"]

    def run(*arguments):
        experts = arguments[12].shape[0]
        if experts > 4 * TOPK or experts != count or mesh.shape["wa"] != 2 or count % 8:
            return jax.shard_map(
                shards,
                mesh=mesh,
                in_specs=tuple(P(*spec) for spec in IN_SPECS),
                out_specs=tuple(P(*spec) for spec in OUT_SPECS),
                check_vma=False,
            )(*arguments)
        grid = Mesh(mesh.devices.reshape(count // 4, 2, 2, 2), ("z", "x", "c", "y"))
        names = {"ctx": CTX, "wa": "y", None: None}
        return jax.shard_map(
            dense_shards,
            mesh=grid,
            in_specs=tuple(P(*[names[n] for n in spec]) for spec in IN_SPECS),
            out_specs=tuple(P(*[names[n] for n in spec]) for spec in OUT_SPECS),
            check_vma=False,
        )(*arguments)

    return run
```
